32 devices in a mesh: rows: 8 (over z, y), seq: 4 (over x, core).
Axes of the slice: x: 2, y: 2, z: 4, core: 2. Of those that a mesh axis runs over, the one named last changes fastest.
Arguments:
- frames: bfloat16 [16, 1024, 768], P('rows', 'seq'), may hold values from -6 to 6
- utterance_lengths: int32 [16, 8], P('rows'), may hold values from 1 to 893, as said below
- tap_dir: bfloat16 [128, 48, 768], replicated, may hold values from -6 to 6
- tap_scale: float32 [128], replicated, may hold values from 1.5 to 4
- conv_bias: float32 [768], replicated, may hold values from -3 to 3
- pos_gain: float32 [768], replicated, may hold values from 0.5 to 1.5
- pos_shift: float32 [768], replicated, may hold values from -2 to 2
- query_weight: bfloat16 [768, 768], replicated, may hold values from -0.3125 to 0.3125
- query_bias: float32 [768], replicated, may hold values from -2 to 2
- key_weight: bfloat16 [768, 768], replicated, may hold values from -0.3125 to 0.3125
- value_weight: bfloat16 [768, 768], replicated, may hold values from -0.21875 to 0.21875
- value_bias: float32 [768], replicated, may hold values from -2 to 2
- proj_weight: bfloat16 [768, 768], replicated, may hold values from -0.625 to 0.625
- proj_bias: float32 [768], replicated, may hold values from -2 to 2
- attend_gain: float32 [768], replicated, may hold values from 0.5 to 1.5
- attend_shift: float32 [768], replicated, may hold values from -2 to 2
- inner_weight: bfloat16 [768, 3072], replicated, may hold values from -0.21875 to 0.21875
- inner_bias: float32 [3072], replicated, may hold values from -2 to 2
- outer_weight: bfloat16 [3072, 768], replicated, may hold values from -0.109375 to 0.109375
- outer_bias: float32 [768], replicated, may hold values from -2 to 2
- final_gain: float32 [768], replicated, may hold values from 0.5 to 1.5
- final_shift: float32 [768], replicated, may hold values from -2 to 2
- out_grad: bfloat16 [16, 1024, 768], P('rows', 'seq'), may hold values from -6 to 6
Outputs:
- layer_out: bfloat16 [16, 1024, 768], P('rows', 'seq')
- frames_grad: bfloat16 [16, 1024, 768], P('rows', 'seq')
- tap_dir_grad: float32 [128, 48, 768], P(None, None, 'seq')
- tap_scale_grad: float32 [128], P('seq')
- conv_bias_grad: float32 [768], P('seq')
- pos_gain_grad: float32 [768], P('seq')
- pos_shift_grad: float32 [768], P('seq')
- query_weight_grad: float32 [768, 768], P(None, 'seq')
- query_bias_grad: float32 [768], P('seq')
- key_weight_grad: float32 [768, 768], P(None, 'seq')
- value_weight_grad: float32 [768, 768], P(None, 'seq')
- value_bias_grad: float32 [768], P('seq')
- proj_weight_grad: float32 [768, 768], P(None, 'seq')
- proj_bias_grad: float32 [768], P('seq')
- attend_gain_grad: float32 [768], P('seq')
- attend_shift_grad: float32 [768], P('seq')
- inner_weight_grad: float32 [768, 3072], P(None, 'seq')
- inner_bias_grad: float32 [3072], P('seq')
- outer_weight_grad: float32 [3072, 768], P(None, 'seq')
- outer_bias_grad: float32 [768], P('seq')
- final_gain_grad: float32 [768], P('seq')
- final_shift_grad: float32 [768], P('seq')
The draws below stay inside these ranges and needn't reach their ends.
Inputs may be any that keep to these rules, and one draw needn't show every extreme that they name: `utterance_lengths`: each row's 8 lengths sum to 1024. One utterance of each row, among its first four, has exactly the largest length, starts within the row's first 256 frames and ends within its last 256; every other utterance has at most 32 frames.
All inputs are finite; a program needn't handle non-finite values.
Results may differ from the reference program's by a relative error of at most 0.018.
Values may be sent and summed in bfloat16 or wider, within the bound.
No kernel may reach another device: no remote copies, remote signals or barrier semaphores. Data moves between devices by JAX's collectives and lax.ppermute only.
A program may use at most 256 MiB of HBM per device.

```python
import math
import jax
import jax.numpy as jnp
from jax import lax

D = 768
HEADS = 12
HEAD_DIM = 64
FF = 3072
K = 128
GROUPS = 16
SEGS = 8
TIME_DEV = 256
ROWS = 16
ROW_LEN = 1024


def draw_utterance_lengths(key, part):
    key = jax.random.fold_in(key, 7)
    short_key, order_key, place_key = jax.random.split(key, 3)
    most = TIME_DEV // 8
    pair_count = (SEGS - 1) // 2
    firsts = jax.random.randint(short_key, (ROWS, pair_count), 1, most + 1, dtype=jnp.int32)
    seconds = most + 1 - firsts
    shorts = jnp.stack([firsts, seconds], axis=2).reshape(ROWS, 2 * pair_count)
    if (SEGS - 1) % 2 == 1:
        shorts = jnp.concatenate([shorts, jnp.full((ROWS, 1), most, jnp.int32)], axis=1)
    order_keys = jax.random.split(order_key, ROWS)
    orders = jax.vmap(lambda k: jax.random.permutation(k, SEGS - 1))(order_keys).astype(jnp.int32)
    shorts = jnp.take_along_axis(shorts, orders, axis=1)
    longest = ROW_LEN - pair_count * (most + 1) - (SEGS - 1) % 2 * most
    places = jax.random.randint(place_key, (ROWS, 1), 0, 4, dtype=jnp.int32)
    columns = jnp.arange(SEGS, dtype=jnp.int32)[None, :]
    source = jnp.clip(columns - (columns > places).astype(jnp.int32), 0, SEGS - 2)
    moved = jnp.take_along_axis(shorts, jnp.broadcast_to(source, (ROWS, SEGS)), axis=1)
    return jnp.where(columns == places, jnp.int32(longest), moved).astype(jnp.int32)


def levels(own_key, shape, cuts, smallest, top_value):
    def one(axis_at, blocks):
        steps = jax.random.uniform(jax.random.fold_in(jax.random.fold_in(own_key, 6), axis_at), (blocks,), jnp.float32, smallest / len(cuts), top_value / len(cuts))
        return jnp.repeat(jnp.exp(steps), shape[axis_at] // blocks).reshape((-1,) + (1,) * (len(shape) - axis_at - 1))

    level = one(*cuts[0])
    for cut in cuts[1:]:
        level = level * one(*cut)
    return level


def normal_values(stream_key, dims, scale, most, cuts=(), kind=jnp.bfloat16):
    values = scale * jax.random.normal(stream_key, dims, jnp.float32)
    if cuts:
        values = values * levels(stream_key, dims, cuts, -0.22, 0.18)
    return jnp.clip(values, -most, most).astype(kind)


def setup_inputs(seed: int = 0) -> dict:
    arg_keys = jax.random.split(jax.random.key(seed), 24)
    return {
        "frames": normal_values(arg_keys[0], (ROWS, ROW_LEN, D), 1.0, 6.0, ((0, 8), (1, 4))),
        "utterance_lengths": draw_utterance_lengths(jax.random.fold_in(arg_keys[23], 71), 0),
        "tap_dir": normal_values(arg_keys[2], (K, D // GROUPS, D), 1.0, 6.0),
        "tap_scale": jnp.clip(jnp.exp(jax.random.uniform(arg_keys[3], (K,), jnp.float32, math.log(1.5), math.log(4.0))), 1.5, 4.0),
        "conv_bias": normal_values(arg_keys[4], (D,), 0.5, 3.0, (), jnp.float32),
        "pos_gain": jnp.clip(1.0 + 0.1 * jax.random.normal(arg_keys[5], (D,), jnp.float32), 0.5, 1.5),
        "pos_shift": normal_values(arg_keys[6], (D,), 0.3, 2.0, (), jnp.float32),
        "query_weight": normal_values(arg_keys[7], (D, D), (D // 2) ** -0.5, 0.3125),
        "query_bias": normal_values(arg_keys[8], (D,), 0.3, 2.0, (), jnp.float32),
        "key_weight": normal_values(arg_keys[9], (D, D), (D // 2) ** -0.5, 0.3125),
        "value_weight": normal_values(arg_keys[10], (D, D), D ** -0.5, 0.21875),
        "value_bias": normal_values(arg_keys[11], (D,), 0.3, 2.0, (), jnp.float32),
        "proj_weight": normal_values(arg_keys[12], (D, D), (D // 8) ** -0.5, 0.625),
        "proj_bias": normal_values(arg_keys[13], (D,), 0.3, 2.0, (), jnp.float32),
        "attend_gain": jnp.clip(1.0 + 0.1 * jax.random.normal(arg_keys[14], (D,), jnp.float32), 0.5, 1.5),
        "attend_shift": normal_values(arg_keys[15], (D,), 0.3, 2.0, (), jnp.float32),
        "inner_weight": normal_values(arg_keys[16], (D, FF), D ** -0.5, 0.21875),
        "inner_bias": normal_values(arg_keys[17], (FF,), 0.3, 2.0, (), jnp.float32),
        "outer_weight": normal_values(arg_keys[18], (FF, D), FF ** -0.5, 0.109375),
        "outer_bias": normal_values(arg_keys[19], (D,), 0.3, 2.0, (), jnp.float32),
        "final_gain": jnp.clip(1.0 + 0.1 * jax.random.normal(arg_keys[20], (D,), jnp.float32), 0.5, 1.5),
        "final_shift": normal_values(arg_keys[21], (D,), 0.3, 2.0, (), jnp.float32),
        "out_grad": normal_values(arg_keys[22], (ROWS, ROW_LEN, D), 1.0, 6.0, ((0, 8), (1, 4))),
    }


HIGH = lax.Precision.HIGHEST
epsilon = 1e-05
tap_block = 8
big_negative = -1e+30

@jax.custom_vjp
def low(v):
    return lax.optimization_barrier(v.astype(jnp.bfloat16)).astype(jnp.float32)

@jax.custom_vjp
def low_back(v):
    return v

def low_keep(v):
    return (low(v), None)

def low_pass(kept, grad):
    return (grad,)

def back_keep(v):
    return (v, None)

def back_low(kept, grad):
    return (low(grad),)
low.defvjp(low_keep, low_pass)
low_back.defvjp(back_keep, back_low)

def layer_norm(values, gain, shift):
    centred = values - lax.optimization_barrier(jnp.mean(values, axis=-1, keepdims=True))
    spread = lax.optimization_barrier(jnp.mean(centred * centred, axis=-1, keepdims=True))
    return centred * lax.rsqrt(spread + epsilon) * gain + shift

def normed_taps(tap_dir, tap_scale):
    norms = jnp.sqrt(lax.optimization_barrier(jnp.sum(tap_dir * tap_dir, axis=(1, 2))))
    return tap_dir * (tap_scale / norms)[:, None, None]

def segment_ids(lengths, total):
    ends = jnp.cumsum(lengths, dtype=jnp.int32)
    places = jnp.arange(total, dtype=jnp.int32)
    return lax.optimization_barrier(jnp.sum((places[:, None] >= ends[None, :]).astype(jnp.int32), axis=1))

def gelu(values):
    return jax.nn.gelu(values, approximate=False)

def product(left, right):
    return jnp.dot(left, right, precision=HIGH)

def conv_row(row, segs, taps):
    total, width = row.shape
    taps_count = taps.shape[0]
    half = taps_count // 2
    channel = width // GROUPS
    padded = jnp.pad(row, ((half, half), (0, 0)))
    rim = jnp.full((half,), -1, jnp.int32)
    seg_padded = jnp.concatenate([rim, segs, rim])
    tap_groups = taps.reshape(taps_count // tap_block, tap_block, channel, GROUPS, channel)

    def one_block(running, block):
        block_index, weights = block

        def one_tap(offset):
            start = block_index * tap_block + offset
            piece = lax.dynamic_slice_in_dim(padded, start, total, 0)
            marks = lax.dynamic_slice_in_dim(seg_padded, start, total, 0) == segs
            return jnp.where(marks[:, None], piece, jnp.zeros((), jnp.float32))
        stacked = jnp.stack([one_tap(offset) for offset in range(tap_block)], axis=1)
        stacked = stacked.reshape(total, tap_block, GROUPS, channel)
        return (running + jnp.einsum('tjgc,jcgo->tgo', stacked, weights, precision=HIGH), None)
    start_sum = jnp.zeros((total, GROUPS, channel), jnp.float32)
    block_ids = jnp.arange(taps_count // tap_block, dtype=jnp.int32)
    summed, _ = lax.scan(jax.checkpoint(one_block), start_sum, (block_ids, tap_groups))
    return summed.reshape(total, width)

def attend_row(queries, keys_all, values_all, segs):
    total = queries.shape[0]
    block = min(512, total)
    query_blocks = queries.reshape(total // block, block, HEADS, HEAD_DIM)
    seg_blocks = segs.reshape(total // block, block)

    def one_block(pair):
        block_queries, block_segs = pair
        scores = low_back(jnp.einsum('qhe,khe->hqk', block_queries, keys_all, precision=HIGH))
        allowed = (block_segs[:, None] == segs[None, :])[None]
        scores = jnp.where(allowed, scores, big_negative)
        weights = low(jax.nn.softmax(scores, axis=-1))
        return jnp.einsum('hqk,khe->qhe', weights, values_all, precision=HIGH)
    outputs = lax.map(jax.checkpoint(one_block), (query_blocks, seg_blocks))
    return outputs.reshape(total, HEADS * HEAD_DIM)

def reference(frames, utterance_lengths, tap_dir, tap_scale, conv_bias, pos_gain, pos_shift, query_weight, query_bias, key_weight, value_weight, value_bias, proj_weight, proj_bias, attend_gain, attend_shift, inner_weight, inner_bias, outer_weight, outer_bias, final_gain, final_shift, out_grad):
    total = frames.shape[1]
    all_segs = jax.vmap(lambda lengths: segment_ids(lengths, total))(utterance_lengths)
    scale_factor = HEAD_DIM ** (-0.5)

    def forward(frames_f, tap_dir_f, tap_scale_f, conv_bias_f, pos_gain_f, pos_shift_f, query_weight_f, query_bias_f, key_weight_f, value_weight_f, value_bias_f, proj_weight_f, proj_bias_f, attend_gain_f, attend_shift_f, inner_weight_f, inner_bias_f, outer_weight_f, outer_bias_f, final_gain_f, final_shift_f):
        taps = low(normed_taps(tap_dir_f, tap_scale_f))

        def one_row(carry, pair):
            row, segs = pair
            pre = low_back(conv_row(row, segs, taps) + conv_bias_f)
            mixed = layer_norm(row + gelu(pre), pos_gain_f, pos_shift_f)
            mixed_low = low(mixed)
            queries = low_back(low((product(mixed_low, query_weight_f) + query_bias_f) * scale_factor))
            keys_all = low_back(low(product(mixed_low, key_weight_f)))
            values_all = low_back(low(product(mixed_low, value_weight_f) + value_bias_f))
            attended = attend_row(queries, keys_all.reshape(total, HEADS, HEAD_DIM), values_all.reshape(total, HEADS, HEAD_DIM), segs)
            attended = low_back(low(attended))
            projected = low_back(product(attended, proj_weight_f) + proj_bias_f)
            middle = layer_norm(mixed + projected, attend_gain_f, attend_shift_f)
            middle_low = low(middle)
            inner = low_back(product(middle_low, inner_weight_f) + inner_bias_f)
            activated = low(gelu(inner))
            outer = low_back(product(activated, outer_weight_f) + outer_bias_f)
            return (carry, layer_norm(middle + outer, final_gain_f, final_shift_f))
        _, outputs = lax.scan(one_row, jnp.zeros((), jnp.float32), (frames_f, all_segs))
        return outputs
    primals = (frames.astype(jnp.float32), tap_dir.astype(jnp.float32), tap_scale, conv_bias, pos_gain, pos_shift, query_weight.astype(jnp.float32), query_bias, key_weight.astype(jnp.float32), value_weight.astype(jnp.float32), value_bias, proj_weight.astype(jnp.float32), proj_bias, attend_gain, attend_shift, inner_weight.astype(jnp.float32), inner_bias, outer_weight.astype(jnp.float32), outer_bias, final_gain, final_shift)
    result, pull = jax.vjp(forward, *primals)
    grads = pull(out_grad.astype(jnp.float32))
    return (result.astype(jnp.bfloat16), grads[0].astype(jnp.bfloat16), grads[1], grads[2], grads[3], grads[4], grads[5], grads[6], grads[7], grads[8], grads[9], grads[10], grads[11], grads[12], grads[13], grads[14], grads[15], grads[16], grads[17], grads[18], grads[19], grads[20])
```

```python
import jax, jax.numpy as jnp
from jax import lax
from jax.sharding import PartitionSpec as P
from jax.experimental import pallas as pl
from jax.experimental.pallas import tpu as pltpu
F32=jnp.float32; BF=jnp.bfloat16
CH=48; PH=4; LW=PH*CH
NJ=33; SEGL=48; XROWS=(SEGL+NJ-1)*16; MROWS=SEGL*16
VM=60*1024*1024

def dot(a,b): return jnp.dot(a,b,preferred_element_type=F32)
def dot_nt(a,b): return lax.dot_general(a,b,(((1,),(1,)),((),())),preferred_element_type=F32)
def dot_tn(a,b): return lax.dot_general(a,b,(((0,),(0,)),((),())),preferred_element_type=F32)

def erf_gelu_parts(v):
    phi=0.5*(1.0+lax.erf(v*0.7071067811865476))
    return phi

WROWS=6400
def build_w_kernel(t_ref, w_ref, tp, rs):
    g=pl.program_id(0)
    rows=t_ref.shape[0]
    @pl.when(g==0)
    def _():
        tp[0:144,:]=jnp.zeros((144,LW),BF)
        tp[144:144+rows,:]=t_ref[...]
        tp[144+rows:,:]=jnp.zeros((256,LW),BF)
    src=lax.broadcasted_iota(jnp.int32,(LW,256),0); l=lax.broadcasted_iota(jnp.int32,(LW,256),1)
    pick=((src==48*g+lax.rem(l,48))&(l<LW)).astype(F32).astype(BF)
    n=640
    lane=lax.broadcasted_iota(jnp.int32,(n,256),1)
    for i in range(WROWS//n):
        r0=i*n
        R=dot(tp[r0:r0+n+144,:],pick).astype(BF)
        lo=jnp.where(lane[:,:128]<96,jnp.where(lane[:,:128]<48,R[144:144+n,:128],R[96:96+n,:128]),R[48:48+n,:128])
        hi=jnp.where(lane[:,128:]<144,R[48:48+n,128:],R[0:n,128:])
        w_ref[0,r0:r0+n,:128]=lo
        w_ref[0,r0:r0+n,128:]=hi

def build_w(taps2):
    rows=taps2.shape[0]
    return pl.pallas_call(build_w_kernel,grid=(4,),
        in_specs=[pl.BlockSpec((rows,LW),lambda g:(0,0))],
        out_specs=pl.BlockSpec((1,WROWS,256),lambda g:(g,0,0)),
        out_shape=jax.ShapeDtypeStruct((4,WROWS,256),BF),
        scratch_shapes=[pltpu.VMEM((rows+144+256,LW),BF),pltpu.VMEM((640+144,256),BF)],
        compiler_params=pltpu.CompilerParams(vmem_limit_bytes=VM))(taps2)

def sload(ref,start,n,stride):
    return jnp.concatenate([ref[0,pl.ds(start,n,stride=stride),:],ref[1,pl.ds(start,n,stride=stride),:]],axis=1)[:,:LW]
def sstore(ref,start,n,stride,v):
    ref[0,pl.ds(start,n,stride=stride),:]=v[:,:128]
    ref[1,pl.ds(start,n,stride=stride),:]=jnp.concatenate([v[:,128:],jnp.zeros((n,64),v.dtype)],axis=1)
def fload(ref,start,n):
    return jnp.concatenate([ref[0,pl.ds(start,n),:],ref[1,pl.ds(start,n),:]],axis=1)[:,:LW]
def fstore(ref,start,n,v):
    ref[0,pl.ds(start,n),:]=v[:,:128]
    ref[1,pl.ds(start,n),:]=jnp.concatenate([v[:,128:],jnp.zeros((n,64),v.dtype)],axis=1)

def pick_matrix(g,a):
    ch=lax.broadcasted_iota(jnp.int32,(LW,LW),0); l=lax.broadcasted_iota(jnp.int32,(LW,LW),1)
    return ((ch==48*g+(l-48*a))&(l>=48*a)&(l<48*a+48)).astype(F32).astype(BF)

def lane_times():
    sub=lax.broadcasted_iota(jnp.int32,(16,LW),0); l=lax.broadcasted_iota(jnp.int32,(16,LW),1)
    a=(l>=48).astype(jnp.int32)+(l>=96).astype(jnp.int32)+(l>=144).astype(jnp.int32)
    return 4*sub+a

def bounds(seg_ref,r,q):
    lo=seg_ref[r,q-1] if q>0 else 0
    return lo,seg_ref[r,q]

def respace(seg_ref,pair,src,xr,xsf):
    xsf[0,1280:1296,:]=jnp.zeros((16,128),F32); xsf[1,1280:1296,:]=jnp.zeros((16,128),F32)
    tin=lane_times()
    for r in range(2):
        bl=[bounds(seg_ref,pair*2+r,q) for q in range(8)]
        for B in range(26):
            v=jnp.zeros((16,LW),F32)
            for q in range(8):
                bb=B-1-q
                if 0<=bb<16:
                    t=tin+64*bb
                    v=jnp.where((t>=bl[q][0])&(t<bl[q][1]),src[pl.ds(r*256+16*bb,16),:],v)
            xr[r,pl.ds(16*B,16),:]=v
        for sp in range(8):
            sstore(xsf,r*8+sp,80,16,xr[r,pl.ds(48*sp,80),:])

def unspace(seg_ref,pair,acc,yr,emit):
    tin=lane_times()
    for r in range(2):
        bl=[bounds(seg_ref,pair*2+r,q) for q in range(8)]
        for sp in range(8):
            yr[r,pl.ds(48*sp,48),:]=sload(acc,r*8+sp,48,16)
        for bb in range(16):
            v=jnp.zeros((16,LW),F32)
            t=tin+64*bb
            for q in range(8):
                v=jnp.where((t>=bl[q][0])&(t<bl[q][1]),yr[r,pl.ds(16*(bb+q),16),:],v)
            emit(r*256+16*bb,v)

def conv_fwd_kernel(seg_ref,idx_ref,x0_ref,x1_ref,x2_ref,x3_ref,w_ref,bias_ref,first_ref,pre_ref,xs_ref,xt,xa,x4,xr,xsf,acc,yr,facc,accv,pk):
    pair=pl.program_id(0); g=pl.program_id(1)
    @pl.when(g==0)
    def _():
        for m,x_ref in enumerate((x0_ref,x1_ref,x2_ref,x3_ref)):
            k=pl.multiple_of((idx_ref[0]^m)*256,256)
            for r in range(2):
                fstore(xt,r*1024+k,256,x_ref[r].astype(F32))
        for a in range(4):
            xa[a]=sload(xt,a,512,4).astype(BF)
    v=dot(xa[0],pick_matrix(g,0))
    for a in range(1,4):
        v=v+dot(xa[a],pick_matrix(g,a))
    x4[...]=v
    respace(seg_ref,pair,x4,xr,xsf)
    n=XROWS
    zt=jnp.zeros((n+16,64),F32)
    va=xsf[0,0:n+16,:]; vb=xsf[1,0:n+16,:]
    z0=jnp.concatenate([zt,va[:,:64]],axis=1); z1=jnp.concatenate([va[:,64:],vb[:,:64]],axis=1)
    pk[n:n+32,:]=jnp.zeros((32,384),BF)
    pk[0:n,0:128]=va[0:n].astype(BF)
    pk[0:n,128:256]=(vb[0:n]+z0[16:]).astype(BF)
    pk[0:n,256:384]=z1[16:].astype(BF)
    xs_ref[0,0,:,0:384]=pk[0:n]
    xs_ref[0,0,:,384:768]=pk[32:32+n]
    s=dot(xs_ref[0,0,512:512+MROWS,0:256],w_ref[0,6144:6400,:])
    for J in range(8):
        s=s+dot(xs_ref[0,0,64*J:64*J+MROWS,:],w_ref[0,768*J:768*J+768,:])
    accv[...]=s
    bias=bias_ref[0]
    def emit(row,v):
        pre_ref[0,0,pl.ds(row,16),:]=v+bias
    acc[0]=accv[:,:128]; acc[1]=accv[:,128:]
    unspace(seg_ref,pair,acc,yr,emit)
    pre=pre_ref[0,0]
    fs=(x4[...]+pre*erf_gelu_parts(pre)).astype(BF)
    for a in range(4):
        f=dot_nt(fs,pick_matrix(g,a))
        @pl.when(g==0)
        def _(): facc[a]=f
        @pl.when(g>0)
        def _(): facc[a]=facc[a]+f
    @pl.when(g==3)
    def _():
        for a in range(4):
            sstore(xt,a,512,4,facc[a])
        first_ref[...]=fload(xt,0,2048).astype(BF)

def conv_fwd(ends,idx,xs4,w,bias4):
    R=xs4[0].shape[0]; pairs=R//2
    return pl.pallas_call(conv_fwd_kernel,grid=(pairs,4),
        in_specs=[pl.BlockSpec(memory_space=pltpu.SMEM)]*2+[pl.BlockSpec((2,256,LW),lambda p,g:(p,0,0))]*4+[
                  pl.BlockSpec((1,WROWS,256),lambda p,g:(g,0,0)),
                  pl.BlockSpec((1,1,LW),lambda p,g:(g,0,0))],
        out_specs=[pl.BlockSpec((2048,LW),lambda p,g:(p,0)),
                   pl.BlockSpec((1,1,512,LW),lambda p,g:(p,g,0,0)),
                   pl.BlockSpec((1,1,XROWS,768),lambda p,g:(p,g,0,0))],
        out_shape=[jax.ShapeDtypeStruct((R*1024,LW),BF),
                   jax.ShapeDtypeStruct((pairs,4,512,LW),F32),
                   jax.ShapeDtypeStruct((pairs,4,XROWS,768),BF)],
        scratch_shapes=[pltpu.VMEM((2,2048,128),F32),pltpu.VMEM((4,512,LW),BF),pltpu.VMEM((512,LW),F32),
            pltpu.VMEM((2,416,LW),F32),pltpu.VMEM((2,XROWS+16,128),F32),pltpu.VMEM((2,MROWS,128),F32),pltpu.VMEM((2,384,LW),F32),
            pltpu.VMEM((4,512,LW),F32),pltpu.VMEM((MROWS,256),F32),pltpu.VMEM((XROWS+32,384),BF)],
        compiler_params=pltpu.CompilerParams(vmem_limit_bytes=VM))(ends,idx,*xs4,w,bias4)

def tap_kernel(seg_ref,e0_ref,e1_ref,first_ref,stat_ref,mom_ref,gain_ref,pre_ref,xs_ref,tap_ref,ds_ref,d4_ref,bias_ref,vec_ref,xt,xa,dc,xr,xsf,A):
    pair=pl.program_id(0); g=pl.program_id(1)
    @pl.when(g==0)
    def _():
        gain=gain_ref[...]
        sg=jnp.zeros((1,LW),F32); sh=jnp.zeros((1,LW),F32)
        for t in range(8):
            rows=slice(256*t,256*t+256)
            e=e0_ref[rows]+e1_ref[rows].astype(F32)
            st=stat_ref[rows]
            mean=st[:,0:1]; rstd=st[:,1:2]
            mom=jnp.concatenate([mom_ref[t],jnp.zeros((120,256),F32)],axis=0).T*(1.0/768)
            xhat=(first_ref[rows].astype(F32)-mean)*rstd
            sg=sg+jnp.sum(e*xhat,axis=0,keepdims=True); sh=sh+jnp.sum(e,axis=0,keepdims=True)
            fstore(xt,256*t,256,rstd*(e*gain-mom[:,0:1]-xhat*mom[:,1:2]))
        vec_ref[0,0:1]=sg; vec_ref[0,1:2]=sh; vec_ref[0,2:8]=jnp.zeros((6,LW),F32)
        for a in range(4):
            xa[a]=sload(xt,a,512,4).astype(BF)
    v=dot(xa[0],pick_matrix(g,0))
    for a in range(1,4):
        v=v+dot(xa[a],pick_matrix(g,a))
    d4_ref[0,0]=v.astype(BF)
    pre=pre_ref[0,0]
    cdf=erf_gelu_parts(pre)
    slope=cdf+pre*(jnp.exp(-0.5*pre*pre)*0.3989422804014327)
    d=v*slope
    dc[...]=d
    bias_ref[0,0]=jnp.sum(d,axis=0,keepdims=True)
    respace(seg_ref,pair,dc,xr,xsf)
    ds_ref[0,0,:,0:128]=xsf[0,0:XROWS].astype(BF); ds_ref[0,0,:,128:256]=xsf[1,0:XROWS].astype(BF)
    DT=fload(xsf,256,MROWS).astype(BF).T
    for J in range(8):
        A[:,768*J:768*J+768]=dot(DT,xs_ref[0,0,64*J:64*J+MROWS,:])
    A[:,6144:6400]=dot(DT,xs_ref[0,0,512:512+MROWS,0:256])
    n=6144
    o=A[0:48,0:n]
    for b in range(1,4):
        o=o+A[48*b:48*b+48,48*b:48*b+n]
    for J in range(8):
        tap_ref[0,0,48*J:48*J+48]=o[:,768*J:768*J+768].astype(BF)

def tap_grads(ends,e0,e1,first,stat,mom,gain,pre,xs):
    R=e0.shape[0]//1024; pairs=R//2
    return pl.pallas_call(tap_kernel,grid=(pairs,4),
        in_specs=[pl.BlockSpec(memory_space=pltpu.SMEM),
                  pl.BlockSpec((2048,LW),lambda p,g:(p,0)),
                  pl.BlockSpec((2048,LW),lambda p,g:(p,0)),
                  pl.BlockSpec((2048,LW),lambda p,g:(p,0)),
                  pl.BlockSpec((2048,128),lambda p,g:(p,0)),
                  pl.BlockSpec((8,8,256),lambda p,g:(p,0,0)),
                  pl.BlockSpec((1,LW),lambda p,g:(0,0)),
                  pl.BlockSpec((1,1,512,LW),lambda p,g:(p,g,0,0)),
                  pl.BlockSpec((1,1,XROWS,768),lambda p,g:(p,g,0,0))],
        out_specs=[pl.BlockSpec((1,1,384,768),lambda p,g:(p,g,0,0)),
                   pl.BlockSpec((1,1,XROWS,256),lambda p,g:(p,g,0,0)),
                   pl.BlockSpec((1,1,512,LW),lambda p,g:(p,g,0,0)),
                   pl.BlockSpec((1,1,1,LW),lambda p,g:(p,g,0,0)),
                   pl.BlockSpec((1,8,LW),lambda p,g:(p,0,0))],
        out_shape=[jax.ShapeDtypeStruct((pairs,4,384,768),BF),
                   jax.ShapeDtypeStruct((pairs,4,XROWS,256),BF),
                   jax.ShapeDtypeStruct((pairs,4,512,LW),BF),
                   jax.ShapeDtypeStruct((pairs,4,1,LW),F32),jax.ShapeDtypeStruct((pairs,8,LW),F32)],
        scratch_shapes=[pltpu.VMEM((2,2048,128),F32),pltpu.VMEM((4,512,LW),BF),pltpu.VMEM((512,LW),F32),
            pltpu.VMEM((2,416,LW),F32),pltpu.VMEM((2,XROWS+16,128),F32),pltpu.VMEM((LW,6400),F32)],
        compiler_params=pltpu.CompilerParams(vmem_limit_bytes=VM))(ends,e0,e1,first,stat,mom,gain,pre,xs)

def back_kernel(seg_ref,idx_ref,ds_ref,d4_ref,w_ref,out_ref,xt,acc,yr,fs,facc,accv):
    pair=pl.program_id(0); g=pl.program_id(1)
    s=None
    for j in range(NJ):
        p=dot_nt(ds_ref[0,0,16*(NJ-1-j):16*(NJ-1-j)+MROWS,:],w_ref[0,LW*j:LW*j+256,:])
        s=p if s is None else s+p
    accv[...]=s
    def emit(row,v):
        fs[pl.ds(row,16),:]=(v+d4_ref[0,0,pl.ds(row,16),:].astype(F32)).astype(BF)
    acc[0]=accv[:,:128]; acc[1]=accv[:,128:]
    unspace(seg_ref,pair,acc,yr,emit)
    for a in range(4):
        f=dot_nt(fs[...],pick_matrix(g,a))
        @pl.when(g==0)
        def _(): facc[a]=f
        @pl.when(g>0)
        def _(): facc[a]=facc[a]+f
    @pl.when(g==3)
    def _():
        for a in range(4):
            sstore(xt,a,512,4,facc[a])
        for r in range(2):
            for k in range(4):
                out_ref[idx_ref[0]^k,r]=fload(xt,r*1024+k*256,256).astype(BF)

def conv_back(ends,idx,ds,d4,w):
    pairs=ds.shape[0]; R=2*pairs
    return pl.pallas_call(back_kernel,grid=(pairs,4),
        in_specs=[pl.BlockSpec(memory_space=pltpu.SMEM),pl.BlockSpec(memory_space=pltpu.SMEM),
                  pl.BlockSpec((1,1,XROWS,256),lambda p,g:(p,g,0,0)),
                  pl.BlockSpec((1,1,512,LW),lambda p,g:(p,g,0,0)),
                  pl.BlockSpec((1,WROWS,256),lambda p,g:(g,0,0))],
        out_specs=pl.BlockSpec((4,2,256,LW),lambda p,g:(0,p,0,0)),
        out_shape=jax.ShapeDtypeStruct((4,R,256,LW),BF),
        scratch_shapes=[pltpu.VMEM((2,2048,128),F32),pltpu.VMEM((2,MROWS,128),F32),pltpu.VMEM((2,384,LW),F32),
            pltpu.VMEM((512,LW),BF),pltpu.VMEM((4,512,LW),F32),pltpu.VMEM((MROWS,256),F32)],
        compiler_params=pltpu.CompilerParams(vmem_limit_bytes=VM))(ends,idx,ds,d4,w)


def qkv_kernel(f0,f1,f2,f3,w_ref,bias_ref,gain_ref,shift_ref,q_ref,k_ref,v_ref,ml_ref,stat_ref):
    fs=[f[...].astype(F32) for f in (f0,f1,f2,f3)]
    mean=sum(jnp.sum(f,axis=1,keepdims=True) for f in fs)*(1.0/768)
    cs=[f-mean for f in fs]
    var=sum(jnp.sum(c*c,axis=1,keepdims=True) for c in cs)*(1.0/768)
    rstd=lax.rsqrt(var+1e-5)
    n=mean.shape[0]
    pad=jnp.zeros((n,64),BF)
    out=None
    for m in range(4):
        ml=(cs[m]*rstd*gain_ref[m]+shift_ref[m]).astype(BF)
        ml_ref[m]=ml
        p=dot(jnp.concatenate([ml,pad],axis=1),w_ref[m])
        out=p if out is None else out+p
    out=(out+bias_ref[...]).astype(BF)
    q_ref[...]=out[:,0:192]; k_ref[...]=out[:,256:448]; v_ref[...]=out[:,512:704]
    lane=lax.broadcasted_iota(jnp.int32,(n,128),1)
    stat_ref[...]=jnp.where(lane==0,mean,jnp.where(lane==1,rstd,0.0))

def qkv(fs,w,bias,gain,shift):
    N=fs[0].shape[0]; B=512
    row=pl.BlockSpec((B,LW),lambda i:(i,0))
    full=lambda a: pl.BlockSpec(a.shape,lambda i:(0,)*a.ndim)
    return pl.pallas_call(qkv_kernel,grid=(N//B,),
        in_specs=[row]*4+[full(w),full(bias),full(gain),full(shift)],
        out_specs=[row]*3+[pl.BlockSpec((4,B,LW),lambda i:(0,i,0)),pl.BlockSpec((B,128),lambda i:(i,0))],
        out_shape=[jax.ShapeDtypeStruct((N,LW),BF)]*3+[jax.ShapeDtypeStruct((4,N,LW),BF),jax.ShapeDtypeStruct((N,128),F32)],
        compiler_params=pltpu.CompilerParams(vmem_limit_bytes=VM))(*fs,w,bias,gain,shift)

def seg_vec(seg_ref,r,shape,axis,start):
    t=lax.broadcasted_iota(jnp.int32,shape,axis)+start
    v=jnp.zeros(shape,jnp.int32)
    for i in range(8):
        v=v+(t>=seg_ref[r,i]).astype(jnp.int32)
    return v

def attn_kernel(idx_ref,seg_ref,q_ref,k_ref,v_ref,o_ref,lse_ref):
    r=pl.program_id(0); kb=pl.program_id(1)
    sq=seg_vec(seg_ref,r,(256,1),0,kb*256); sk=seg_vec(seg_ref,r,(1,1024),1,0)
    same=sq==sk
    outs=[]; rows=[]
    for h in range(3):
        c=slice(64*h,64*h+64)
        s=jnp.where(same,dot_nt(q_ref[:,c],k_ref[:,c]),-1e30)
        mx=jnp.max(s,axis=1,keepdims=True)
        p=jnp.exp(s-mx)
        tot=jnp.sum(p,axis=1,keepdims=True)
        outs.append(dot(p.astype(BF),v_ref[:,c])/tot)
        rows.append(jnp.broadcast_to(mx+jnp.log(tot),(256,128)).T[0:1,:])
    o_ref[0,0]=jnp.concatenate(outs,axis=1).astype(BF)
    lse_ref[0,0]=jnp.concatenate(rows+[jnp.zeros((5,256),F32)],axis=0)

def attn(idx,ends,q,k,v):
    R=ends.shape[0]
    return pl.pallas_call(attn_kernel,
        grid_spec=pltpu.PrefetchScalarGridSpec(num_scalar_prefetch=2,grid=(R,4),
        in_specs=[pl.BlockSpec((256,LW),lambda r,b,i,s:(4*r+b,0)),pl.BlockSpec((1024,LW),lambda r,b,i,s:(r,0)),pl.BlockSpec((1024,LW),lambda r,b,i,s:(r,0))],
        out_specs=[pl.BlockSpec((1,1,256,LW),lambda r,b,i,s:(b^i[0],r,0,0)),pl.BlockSpec((1,1,8,256),lambda r,b,i,s:(r,b,0,0))]),
        out_shape=[jax.ShapeDtypeStruct((4,R,256,LW),BF),jax.ShapeDtypeStruct((R,4,8,256),F32)],
        compiler_params=pltpu.CompilerParams(vmem_limit_bytes=VM))(idx,ends,q,k,v)

def attn_bwd_kernel(idx_ref,seg_ref,q_ref,k_ref,v_ref,o_ref,do_ref,lse_ref,dq_ref,dk_ref,dv_ref,dks,dvs):
    r=pl.program_id(0); kb=pl.program_id(1)
    sq=seg_vec(seg_ref,r,(1,256),1,kb*256); sk=seg_vec(seg_ref,r,(1024,1),0,0)
    same=sk==sq
    @pl.when(kb==0)
    def _():
        dks[...]=jnp.zeros_like(dks); dvs[...]=jnp.zeros_like(dvs)
    dqs=[]; ks=[]; vs=[]
    for h in range(3):
        c=slice(64*h,64*h+64)
        q=q_ref[:,c]; k=k_ref[:,c]; do=do_ref[0,0,:,c]
        delta=jnp.sum(do.astype(F32)*o_ref[0,0,:,c].astype(F32),axis=1,keepdims=True)
        delta=jnp.broadcast_to(delta,(256,128)).T[0:1,:]
        st=jnp.where(same,dot_nt(k,q)-lse_ref[0,0,h:h+1,:],-1e30)
        p=jnp.exp(st)
        dp=dot_nt(v_ref[:,c],do)
        ds=(p*(dp-delta)).astype(BF)
        vs.append(dot(p.astype(BF),do)); ks.append(dot(ds,q)); dqs.append(dot_tn(ds,k))
    dks[...]+=jnp.concatenate(ks,axis=1); dvs[...]+=jnp.concatenate(vs,axis=1)
    dq_ref[...]=jnp.concatenate(dqs,axis=1).astype(BF)
    @pl.when(kb==3)
    def _():
        dk_ref[...]=dks[...].astype(BF); dv_ref[...]=dvs[...].astype(BF)

def attn_bwd(idx,ends,q,k,v,o,dos,lse):
    R=ends.shape[0]
    blk=pl.BlockSpec((256,LW),lambda r,b,i,s:(4*r+b,0)); full=pl.BlockSpec((1024,LW),lambda r,b,i,s:(r,0))
    x4=pl.BlockSpec((1,1,256,LW),lambda r,b,i,s:(b^i[0],r,0,0))
    return pl.pallas_call(attn_bwd_kernel,
        grid_spec=pltpu.PrefetchScalarGridSpec(num_scalar_prefetch=2,grid=(R,4),
        in_specs=[blk,full,full,x4,x4,pl.BlockSpec((1,1,8,256),lambda r,b,i,s:(r,b,0,0))],
        out_specs=[blk,full,full],scratch_shapes=[pltpu.VMEM((1024,LW),F32)]*2),
        out_shape=[jax.ShapeDtypeStruct((R*1024,LW),BF)]*3,
        compiler_params=pltpu.CompilerParams(vmem_limit_bytes=VM))(idx,ends,q,k,v,o,dos,lse)

def pad3(a,b,c):
    z=jnp.zeros((a.shape[0],64),BF)
    return jnp.concatenate([a,z,b,z,c,z],axis=1)

def dmix_kernel(idx_ref,dq_ref,dk_ref,dv_ref,w_ref,sec_ref,f0,f1,f2,f3,stat_ref,gain_ref,p0,p1,p2,p3,mom_ref):
    kb=pl.program_id(1)
    d=pad3(dq_ref[...],dk_ref[...],dv_ref[...])
    st=stat_ref[...]; mean=st[:,0:1]; rstd=st[:,1:2]
    mine=(kb==idx_ref[0]).astype(F32)
    m1=None
    for m,(f,p) in enumerate(zip((f0,f1,f2,f3),(p0,p1,p2,p3))):
        part=dot_nt(d,w_ref[m])[:,:LW]
        part=part+mine*sec_ref[m,0]
        p[...]=part.astype(p.dtype)
        eg=part*gain_ref[m]
        xh=(f[...].astype(F32)-mean)*rstd
        a=jnp.sum(eg,axis=1,keepdims=True); b=jnp.sum(eg*xh,axis=1,keepdims=True)
        m1=(a,b) if m1 is None else (m1[0]+a,m1[1]+b)
    lane=lax.broadcasted_iota(jnp.int32,(256,128),1)
    mom_ref[0]=jnp.where(lane==0,m1[0],jnp.where(lane==1,m1[1],0.0)).T[0:8,:]

def dmix(idx,dq,dk,dv,w,sec,fs,stat,gain):
    N=dq.shape[0]; R=N//1024
    blk=pl.BlockSpec((256,LW),lambda r,b,i:(4*r+b,0))
    full=lambda a: pl.BlockSpec(a.shape,lambda r,b,i:(0,)*a.ndim)
    return pl.pallas_call(dmix_kernel,
        grid_spec=pltpu.PrefetchScalarGridSpec(num_scalar_prefetch=1,grid=(R,4),
        in_specs=[blk]*3+[full(w),pl.BlockSpec((4,1,256,LW),lambda r,b,i:(0,r,0,0))]+[blk]*4+[pl.BlockSpec((256,128),lambda r,b,i:(4*r+b,0)),full(gain)],
        out_specs=[blk]*4+[pl.BlockSpec((1,8,256),lambda r,b,i:(4*r+b,0,0))]),
        out_shape=[jax.ShapeDtypeStruct((N,LW),F32)]+[jax.ShapeDtypeStruct((N,LW),BF)]*3+[jax.ShapeDtypeStruct((4*R,8,256),F32)],
        compiler_params=pltpu.CompilerParams(vmem_limit_bytes=VM))(idx,dq,dk,dv,w,sec,*fs,stat,gain)

def qkvw_kernel(dq_ref,dk_ref,dv_ref,ml_ref,out_ref,bias_ref,acc):
    i=pl.program_id(0)
    d=pad3(dq_ref[...],dk_ref[...],dv_ref[...])
    dt=d.T
    @pl.when(i==0)
    def _(): acc[...]=jnp.zeros_like(acc); bias_ref[...]=jnp.zeros_like(bias_ref)
    bias_ref[...]+=jnp.broadcast_to(jnp.sum(d.astype(F32),axis=0,keepdims=True),bias_ref.shape)
    pad=jnp.zeros((d.shape[0],64),BF)
    for m in range(4):
        acc[m]+=dot(dt,jnp.concatenate([ml_ref[m],pad],axis=1))
    @pl.when(i==pl.num_programs(0)-1)
    def _():
        for t in range(3):
            for m in range(4):
                out_ref[t,m]=acc[m,256*t:256*t+192,:LW].astype(BF)

def qkvw(dq,dk,dv,ml):
    N=dq.shape[0]; B=512
    row=pl.BlockSpec((B,LW),lambda i:(i,0))
    return pl.pallas_call(qkvw_kernel,grid=(N//B,),
        in_specs=[row]*3+[pl.BlockSpec((4,B,LW),lambda i:(0,i,0))],
        out_specs=[pl.BlockSpec((3,4,LW,LW),lambda i:(0,0,0,0)),pl.BlockSpec((8,768),lambda i:(0,0))],
        out_shape=[jax.ShapeDtypeStruct((3,4,LW,LW),BF),jax.ShapeDtypeStruct((8,768),F32)],
        scratch_shapes=[pltpu.VMEM((4,768,256),F32)],
        compiler_params=pltpu.CompilerParams(vmem_limit_bytes=VM))(dq,dk,dv,ml)


def swap(x, axis, bit):
    return lax.ppermute(x, axis, [(i, i ^ bit) for i in range(lax.axis_size(axis))])


def halve(x, axis, bit):
    on = (lax.axis_index(axis) & bit) != 0
    h = x.shape[0] // 2
    lo, hi = x[:h], x[h:]
    got = swap(jnp.where(on, lo, hi), axis, bit)
    return (jnp.where(on, hi, lo).astype(F32) + got.astype(F32)).astype(BF)


def double(x, axis, bit):
    on = (lax.axis_index(axis) & bit) != 0
    got = swap(x, axis, bit)
    return jnp.concatenate([jnp.where(on, got, x), jnp.where(on, x, got)], axis=0)


def sum_rows(x):
    n = lax.axis_size("rows")
    bits = [1 << i for i in range(n.bit_length() - 1)]
    orders = (bits, bits[1::-1] + bits[2:])
    count = x.shape[0]
    step = 2 * n * 8
    full = -(-count // step) * step
    if full != count:
        x = jnp.concatenate([x, jnp.zeros((full - count,) + x.shape[1:], x.dtype)], axis=0)
    parts = [x[: full // 2], x[full // 2 :]]
    for s in range(len(bits)):
        parts = [halve(p, "rows", o[s]) for p, o in zip(parts, orders)]
    for s in reversed(range(len(bits))):
        parts = [double(p, "rows", o[s]) for p, o in zip(parts, orders)]
    return jnp.concatenate(parts, axis=0)[:count]


def gather_seq(x):
    far = swap(x, "seq", 2)
    near = swap(x, "seq", 1)
    return [x, near, far, swap(far, "seq", 1)]


def trade(blocks):
    return [blocks[0], swap(blocks[1], "seq", 1), swap(blocks[2], "seq", 2), swap(blocks[3], "seq", 3)]


def scatter_parts(blocks):
    three = swap(blocks[3], "seq", 1)
    one = swap(blocks[1], "seq", 1)
    far = (blocks[2].astype(F32) + three.astype(F32)).astype(BF)
    return blocks[0].astype(F32) + one.astype(F32), swap(far, "seq", 2)


def assemble(blocks, index):
    low = (index & 1) != 0
    high = (index & 2) != 0
    b = [jnp.where(low, blocks[m ^ 1], blocks[m]) for m in range(4)]
    return [jnp.where(high, b[m ^ 2], b[m]) for m in range(4)]


def cut(x, start, size, axis):
    return lax.dynamic_slice_in_dim(x, start, size, axis)


def layer_norm(values, gain, shift):
    centred = values - jnp.mean(values, axis=-1, keepdims=True)
    spread = jnp.mean(centred * centred, axis=-1, keepdims=True)
    return centred * lax.rsqrt(spread + 1e-5) * gain + shift


def gelu(values):
    return jax.nn.gelu(values, approximate=False)


def local(
    frames,
    utterance_lengths,
    tap_dir,
    tap_scale,
    conv_bias,
    pos_gain,
    pos_shift,
    query_weight,
    query_bias,
    key_weight,
    value_weight,
    value_bias,
    proj_weight,
    proj_bias,
    attend_gain,
    attend_shift,
    inner_weight,
    inner_bias,
    outer_weight,
    outer_bias,
    final_gain,
    final_shift,
    out_grad,
):
    R = frames.shape[0]
    index = lax.axis_index("seq")
    idx = jnp.full((1,), index, jnp.int32)
    ends = jnp.cumsum(utterance_lengths, axis=1, dtype=jnp.int32)
    order = [index ^ m for m in range(4)]
    own = index * LW

    sent = trade([cut(frames, b * LW, LW, 2) for b in order])
    norms = jnp.sqrt(jnp.sum(jnp.square(tap_dir.astype(F32)), axis=(1, 2)))
    coef = tap_scale / norms
    dir_own = cut(tap_dir, own, LW, 2).astype(F32)
    taps = (dir_own * coef[:, None, None]).astype(BF).reshape(128 * 48, LW)
    w = build_w(taps)
    bias4 = jnp.tile(cut(conv_bias, own, LW, 0).reshape(4, 1, 48), (1, 4, 1)).reshape(4, 1, LW)
    first, pre, xs = conv_fwd(ends, idx, sent, w, bias4)
    firsts = gather_seq(first)

    def xor_rows(a):
        return jnp.stack([cut(a, b * LW, LW, 0) for b in order])

    def pad_to(a, axis, size):
        widths = [(0, 0)] * a.ndim
        widths[axis] = (0, size - a.shape[axis])
        return jnp.pad(a, widths)

    own_cols = [
        pad_to(cut(a, own, LW, 1), 1, 256)
        for a in (query_weight * jnp.asarray(0.125, BF), key_weight, value_weight)
    ]
    w_qkv = pad_to(xor_rows(jnp.concatenate(own_cols, axis=1)), 1, 256)
    b_qkv = jnp.concatenate(
        [
            pad_to(cut(query_bias, own, LW, 0) * 0.125, 0, 512),
            pad_to(cut(value_bias, own, LW, 0), 0, 256),
        ]
    )[None]
    gain_x = xor_rows(pos_gain)[:, None]
    shift_x = xor_rows(pos_shift)[:, None]
    q, k, v, mixed_low, stat = qkv(firsts, w_qkv, b_qkv, gain_x, shift_x)
    att, lse = attn(idx, ends, q, k, v)
    att_blocks = trade([att[m] for m in range(4)])

    mine = [cut(f.reshape(R, 4, 256, LW), index, 1, 1)[:, 0] for f in firsts]
    first_mine = jnp.concatenate(assemble(mine, index), axis=-1).astype(F32).reshape(R * 256, 768)
    mixed = layer_norm(first_mine, pos_gain, pos_shift)
    attended = jnp.concatenate(assemble(att_blocks, index), axis=-1).reshape(R * 256, 768)
    second_sum = mixed + dot(attended, proj_weight) + proj_bias
    middle = layer_norm(second_sum, attend_gain, attend_shift)
    middle_low = middle.astype(BF)
    inner = dot(middle_low, inner_weight) + inner_bias
    activated = gelu(inner).astype(BF)
    third_sum = middle + dot(activated, outer_weight) + outer_bias
    layer_out, final_pull = jax.vjp(layer_norm, third_sum, final_gain, final_shift)
    d_third, g_final_gain, g_final_shift = final_pull(out_grad.reshape(R * 256, 768).astype(F32))
    layer_out = layer_out.astype(BF).reshape(R, 256, 768)
    d_outer = d_third.astype(BF)
    _, inner_pull = jax.vjp(gelu, inner)
    d_inner = inner_pull(dot_nt(d_outer, outer_weight))[0].astype(BF)
    d_middle = d_third + dot_nt(d_inner, inner_weight)
    _, middle_pull = jax.vjp(layer_norm, second_sum, attend_gain, attend_shift)
    d_second, g_attend_gain, g_attend_shift = middle_pull(d_middle)
    d_proj = d_second.astype(BF)
    d_attended = dot_nt(d_proj, proj_weight).astype(BF).reshape(R, 256, 768)
    do_blocks = trade([cut(d_attended, b * LW, LW, 2) for b in order])
    dos = jnp.stack(do_blocks)
    early = jnp.concatenate(
        [
            g_final_gain,
            g_final_shift,
            jnp.sum(d_outer.astype(F32), axis=0),
            jnp.sum(d_inner.astype(F32), axis=0),
            g_attend_gain,
            g_attend_shift,
            jnp.sum(d_proj.astype(F32), axis=0),
        ]
    )
    g_outer = dot_tn(d_outer, activated).astype(BF)
    g_inner = dot_tn(middle_low, d_inner).astype(BF)
    g_proj = dot_tn(d_proj, attended).astype(BF)

    def bulk(b):
        o = cut(g_outer, b * LW, LW, 0)
        return jnp.concatenate(
            [cut(g_inner, b * 768, 768, 1)]
            + [o[:, 768 * i : 768 * i + 768] for i in range(4)]
            + [cut(g_proj, b * LW, LW, 0)],
            axis=0,
        )

    near, far = scatter_parts([bulk(b) for b in order])
    bulk_sum = sum_rows((near + far.astype(F32)).astype(BF))
    t_inner = bulk_sum[:768].astype(F32)
    t_outer = jnp.concatenate([bulk_sum[768 + LW * i : 768 + LW * i + LW].T for i in range(4)]).astype(F32)
    t_proj = bulk_sum[1536:1728].T.astype(F32)

    dq, dk, dv = attn_bwd(idx, ends, q, k, v, att, dos, lse)
    second_x = jnp.stack([cut(d_second.reshape(R, 256, 768), b * LW, LW, 2) for b in order])
    *parts, moments = dmix(idx, dq, dk, dv, w_qkv, second_x, firsts, stat, gain_x)
    e_near, e_far = scatter_parts(parts)
    m1 = moments + swap(moments, "seq", 1)
    moments = m1 + swap(m1, "seq", 2)
    g_qkv, b_grads = qkvw(dq, dk, dv, mixed_low)
    qkv_sum = sum_rows(g_qkv.reshape(3 * 4 * LW, LW)).reshape(3, 4, LW, LW)
    qkv_std = assemble([qkv_sum[:, m] for m in range(4)], index)
    t_qkv = jnp.concatenate([jnp.swapaxes(b, 1, 2) for b in qkv_std], axis=1).astype(F32)

    tap_part, ds, d4, conv_b, vec = tap_grads(
        ends, e_near, e_far, first, stat, moments, cut(pos_gain, own, LW, 0)[None], pre, xs
    )
    if R > 2:
        tap_part = jnp.sum(tap_part.astype(F32), axis=0).astype(BF)
    tap_sum = sum_rows(tap_part.reshape(1536, 768)).reshape(4, 8, 48, 768)
    back = trade_out(conv_back(ends, idx, ds, d4, w))
    frames_grad = jnp.concatenate(assemble(back, index), axis=-1)
    tap_grad = tap_sum.transpose(1, 3, 0, 2).reshape(128, 48, LW).astype(F32)
    dots = lax.psum(jnp.sum(tap_grad * dir_own, axis=(1, 2)), "seq")
    g_tap_dir = coef[:, None, None] * (tap_grad - dir_own * (dots / (norms * norms))[:, None, None])
    g_tap_scale = cut(dots / norms, index * 32, 32, 0)

    late = jnp.concatenate(
        [
            jnp.sum(conv_b, axis=(0, 2)).reshape(4, 4, 48).sum(1).reshape(LW),
            jnp.sum(vec[:, 0], axis=0),
            jnp.sum(vec[:, 1], axis=0),
            b_grads[0, 0:LW] * 0.125,
            b_grads[0, 512 : 512 + LW],
        ]
    )
    late = lax.psum(late, "rows")
    early = lax.psum(early, ("rows", "seq"))

    def share(a, start, size):
        return cut(a, start + index * size, size, 0)

    return (
        layer_out,
        frames_grad,
        g_tap_dir,
        g_tap_scale,
        late[0:LW],
        late[LW : 2 * LW],
        late[2 * LW : 3 * LW],
        t_qkv[0] * 0.125,
        late[3 * LW : 4 * LW],
        t_qkv[1],
        t_qkv[2],
        late[4 * LW : 5 * LW],
        t_proj,
        share(early, 6912, LW),
        share(early, 5376, LW),
        share(early, 6144, LW),
        t_inner,
        share(early, 2304, 768),
        t_outer,
        share(early, 1536, LW),
        share(early, 0, LW),
        share(early, 768, LW),
    )


def trade_out(x):
    return trade([x[m] for m in range(4)])


def solution(mesh):
    split = P("rows", "seq", None)
    col = P(None, "seq")
    one = P("seq")
    return jax.shard_map(
        local,
        mesh=mesh,
        in_specs=(split, P("rows", None)) + (P(),) * 20 + (split,),
        out_specs=(split, split, P(None, None, "seq"), one, one, one, one)
        + (col, one, col, col, one, col, one, one, one, col, one, col, one, one, one),
        check_vma=False,
    )
```

```python
import jax, jax.numpy as jnp
from jax import lax
from jax.sharding import PartitionSpec as P
from jax.experimental import pallas as pl
from jax.experimental.pallas import tpu as pltpu
F32=jnp.float32; BF=jnp.bfloat16
CH=48; PH=4; LW=PH*CH
NJ=33; SEGL=48; XROWS=(SEGL+NJ-1)*16; MROWS=SEGL*16
VM=60*1024*1024

def cost(us):
    return pl.CostEstimate(flops=int(us*1.0e9),bytes_accessed=int(us*3.0e6),transcendentals=0)

ANY=pl.BlockSpec(memory_space=pl.ANY)
PW=2*LW

def skip(kernel,at,count):
    if not count:
        return kernel
    return lambda *refs: kernel(*refs[:at],*refs[at+count:])

def dot(a,b): return jnp.dot(a,b,preferred_element_type=F32)
def dot_nt(a,b): return lax.dot_general(a,b,(((1,),(1,)),((),())),preferred_element_type=F32)
def dot_tn(a,b): return lax.dot_general(a,b,(((0,),(0,)),((),())),preferred_element_type=F32)

def erf_gelu_parts(v):
    phi=0.5*(1.0+lax.erf(v*0.7071067811865476))
    return phi

WROWS=6400
def build_w_kernel(t_ref, w_ref, tp, rs):
    g=pl.program_id(0)
    rows=t_ref.shape[0]
    @pl.when(g==0)
    def _():
        tp[0:144,:]=jnp.zeros((144,LW),BF)
        tp[144:144+rows,:]=t_ref[...]
        tp[144+rows:,:]=jnp.zeros((256,LW),BF)
    src=lax.broadcasted_iota(jnp.int32,(LW,256),0); l=lax.broadcasted_iota(jnp.int32,(LW,256),1)
    pick=((src==48*g+lax.rem(l,48))&(l<LW)).astype(F32).astype(BF)
    n=640
    lane=lax.broadcasted_iota(jnp.int32,(n,256),1)
    for i in range(WROWS//n):
        r0=i*n
        R=dot(tp[r0:r0+n+144,:],pick).astype(BF)
        lo=jnp.where(lane[:,:128]<96,jnp.where(lane[:,:128]<48,R[144:144+n,:128],R[96:96+n,:128]),R[48:48+n,:128])
        hi=jnp.where(lane[:,128:]<144,R[48:48+n,128:],R[0:n,128:])
        w_ref[0,r0:r0+n,:128]=lo
        w_ref[0,r0:r0+n,128:]=hi

def build_w(taps2):
    rows=taps2.shape[0]
    return pl.pallas_call(build_w_kernel,grid=(4,),
        in_specs=[pl.BlockSpec((rows,LW),lambda g:(0,0))],
        out_specs=pl.BlockSpec((1,WROWS,256),lambda g:(g,0,0)),
        out_shape=jax.ShapeDtypeStruct((4,WROWS,256),BF),
        scratch_shapes=[pltpu.VMEM((rows+144+256,LW),BF),pltpu.VMEM((640+144,256),BF)],
        cost_estimate=cost(10),
        compiler_params=pltpu.CompilerParams(vmem_limit_bytes=VM))(taps2)

def sload(ref,start,n,stride):
    return jnp.concatenate([ref[0,pl.ds(start,n,stride=stride),:],ref[1,pl.ds(start,n,stride=stride),:]],axis=1)[:,:LW]
def sstore(ref,start,n,stride,v):
    ref[0,pl.ds(start,n,stride=stride),:]=v[:,:128]
    ref[1,pl.ds(start,n,stride=stride),:]=jnp.concatenate([v[:,128:],jnp.zeros((n,64),v.dtype)],axis=1)
def fload(ref,start,n):
    return jnp.concatenate([ref[0,pl.ds(start,n),:],ref[1,pl.ds(start,n),:]],axis=1)[:,:LW]
def fstore(ref,start,n,v):
    ref[0,pl.ds(start,n),:]=v[:,:128]
    ref[1,pl.ds(start,n),:]=jnp.concatenate([v[:,128:],jnp.zeros((n,64),v.dtype)],axis=1)

def pick_matrix(g,a):
    ch=lax.broadcasted_iota(jnp.int32,(LW,LW),0); l=lax.broadcasted_iota(jnp.int32,(LW,LW),1)
    return ((ch==48*g+(l-48*a))&(l>=48*a)&(l<48*a+48)).astype(F32).astype(BF)

def lane_times():
    sub=lax.broadcasted_iota(jnp.int32,(16,LW),0); l=lax.broadcasted_iota(jnp.int32,(16,LW),1)
    a=(l>=48).astype(jnp.int32)+(l>=96).astype(jnp.int32)+(l>=144).astype(jnp.int32)
    return 4*sub+a

def bounds(seg_ref,r,q):
    lo=seg_ref[r,q-1] if q>0 else 0
    return lo,seg_ref[r,q]

def respace(seg_ref,pair,src,xr,xsf):
    xsf[0,1280:1296,:]=jnp.zeros((16,128),F32); xsf[1,1280:1296,:]=jnp.zeros((16,128),F32)
    tin=lane_times()
    for r in range(2):
        bl=[bounds(seg_ref,pair*2+r,q) for q in range(8)]
        for B in range(26):
            v=jnp.zeros((16,LW),F32)
            for q in range(8):
                bb=B-1-q
                if 0<=bb<16:
                    t=tin+64*bb
                    v=jnp.where((t>=bl[q][0])&(t<bl[q][1]),src[pl.ds(r*256+16*bb,16),:],v)
            xr[r,pl.ds(16*B,16),:]=v
        for sp in range(8):
            sstore(xsf,r*8+sp,80,16,xr[r,pl.ds(48*sp,80),:])

def unspace(seg_ref,pair,acc,yr,emit):
    tin=lane_times()
    for r in range(2):
        bl=[bounds(seg_ref,pair*2+r,q) for q in range(8)]
        for sp in range(8):
            yr[r,pl.ds(48*sp,48),:]=sload(acc,r*8+sp,48,16)
        for bb in range(16):
            v=jnp.zeros((16,LW),F32)
            t=tin+64*bb
            for q in range(8):
                v=jnp.where((t>=bl[q][0])&(t<bl[q][1]),yr[r,pl.ds(16*(bb+q),16),:],v)
            emit(r*256+16*bb,v)

def conv_fwd_kernel(seg_ref,idx_ref,x0_ref,x1_ref,x2_ref,x3_ref,w_ref,bias_ref,first_ref,pre_ref,xs_ref,xt,xa,x4,xr,xsf,acc,yr,facc,accv,pk):
    pair=pl.program_id(0); g=pl.program_id(1)
    @pl.when(g==0)
    def _():
        for m,x_ref in enumerate((x0_ref,x1_ref,x2_ref,x3_ref)):
            k=pl.multiple_of((idx_ref[0]^m)*256,256)
            for r in range(2):
                fstore(xt,r*1024+k,256,x_ref[...].astype(F32)[:,LW*r:LW*r+LW])
        for a in range(4):
            xa[a]=sload(xt,a,512,4).astype(BF)
    v=dot(xa[0],pick_matrix(g,0))
    for a in range(1,4):
        v=v+dot(xa[a],pick_matrix(g,a))
    x4[...]=v
    respace(seg_ref,pair,x4,xr,xsf)
    n=XROWS
    zt=jnp.zeros((n+16,64),F32)
    va=xsf[0,0:n+16,:]; vb=xsf[1,0:n+16,:]
    z0=jnp.concatenate([zt,va[:,:64]],axis=1); z1=jnp.concatenate([va[:,64:],vb[:,:64]],axis=1)
    pk[n:n+32,:]=jnp.zeros((32,384),BF)
    pk[0:n,0:128]=va[0:n].astype(BF)
    pk[0:n,128:256]=(vb[0:n]+z0[16:]).astype(BF)
    pk[0:n,256:384]=z1[16:].astype(BF)
    xs_ref[0,0,:,0:384]=pk[0:n]
    xs_ref[0,0,:,384:768]=pk[32:32+n]
    s=dot(xs_ref[0,0,512:512+MROWS,0:256],w_ref[0,6144:6400,:])
    for J in range(8):
        s=s+dot(xs_ref[0,0,64*J:64*J+MROWS,:],w_ref[0,768*J:768*J+768,:])
    accv[...]=s
    bias=bias_ref[0]
    def emit(row,v):
        pre_ref[0,0,pl.ds(row,16),:]=v+bias
    acc[0]=accv[:,:128]; acc[1]=accv[:,128:]
    unspace(seg_ref,pair,acc,yr,emit)
    pre=pre_ref[0,0]
    fs=(x4[...]+pre*erf_gelu_parts(pre)).astype(BF)
    for a in range(4):
        f=dot_nt(fs,pick_matrix(g,a))
        @pl.when(g==0)
        def _(): facc[a]=f
        @pl.when(g>0)
        def _(): facc[a]=facc[a]+f
    @pl.when(g==3)
    def _():
        for a in range(4):
            sstore(xt,a,512,4,facc[a])
        first_ref[...]=jnp.concatenate([fload(xt,0,1024),fload(xt,1024,1024)],axis=1).astype(BF)

def conv_fwd(ends,idx,xs4,w,bias4):
    pairs=xs4[0].shape[0]//256
    return pl.pallas_call(conv_fwd_kernel,grid=(pairs,4),
        in_specs=[pl.BlockSpec(memory_space=pltpu.SMEM)]*2+[pl.BlockSpec((256,PW),lambda p,g:(p,0))]*4+[
                  pl.BlockSpec((1,WROWS,256),lambda p,g:(g,0,0)),
                  pl.BlockSpec((1,1,LW),lambda p,g:(g,0,0))],
        out_specs=[pl.BlockSpec((1024,PW),lambda p,g:(p,0)),
                   pl.BlockSpec((1,1,512,LW),lambda p,g:(p,g,0,0)),
                   pl.BlockSpec((1,1,XROWS,768),lambda p,g:(p,g,0,0))],
        out_shape=[jax.ShapeDtypeStruct((pairs*1024,PW),BF),
                   jax.ShapeDtypeStruct((pairs,4,512,LW),F32),
                   jax.ShapeDtypeStruct((pairs,4,XROWS,768),BF)],
        scratch_shapes=[pltpu.VMEM((2,2048,128),F32),pltpu.VMEM((4,512,LW),BF),pltpu.VMEM((512,LW),F32),
            pltpu.VMEM((2,416,LW),F32),pltpu.VMEM((2,XROWS+16,128),F32),pltpu.VMEM((2,MROWS,128),F32),pltpu.VMEM((2,384,LW),F32),
            pltpu.VMEM((4,512,LW),F32),pltpu.VMEM((MROWS,256),F32),pltpu.VMEM((XROWS+32,384),BF)],
        cost_estimate=cost(35),
        compiler_params=pltpu.CompilerParams(vmem_limit_bytes=VM))(ends,idx,*xs4,w,bias4)

def tap_kernel(seg_ref,e0_ref,e1_ref,first_ref,stat_ref,mom_ref,gain_ref,pre_ref,xs_ref,qkv_ref,tap_ref,ds_ref,d4_ref,bias_ref,vec_ref,xt,xa,dc,xr,xsf,A):
    pair=pl.program_id(0); g=pl.program_id(1)
    @pl.when(g==0)
    def _():
        gain=gain_ref[...]
        sg=jnp.zeros((1,LW),F32); sh=jnp.zeros((1,LW),F32)
        for t in range(8):
            r,k=t//4,t%4
            rows=slice(256*k,256*k+256); cols=slice(LW*r,LW*r+LW)
            e=(e0_ref[rows]+e1_ref[rows].astype(F32))[:,cols]
            st=stat_ref[256*t:256*t+256]
            mean=st[:,0:1]; rstd=st[:,1:2]
            mom=jnp.concatenate([mom_ref[t],jnp.zeros((120,256),F32)],axis=0).T*(1.0/768)
            xhat=(first_ref[rows].astype(F32)[:,cols]-mean)*rstd
            sg=sg+jnp.sum(e*xhat,axis=0,keepdims=True); sh=sh+jnp.sum(e,axis=0,keepdims=True)
            fstore(xt,256*t,256,rstd*(e*gain-mom[:,0:1]-xhat*mom[:,1:2]))
        vec_ref[0,0:1]=sg; vec_ref[0,1:2]=sh; vec_ref[0,2:8]=jnp.zeros((6,LW),F32)
        for a in range(4):
            xa[a]=sload(xt,a,512,4).astype(BF)
    v=dot(xa[0],pick_matrix(g,0))
    for a in range(1,4):
        v=v+dot(xa[a],pick_matrix(g,a))
    d4_ref[0,0]=v.astype(BF)
    pre=pre_ref[0,0]
    cdf=erf_gelu_parts(pre)
    slope=cdf+pre*(jnp.exp(-0.5*pre*pre)*0.3989422804014327)
    d=v*slope
    dc[...]=d
    bias_ref[0,0]=jnp.sum(d,axis=0,keepdims=True)
    respace(seg_ref,pair,dc,xr,xsf)
    ds_ref[0,0,:,0:128]=xsf[0,0:XROWS].astype(BF); ds_ref[0,0,:,128:256]=xsf[1,0:XROWS].astype(BF)
    DT=fload(xsf,256,MROWS).astype(BF).T
    for J in range(8):
        A[:,768*J:768*J+768]=dot(DT,xs_ref[0,0,64*J:64*J+MROWS,:])
    A[:,6144:6400]=dot(DT,xs_ref[0,0,512:512+MROWS,0:256])
    n=6144
    o=A[0:48,0:n]
    for b in range(1,4):
        o=o+A[48*b:48*b+48,48*b:48*b+n]
    for J in range(8):
        tap_ref[0,J]=o[:,768*J:768*J+768].astype(BF)
    tap_ref[0,8:11]=jnp.where(pair==0,qkv_ref[...],jnp.zeros((3,48,768),BF))

def tap_grads(ends,e0,e1,first,stat,mom,gain,pre,xs,g_qkv,deps=()):
    pairs=e0.shape[0]//1024
    return pl.pallas_call(skip(tap_kernel,10,len(deps)),grid=(pairs,4),
        in_specs=[pl.BlockSpec(memory_space=pltpu.SMEM),
                  pl.BlockSpec((1024,PW),lambda p,g:(p,0)),
                  pl.BlockSpec((1024,PW),lambda p,g:(p,0)),
                  pl.BlockSpec((1024,PW),lambda p,g:(p,0)),
                  pl.BlockSpec((2048,128),lambda p,g:(p,0)),
                  pl.BlockSpec((8,8,256),lambda p,g:(p,0,0)),
                  pl.BlockSpec((1,LW),lambda p,g:(0,0)),
                  pl.BlockSpec((1,1,512,LW),lambda p,g:(p,g,0,0)),
                  pl.BlockSpec((1,1,XROWS,768),lambda p,g:(p,g,0,0)),
                  pl.BlockSpec((3,48,768),lambda p,g:(0,g,0))]+[ANY]*len(deps),
        out_specs=[pl.BlockSpec((1,11,48,768),lambda p,g:(p,0,g,0)),
                   pl.BlockSpec((1,1,XROWS,256),lambda p,g:(p,g,0,0)),
                   pl.BlockSpec((1,1,512,LW),lambda p,g:(p,g,0,0)),
                   pl.BlockSpec((1,1,1,LW),lambda p,g:(p,g,0,0)),
                   pl.BlockSpec((1,8,LW),lambda p,g:(p,0,0))],
        out_shape=[jax.ShapeDtypeStruct((pairs,11,LW,768),BF),
                   jax.ShapeDtypeStruct((pairs,4,XROWS,256),BF),
                   jax.ShapeDtypeStruct((pairs,4,512,LW),BF),
                   jax.ShapeDtypeStruct((pairs,4,1,LW),F32),jax.ShapeDtypeStruct((pairs,8,LW),F32)],
        scratch_shapes=[pltpu.VMEM((2,2048,128),F32),pltpu.VMEM((4,512,LW),BF),pltpu.VMEM((512,LW),F32),
            pltpu.VMEM((2,416,LW),F32),pltpu.VMEM((2,XROWS+16,128),F32),pltpu.VMEM((LW,6400),F32)],
        cost_estimate=cost(24),
        compiler_params=pltpu.CompilerParams(vmem_limit_bytes=VM))(ends,e0,e1,first,stat,mom,gain,pre,xs,g_qkv,*deps)

def back_kernel(at,seg_ref,idx_ref,ds_ref,d4_ref,w_ref,*rest):
    if at:
        part_ref,out_ref,xt,acc,yr,fs,accv=rest
    else:
        facc,acc,yr,fs,accv=rest
    pair=pl.program_id(0); i=pl.program_id(1); g=i+at
    s=None
    for j in range(NJ):
        p=dot_nt(ds_ref[0,0,16*(NJ-1-j):16*(NJ-1-j)+MROWS,:],w_ref[0,LW*j:LW*j+256,:])
        s=p if s is None else s+p
    accv[...]=s
    def emit(row,v):
        fs[pl.ds(row,16),:]=(v+d4_ref[0,0,pl.ds(row,16),:].astype(F32)).astype(BF)
    acc[0]=accv[:,:128]; acc[1]=accv[:,128:]
    unspace(seg_ref,pair,acc,yr,emit)
    if at:
        for a in range(4):
            f=dot_nt(fs[...],pick_matrix(g,a))
            @pl.when(i==0)
            def _(): sstore(xt,a,512,4,f+part_ref[0,a])
            @pl.when(i>0)
            def _(): sstore(xt,a,512,4,f+sload(xt,a,512,4))
        @pl.when(i==1)
        def _():
            for k in range(4):
                out_ref[idx_ref[0]^k]=jnp.concatenate([fload(xt,k*256,256),fload(xt,1024+k*256,256)],axis=1).astype(BF)
    else:
        for a in range(4):
            f=dot_nt(fs[...],pick_matrix(g,a))
            @pl.when(i==0)
            def _(): facc[0,a]=f
            @pl.when(i>0)
            def _(): facc[0,a]=facc[0,a]+f

def conv_back(at,ends,idx,ds,d4,w,part=None,deps=()):
    pairs=ds.shape[0]
    parts=() if part is None else (part,)
    facc=pl.BlockSpec((1,4,512,LW),lambda p,g:(p,0,0,0))
    scratch=[pltpu.VMEM((2,2048,128),F32)] if at else []
    return pl.pallas_call(skip(lambda *refs: back_kernel(at,*refs),5+len(parts),len(deps)),grid=(pairs,2),
        in_specs=[pl.BlockSpec(memory_space=pltpu.SMEM),pl.BlockSpec(memory_space=pltpu.SMEM),
                  pl.BlockSpec((1,1,XROWS,256),lambda p,g:(p,g+at,0,0)),
                  pl.BlockSpec((1,1,512,LW),lambda p,g:(p,g+at,0,0)),
                  pl.BlockSpec((1,WROWS,256),lambda p,g:(g+at,0,0))]+[facc]*len(parts)+[ANY]*len(deps),
        out_specs=pl.BlockSpec((4,256,PW),lambda p,g:(0,p,0)) if at else facc,
        out_shape=jax.ShapeDtypeStruct((4,pairs*256,PW),BF) if at else jax.ShapeDtypeStruct((pairs,4,512,LW),F32),
        scratch_shapes=scratch+[pltpu.VMEM((2,MROWS,128),F32),pltpu.VMEM((2,384,LW),F32),
            pltpu.VMEM((512,LW),BF),pltpu.VMEM((MROWS,256),F32)],
        cost_estimate=cost(15),
        compiler_params=pltpu.CompilerParams(vmem_limit_bytes=VM))(ends,idx,ds,d4,w,*parts,*deps)


def qkv_kernel(f0,f1,f2,f3,w_ref,bias_ref,gain_ref,shift_ref,q_ref,k_ref,v_ref,ml_ref,stat_ref):
    fs=[f[...].astype(F32) for f in (f0,f1,f2,f3)]
    fs=[jnp.concatenate([f[:,:LW],f[:,LW:]],axis=0) for f in fs]
    mean=sum(jnp.sum(f,axis=1,keepdims=True) for f in fs)*(1.0/768)
    cs=[f-mean for f in fs]
    var=sum(jnp.sum(c*c,axis=1,keepdims=True) for c in cs)*(1.0/768)
    rstd=lax.rsqrt(var+1e-5)
    n=mean.shape[0]
    pad=jnp.zeros((n,64),BF)
    out=None
    for m in range(4):
        ml=(cs[m]*rstd*gain_ref[m]+shift_ref[m]).astype(BF)
        ml_ref[m]=ml.reshape(2,256,LW)
        p=dot(jnp.concatenate([ml,pad],axis=1),w_ref[m])
        out=p if out is None else out+p
    out=(out+bias_ref[...]).astype(BF)
    out=out.reshape(2,256,768)
    q_ref[...]=out[:,:,0:192]; k_ref[...]=out[:,:,256:448]; v_ref[...]=out[:,:,512:704]
    lane=lax.broadcasted_iota(jnp.int32,(n,128),1)
    stat_ref[...]=jnp.where(lane==0,mean,jnp.where(lane==1,rstd,0.0)).reshape(2,256,128)

def qkv(fs,w,bias,gain,shift):
    pairs=fs[0].shape[0]//1024; R=2*pairs
    row=pl.BlockSpec((2,256,LW),lambda p,k:(p,k,0))
    full=lambda a: pl.BlockSpec(a.shape,lambda p,k:(0,)*a.ndim)
    return pl.pallas_call(qkv_kernel,grid=(pairs,4),
        in_specs=[pl.BlockSpec((256,PW),lambda p,k:(4*p+k,0))]*4+[full(w),full(bias),full(gain),full(shift)],
        out_specs=[row]*3+[pl.BlockSpec((4,2,256,LW),lambda p,k:(0,p,k,0)),pl.BlockSpec((2,256,128),lambda p,k:(p,k,0))],
        out_shape=[jax.ShapeDtypeStruct((R,1024,LW),BF)]*3+[jax.ShapeDtypeStruct((4,R,1024,LW),BF),jax.ShapeDtypeStruct((R,1024,128),F32)],
        cost_estimate=cost(10),
        compiler_params=pltpu.CompilerParams(vmem_limit_bytes=VM))(*fs,w,bias,gain,shift)

def seg_vec(seg_ref,r,shape,axis,start):
    t=lax.broadcasted_iota(jnp.int32,shape,axis)+start
    v=jnp.zeros(shape,jnp.int32)
    for i in range(8):
        v=v+(t>=seg_ref[r,i]).astype(jnp.int32)
    return v

def attn_kernel(idx_ref,seg_ref,q_ref,k_ref,v_ref,o_ref,of_ref,lse_ref):
    pair=pl.program_id(0); kb=pl.program_id(1)
    for r in range(2):
        sq=seg_vec(seg_ref,2*pair+r,(256,1),0,kb*256); sk=seg_vec(seg_ref,2*pair+r,(1,1024),1,0)
        same=sq==sk
        outs=[]; rows=[]
        for h in range(3):
            c=slice(64*h,64*h+64)
            s=jnp.where(same,dot_nt(q_ref[r,:,c],k_ref[r,:,c]),-1e30)
            mx=jnp.max(s,axis=1,keepdims=True)
            p=jnp.exp(s-mx)
            tot=jnp.sum(p,axis=1,keepdims=True)
            outs.append(dot(p.astype(BF),v_ref[r,:,c])/tot)
            rows.append(jnp.broadcast_to(mx+jnp.log(tot),(256,128)).T[0:1,:])
        o=jnp.concatenate(outs,axis=1)
        of_ref[r]=o
        o_ref[0,:,LW*r:LW*r+LW]=o.astype(BF)
        lse_ref[r,0]=jnp.concatenate(rows+[jnp.zeros((5,256),F32)],axis=0)

def attn(idx,ends,q,k,v):
    R=ends.shape[0]; pairs=R//2
    blk=pl.BlockSpec((2,256,LW),lambda p,b,i,s:(p,b,0)); full=pl.BlockSpec((2,1024,LW),lambda p,b,i,s:(p,0,0))
    return pl.pallas_call(attn_kernel,
        grid_spec=pltpu.PrefetchScalarGridSpec(num_scalar_prefetch=2,grid=(pairs,4),
        in_specs=[blk,full,full],
        out_specs=[pl.BlockSpec((1,256,PW),lambda p,b,i,s:(b^i[0],p,0)),blk,pl.BlockSpec((2,1,8,256),lambda p,b,i,s:(p,b,0,0))]),
        out_shape=[jax.ShapeDtypeStruct((4,pairs*256,PW),BF),jax.ShapeDtypeStruct((R,1024,LW),F32),jax.ShapeDtypeStruct((R,4,8,256),F32)],
        cost_estimate=cost(18),
        compiler_params=pltpu.CompilerParams(vmem_limit_bytes=VM))(idx,ends,q,k,v)

def attn_bwd_kernel(r,idx_ref,seg_ref,q_ref,k_ref,v_ref,o_ref,d0,d1,d2,d3,lse_ref,dq_ref,dk_ref,dv_ref,dks,dvs):
    pair=pl.program_id(0); kb=pl.program_id(1)
    m=kb^idx_ref[0]
    mine=slice(LW*r,LW*r+LW)
    dod=jnp.where(m<2,jnp.where(m==0,d0[...],d1[...]),jnp.where(m==2,d2[...],d3[...])).astype(F32)[:,mine].astype(BF)
    @pl.when(kb==0)
    def _():
        dks[...]=jnp.zeros_like(dks); dvs[...]=jnp.zeros_like(dvs)
    sq=seg_vec(seg_ref,2*pair+r,(1,256),1,kb*256); sk=seg_vec(seg_ref,2*pair+r,(1024,1),0,0)
    same=sk==sq
    dqs=[]; ks=[]; vs=[]
    for h in range(3):
        c=slice(64*h,64*h+64)
        q=q_ref[0,:,c]; k=k_ref[0,:,c]; do=dod[:,c]
        delta=jnp.sum(do.astype(F32)*o_ref[0,:,c],axis=1,keepdims=True)
        delta=jnp.broadcast_to(delta,(256,128)).T[0:1,:]
        st=jnp.where(same,dot_nt(k,q)-lse_ref[0,0,h:h+1,:],-1e30)
        p=jnp.exp(st)
        dp=dot_nt(v_ref[0,:,c],do)
        ds=(p*(dp-delta)).astype(BF)
        vs.append(dot(p.astype(BF),do)); ks.append(dot(ds,q)); dqs.append(dot_tn(ds,k))
    dks[...]+=jnp.concatenate(ks,axis=1); dvs[...]+=jnp.concatenate(vs,axis=1)
    dq_ref[0]=jnp.concatenate(dqs,axis=1).astype(BF)
    @pl.when(kb==3)
    def _():
        dk_ref[0]=dks[...].astype(BF); dv_ref[0]=dvs[...].astype(BF)

def attn_bwd(r,idx,ends,q,k,v,o,dos,lse,deps=()):
    pairs=ends.shape[0]//2
    blk=pl.BlockSpec((1,256,LW),lambda p,b,i,s:(2*p+r,b,0)); full=pl.BlockSpec((1,1024,LW),lambda p,b,i,s:(2*p+r,0,0))
    out=pl.BlockSpec((1,256,LW),lambda p,b,i,s:(p,b,0)); outs=pl.BlockSpec((1,1024,LW),lambda p,b,i,s:(p,0,0))
    return pl.pallas_call(skip(lambda *refs: attn_bwd_kernel(r,*refs),11,len(deps)),
        grid_spec=pltpu.PrefetchScalarGridSpec(num_scalar_prefetch=2,grid=(pairs,4),
        in_specs=[blk,full,full,blk]+[pl.BlockSpec((256,PW),lambda p,b,i,s:(p,0))]*4+[pl.BlockSpec((1,1,8,256),lambda p,b,i,s:(2*p+r,b,0,0))]+[ANY]*len(deps),
        out_specs=[out,outs,outs],scratch_shapes=[pltpu.VMEM((1024,LW),F32)]*2),
        out_shape=[jax.ShapeDtypeStruct((pairs,1024,LW),BF)]*3,
        cost_estimate=cost(60),
        compiler_params=pltpu.CompilerParams(vmem_limit_bytes=VM))(idx,ends,q,k,v,o,*dos,lse,*deps)

def pad3(a,b,c):
    z=jnp.zeros((a.shape[0],64),BF)
    return jnp.concatenate([a,z,b,z,c,z],axis=1)

def dmix_kernel(idx_ref,q0,k0,v0,q1,k1,v1,w_ref,sec_ref,f0,f1,f2,f3,stat_ref,gain_ref,keep_ref,send_ref,mom_ref):
    kb=pl.program_id(1)
    flat=lambda x: x[...].reshape(512,x.shape[-1])
    d=jnp.concatenate([pad3(q0[0],k0[0],v0[0]),pad3(q1[0],k1[0],v1[0])],axis=0)
    st=flat(stat_ref); mean=st[:,0:1]; rstd=st[:,1:2]
    mine=(kb==idx_ref[0]).astype(F32)
    m1=None
    for m,f in enumerate((f0,f1,f2,f3)):
        part=dot_nt(d,w_ref[m])[:,:LW]
        part=part+mine*sec_ref[m].reshape(512,LW)
        both=jnp.concatenate([part[:256],part[256:]],axis=1)
        if m%2: send_ref[m//2]=both.astype(BF)
        else: keep_ref[m//2]=both
        eg=part*gain_ref[m]
        f=f[...].astype(F32)
        xh=(jnp.concatenate([f[:,:LW],f[:,LW:]],axis=0)-mean)*rstd
        a=jnp.sum(eg,axis=1,keepdims=True); b=jnp.sum(eg*xh,axis=1,keepdims=True)
        m1=(a,b) if m1 is None else (m1[0]+a,m1[1]+b)
    lane=lax.broadcasted_iota(jnp.int32,(512,128),1)
    t=jnp.where(lane==0,m1[0],jnp.where(lane==1,m1[1],0.0)).T[0:8,:]
    mom_ref[0,0]=t[:,:256]; mom_ref[1,0]=t[:,256:]

def dmix(idx,heads,w,sec,fs,stat,gain,deps=()):
    pairs=heads[0].shape[0]; R=2*pairs
    blk=pl.BlockSpec((1,256,LW),lambda p,b,i:(p,b,0))
    full=lambda a: pl.BlockSpec(a.shape,lambda p,b,i:(0,)*a.ndim)
    pack=pl.BlockSpec((2,256,PW),lambda p,b,i:(0,4*p+b,0))
    return pl.pallas_call(skip(dmix_kernel,15,len(deps)),
        grid_spec=pltpu.PrefetchScalarGridSpec(num_scalar_prefetch=1,grid=(pairs,4),
        in_specs=[blk]*6+[full(w),pl.BlockSpec((4,2,256,LW),lambda p,b,i:(0,p,0,0))]+[pl.BlockSpec((256,PW),lambda p,b,i:(4*p+b,0))]*4
            +[pl.BlockSpec((2,256,128),lambda p,b,i:(p,b,0)),full(gain)]+[ANY]*len(deps),
        out_specs=[pack,pack,pl.BlockSpec((2,1,8,256),lambda p,b,i:(p,b,0,0))]),
        out_shape=[jax.ShapeDtypeStruct((2,pairs*1024,PW),F32),jax.ShapeDtypeStruct((2,pairs*1024,PW),BF),jax.ShapeDtypeStruct((R,4,8,256),F32)],
        cost_estimate=cost(12),
        compiler_params=pltpu.CompilerParams(vmem_limit_bytes=VM))(idx,*heads,w,sec,*fs,stat,gain,*deps)

def qkvw_kernel(q0,k0,v0,q1,k1,v1,ml_ref,out_ref,bias_ref,acc):
    i=pl.program_id(0)*2+pl.program_id(1)
    @pl.when(i==0)
    def _(): acc[...]=jnp.zeros_like(acc); bias_ref[...]=jnp.zeros_like(bias_ref)
    d=jnp.concatenate([pad3(q0[0],k0[0],v0[0]),pad3(q1[0],k1[0],v1[0])],axis=0)
    dt=d.T
    bias_ref[...]+=jnp.broadcast_to(jnp.sum(d.astype(F32),axis=0,keepdims=True),bias_ref.shape)
    pad=jnp.zeros((d.shape[0],64),BF)
    for m in range(4):
        acc[m]+=dot(dt,jnp.concatenate([ml_ref[m].reshape(d.shape[0],LW),pad],axis=1))
    @pl.when(i==2*pl.num_programs(0)-1)
    def _():
        for t in range(3):
            out_ref[t]=jnp.concatenate([acc[m,256*t:256*t+192,:LW] for m in range(4)],axis=1).astype(BF)

def qkvw(heads,ml,deps=()):
    pairs=heads[0].shape[0]
    row=pl.BlockSpec((1,512,LW),lambda p,i:(p,i,0))
    return pl.pallas_call(skip(qkvw_kernel,7,len(deps)),grid=(pairs,2),
        in_specs=[row]*6+[pl.BlockSpec((4,2,512,LW),lambda p,i:(0,p,i,0))]+[ANY]*len(deps),
        out_specs=[pl.BlockSpec((3,LW,768),lambda p,i:(0,0,0)),pl.BlockSpec((8,768),lambda p,i:(0,0))],
        out_shape=[jax.ShapeDtypeStruct((3,LW,768),BF),jax.ShapeDtypeStruct((8,768),F32)],
        scratch_shapes=[pltpu.VMEM((4,768,256),F32)],
        cost_estimate=cost(8),
        compiler_params=pltpu.CompilerParams(vmem_limit_bytes=VM))(*heads,ml,*deps)


def row_sum(x):
    return jnp.sum(x, axis=0, keepdims=True)


def norm_parts(x):
    c = x - jnp.mean(x, axis=1, keepdims=True)
    rstd = lax.rsqrt(jnp.mean(c * c, axis=1, keepdims=True) + 1e-5)
    return c * rstd, rstd


def norm_back(e, xhat, rstd, gain):
    eg = e * gain
    return rstd * (eg - jnp.mean(eg, axis=1, keepdims=True) - xhat * jnp.mean(eg * xhat, axis=1, keepdims=True))


def in_order(blocks, index):
    low = (index & 1) != 0
    high = (index & 2) != 0
    b = [jnp.where(low, blocks[m ^ 1], blocks[m]) for m in range(4)]
    return jnp.concatenate([jnp.where(high, b[m ^ 2], b[m]) for m in range(4)], axis=1)


def half(r):
    return slice(LW * (r % 2), LW * (r % 2) + LW)


def ff_kernel(
    idx_ref, f0, f1, f2, f3, a0, a1, a2, a3, og_ref, pw_ref, iw_ref, ow_ref, ib_ref, vec_ref,
    out_ref, act_ref, din_ref, ml_ref, do_ref, dp_ref, att_ref, datt_ref, sec_ref, sums_ref, ibg_ref,
    mid, xh2, rs2, acc, slopes,
):
    i = pl.program_id(0)
    index = idx_ref[0]
    R = 2 * f0.shape[0]
    M = R * 256
    pos_gain, pos_shift, proj_bias, gain2, shift2, outer_bias, gain3, shift3 = [vec_ref[j : j + 1, :] for j in range(8)]

    @pl.when(i == 0)
    def _():
        for r in range(R):
            rows = pl.ds(256 * r, 256)
            xhat, _ = norm_parts(in_order([f[r // 2, 0].astype(F32)[:, half(r)] for f in (f0, f1, f2, f3)], index))
            att_ref[rows] = in_order([a[pl.ds(256 * (r // 2), 256)].astype(F32)[:, half(r)] for a in (a0, a1, a2, a3)], index).astype(BF)
            second = xhat * pos_gain + pos_shift + dot(att_ref[rows], pw_ref[...]) + proj_bias
            xhat, rstd = norm_parts(second)
            xh2[rows] = xhat
            rs2[rows] = jnp.broadcast_to(rstd, (256, 128))
            middle = xhat * gain2 + shift2
            mid[rows] = middle
            ml_ref[rows] = middle.astype(BF)
        acc[...] = jnp.zeros_like(acc)

    @pl.when(i < 4)
    def _():
        for r in range(R):
            rows = pl.ds(256 * r, 256)
            inner = dot(ml_ref[rows], iw_ref[...]) + ib_ref[0]
            phi = erf_gelu_parts(inner)
            slopes[i, rows] = (phi + inner * (jnp.exp(-0.5 * inner * inner) * 0.3989422804014327)).astype(BF)
            act_ref[rows] = (inner * phi).astype(BF)
            acc[rows] += dot(act_ref[rows], ow_ref[...])

    @pl.when(i == 3)
    def _():
        g1 = g2 = g3 = jnp.zeros((1, 768), F32)
        for r in range(R):
            rows = pl.ds(256 * r, 256)
            xhat, rstd = norm_parts(mid[rows] + acc[rows] + outer_bias)
            out_ref[rows] = (xhat * gain3 + shift3).astype(BF)
            e = og_ref[rows].astype(F32)
            d = norm_back(e, xhat, rstd, gain3)
            low = d.astype(BF)
            do_ref[rows] = low
            mid[rows] = d
            g1, g2, g3 = g1 + row_sum(e * xhat), g2 + row_sum(e), g3 + row_sum(low.astype(F32))
        sums_ref[0:1] = g1
        sums_ref[1:2] = g2
        sums_ref[2:3] = g3
        sums_ref[3:8] = jnp.zeros((5, 768), F32)

    @pl.when(i >= 4)
    def _():
        g = jnp.zeros((1, 768), F32)
        for r in range(R):
            rows = pl.ds(256 * r, 256)
            d = dot_nt(do_ref[rows], ow_ref[...]) * slopes[7 - i, rows].astype(F32)
            low = d.astype(BF)
            din_ref[rows] = low
            g = g + row_sum(low.astype(F32))
            mid[rows] += dot_nt(low, iw_ref[...])
        ibg_ref[0] = g

    @pl.when(i == 7)
    def _():
        g1 = g2 = g3 = jnp.zeros((1, 768), F32)
        for r in range(R):
            rows = pl.ds(256 * r, 256)
            e = mid[rows]
            xhat = xh2[rows]
            d = norm_back(e, xhat, rs2[rows, 0:1], gain2)
            low = d.astype(BF)
            dp_ref[rows] = low
            datt = dot_nt(low, pw_ref[...]).astype(BF)
            for b in range(4):
                datt_ref[index ^ b, pl.ds(256 * (r // 2), 256), half(r)] = datt[:, LW * b : LW * b + LW]
                sec_ref[index ^ b, r] = d[:, LW * b : LW * b + LW]
            g1, g2, g3 = g1 + row_sum(e * xhat), g2 + row_sum(e), g3 + row_sum(low.astype(F32))
        sums_ref[3:4] = g1
        sums_ref[4:5] = g2
        sums_ref[5:6] = g3


def ff(idx, firsts, atts, out_grad, pw, iw, ow, ib, vec):
    pairs = atts[0].shape[0] // 256
    R = 2 * pairs
    M = R * 256
    chunk = lambda i: jnp.where(i < 4, i, 7 - i)
    whole = lambda *s: pl.BlockSpec(s, lambda i, x: (0,) * len(s))
    return pl.pallas_call(
        ff_kernel,
        grid_spec=pltpu.PrefetchScalarGridSpec(
            num_scalar_prefetch=1,
            grid=(8,),
            in_specs=[pl.BlockSpec((pairs, 1, 256, PW), lambda i, x: (0, x[0], 0, 0))] * 4
            + [whole(pairs * 256, PW)] * 4
            + [
                whole(M, 768),
                whole(768, 768),
                pl.BlockSpec((768, 768), lambda i, x: (0, chunk(i))),
                pl.BlockSpec((768, 768), lambda i, x: (chunk(i), 0)),
                pl.BlockSpec((1, 1, 768), lambda i, x: (chunk(i), 0, 0)),
                whole(8, 768),
            ],
            out_specs=[
                whole(M, 768),
                pl.BlockSpec((M, 768), lambda i, x: (0, jnp.minimum(i, 3))),
                pl.BlockSpec((M, 768), lambda i, x: (0, jnp.minimum(7 - i, 3))),
            ]
            + [whole(M, 768)] * 4
            + [
                whole(4, pairs * 256, PW),
                whole(4, R, 256, LW),
                whole(8, 768),
                pl.BlockSpec((1, 1, 768), lambda i, x: (jnp.minimum(7 - i, 3), 0, 0)),
            ],
            scratch_shapes=[
                pltpu.VMEM((M, 768), F32),
                pltpu.VMEM((M, 768), F32),
                pltpu.VMEM((M, 128), F32),
                pltpu.VMEM((M, 768), F32),
                pltpu.VMEM((4, M, 768), BF),
            ],
        ),
        out_shape=[
            jax.ShapeDtypeStruct((M, 768), BF),
            jax.ShapeDtypeStruct((M, 3072), BF),
            jax.ShapeDtypeStruct((M, 3072), BF),
        ]
        + [jax.ShapeDtypeStruct((M, 768), BF)] * 4
        + [
            jax.ShapeDtypeStruct((4, pairs * 256, PW), BF),
            jax.ShapeDtypeStruct((4, R, 256, LW), F32),
            jax.ShapeDtypeStruct((8, 768), F32),
            jax.ShapeDtypeStruct((4, 1, 768), F32),
        ],
        cost_estimate=cost(40),
        compiler_params=pltpu.CompilerParams(vmem_limit_bytes=VM),
    )(idx, *[f.reshape(pairs, 4, 256, PW) for f in firsts], *atts, out_grad, pw, iw, ow, ib, vec)


BULK = 1792


def ffw_kernel(idx_ref, act_ref, din_ref, ml_ref, do_ref, dp_ref, att_ref, sums_ref, ibg_ref, keep_ref, send_ref):
    c = pl.program_id(0)
    index = idx_ref[0]

    def put(b, rows, value):
        m = index ^ b

        @pl.when((m & 1) == 0)
        def _():
            keep_ref[m >> 1, rows] = value

        @pl.when((m & 1) == 1)
        def _():
            send_ref[m >> 1, rows] = value

    put(c, pl.ds(0, 768), dot_tn(ml_ref[...], din_ref[...]).astype(BF))
    outer = dot_tn(do_ref[...], act_ref[...]).astype(BF)
    for b in range(4):
        put(b, pl.ds(pl.multiple_of(768 + LW * c, LW), LW), outer[LW * b : LW * b + LW])

    @pl.when(c == 0)
    def _():
        proj = dot_tn(dp_ref[...], att_ref[...]).astype(BF)
        for b in range(4):
            put(b, pl.ds(1536, LW), proj[LW * b : LW * b + LW])
            small = jnp.concatenate([sums_ref[:, LW * b : LW * b + LW], jnp.zeros((8, 576), F32)], axis=1)
            small = jnp.concatenate([small, ibg_ref[b], jnp.zeros((7, 768), F32)], axis=0)
            put(b, pl.ds(1728, 16), small.astype(BF))
            put(b, pl.ds(1744, 48), jnp.zeros((48, 768), BF))


def ffw(idx, act, din, ml, do, dp, att, sums, ibg):
    M = ml.shape[0]
    col = pl.BlockSpec((M, 768), lambda i, x: (0, i))
    whole = lambda *s: pl.BlockSpec(s, lambda i, x: (0,) * len(s))
    return pl.pallas_call(
        ffw_kernel,
        grid_spec=pltpu.PrefetchScalarGridSpec(
            num_scalar_prefetch=1,
            grid=(4,),
            in_specs=[col, col] + [whole(M, 768)] * 4 + [whole(8, 768), whole(4, 1, 768)],
            out_specs=[whole(2, BULK, 768)] * 2,
        ),
        out_shape=[jax.ShapeDtypeStruct((2, BULK, 768), BF)] * 2,
        cost_estimate=cost(15),
        compiler_params=pltpu.CompilerParams(vmem_limit_bytes=VM),
    )(idx, act, din, ml, do, dp, att, sums, ibg)


def taps_kernel(own_ref, coef_ref, dir_ref, out_ref, tmp):
    n = dir_ref.shape[0]
    for k in range(n):
        tmp[48 * k : 48 * k + 48] = (dir_ref[k].astype(F32) * coef_ref[pl.program_id(0) * n + k]).astype(BF)
    row = lax.broadcasted_iota(jnp.int32, (PW, 256), 0)
    lane = lax.broadcasted_iota(jnp.int32, (PW, 256), 1)
    pick = ((row == lane + LW * (own_ref[0] & 1)) & (lane < LW)).astype(F32).astype(BF)
    out_ref[...] = dot(tmp[...], pick)[:, :LW].astype(BF)


def own_taps(idx, coef, tap_dir, deps=()):
    return pl.pallas_call(
        skip(taps_kernel, 3, len(deps)),
        grid_spec=pltpu.PrefetchScalarGridSpec(
            num_scalar_prefetch=2,
            grid=(8,),
            in_specs=[pl.BlockSpec((16, 48, PW), lambda i, x, c: (i, 0, x[0] // 2))] + [ANY] * len(deps),
            out_specs=pl.BlockSpec((768, LW), lambda i, x, c: (i, 0)),
            scratch_shapes=[pltpu.VMEM((768, PW), BF)],
        ),
        out_shape=jax.ShapeDtypeStruct((6144, LW), BF),
        cost_estimate=cost(5),
        compiler_params=pltpu.CompilerParams(vmem_limit_bytes=VM),
    )(idx, coef, tap_dir, *deps)


def dots_kernel(tap_ref, dir_ref, out_ref):
    g = tap_ref[0].astype(F32).T
    p = g * dir_ref[...].astype(F32)
    rows = [jnp.sum(p[48 * t : 48 * t + 48], axis=0, keepdims=True) for t in range(16)]
    s = jnp.sum(jnp.concatenate(rows, axis=0), axis=1, keepdims=True)
    out_ref[0] = jnp.broadcast_to(s, (16, 128))


def tap_dots(tap, dirs, deps=()):
    return pl.pallas_call(
        skip(dots_kernel, 2, len(deps)),
        grid=(8,),
        in_specs=[pl.BlockSpec((1, LW, 768), lambda i: (i, 0, 0)), pl.BlockSpec((768, LW), lambda i: (i, 0))] + [ANY] * len(deps),
        out_specs=pl.BlockSpec((1, 16, 128), lambda i: (i, 0, 0)),
        out_shape=jax.ShapeDtypeStruct((8, 16, 128), F32),
        cost_estimate=cost(6),
        compiler_params=pltpu.CompilerParams(vmem_limit_bytes=VM),
    )(tap, dirs, *deps)


def last_kernel(tap_ref, dir_ref, coef_ref, beta_ref, out_ref, turned):
    i = pl.program_id(0)

    @pl.when(i == 0)
    def _():
        for J in range(8):
            t = tap_ref[J].astype(F32).T
            turned[0, 768 * J : 768 * J + 768] = t[:, :128]
            turned[1, 768 * J : 768 * J + 768, :64] = t[:, 128:]

    for c in range(8):
        at = pl.ds(8 * i + c, 128, stride=48)
        g = jnp.concatenate([turned[0, at].T, turned[1, at].T[:64]], axis=0)
        out_ref[c] = g * coef_ref[...] - dir_ref[c].astype(F32) * beta_ref[...]


def last_taps(coef, beta, taps, dirs):
    row = pl.BlockSpec((1, 128), lambda i: (0, 0))
    block = pl.BlockSpec((8, LW, 128), lambda i: (i, 0, 0))
    return pl.pallas_call(
        last_kernel,
        grid=(6,),
        in_specs=[pl.BlockSpec((8, LW, 768), lambda i: (0, 0, 0)), block, row, row],
        out_specs=block,
        out_shape=jax.ShapeDtypeStruct((48, LW, 128), F32),
        scratch_shapes=[pltpu.VMEM((2, 6144, 128), F32)],
        cost_estimate=cost(8),
        compiler_params=pltpu.CompilerParams(vmem_limit_bytes=VM),
    )(taps, dirs, coef[None], beta[None])


def swap(x, axis, bit):
    return lax.ppermute(x, axis, [(i, i ^ bit) for i in range(lax.axis_size(axis))])


def pick_half(x, axis, bit, dim):
    on = (lax.axis_index(axis) & bit) != 0
    lo, hi = jnp.split(x, 2, axis=dim)
    return jnp.where(on, lo, hi), jnp.where(on, hi, lo)


def double(x, axis, bit):
    on = (lax.axis_index(axis) & bit) != 0
    got = swap(x, axis, bit)
    return jnp.concatenate([jnp.where(on, got, x), jnp.where(on, x, got)], axis=0)


class RowSum:
    def __init__(self, x, dim=0):
        n = lax.axis_size("rows")
        bits = [1 << i for i in range(n.bit_length() - 1)]
        self.orders = (bits, bits[1::-1] + bits[2:])
        self.dim = dim
        self.count = x.shape[dim]
        full = -(-self.count // (8 * n)) * (8 * n)
        if full != self.count:
            widths = [(0, 0)] * x.ndim
            widths[dim] = (0, full - self.count)
            x = jnp.pad(x, widths)
        cut_at = -(-full // (16 * n)) * (8 * n)
        self.parts = [lax.slice_in_dim(x, 0, cut_at, axis=dim), lax.slice_in_dim(x, cut_at, full, axis=dim)]
        self.stage = 0
        self.cut()

    def cut(self):
        pairs = [pick_half(p, "rows", o[self.stage], self.dim) for p, o in zip(self.parts, self.orders)]
        self.sends = [p[0] for p in pairs]
        self.keeps = [p[1] for p in pairs]

    def done(self):
        return self.stage == len(self.orders[0])

    def step(self, after=None):
        if after is not None:
            self.keeps = [late(k, after) for k in self.keeps]
        self.parts = [
            (k.astype(F32) + swap(s, "rows", o[self.stage]).astype(F32)).astype(BF)
            for k, s, o in zip(self.keeps, self.sends, self.orders)
        ]
        self.stage += 1
        if not self.done():
            self.cut()

    def finish(self):
        while not self.done():
            self.step()
        parts = self.parts
        if self.dim:
            parts = [(p[0].astype(F32) + swap(p[1], "seq", 2).astype(F32)).astype(BF) for p in parts]
        for s in reversed(range(len(self.orders[0]))):
            parts = [double(p, "rows", o[s]) for p, o in zip(parts, self.orders)]
        return jnp.concatenate(parts, axis=0)[: self.count]


def late(x, after):
    return x + (after[(0,) * after.ndim].astype(F32) * 0.0).astype(x.dtype)


def gather_seq(x):
    far = swap(x, "seq", 2)
    near = swap(x, "seq", 1)
    return [x, near, far, swap(far, "seq", 1)]


def trade(blocks):
    return [blocks[0], swap(blocks[1], "seq", 1), swap(blocks[2], "seq", 2), swap(blocks[3], "seq", 3)]


def scatter_pair(keep, send):
    got = swap(send, "seq", 1).astype(F32)
    far = (keep[1].astype(F32) + got[1]).astype(BF)
    return keep[0].astype(F32) + got[0], far


def all_sum(x, axis):
    for i in range(lax.axis_size(axis).bit_length() - 1):
        x = x + swap(x, axis, 1 << i)
    return x


def assemble(blocks, index):
    low = (index & 1) != 0
    high = (index & 2) != 0
    b = [jnp.where(low, blocks[m ^ 1], blocks[m]) for m in range(4)]
    return [jnp.where(high, b[m ^ 2], b[m]) for m in range(4)]


def cut(x, start, size, axis):
    return lax.dynamic_slice_in_dim(x, start, size, axis)


def local(
    frames,
    utterance_lengths,
    tap_dir,
    tap_scale,
    conv_bias,
    pos_gain,
    pos_shift,
    query_weight,
    query_bias,
    key_weight,
    value_weight,
    value_bias,
    proj_weight,
    proj_bias,
    attend_gain,
    attend_shift,
    inner_weight,
    inner_bias,
    outer_weight,
    outer_bias,
    final_gain,
    final_shift,
    out_grad,
):
    R = frames.shape[0]
    index = lax.axis_index("seq")
    idx = jnp.full((1,), index, jnp.int32)
    ends = jnp.cumsum(utterance_lengths, axis=1, dtype=jnp.int32)
    order = [index ^ m for m in range(4)]
    own = index * LW

    def packed(x):
        return jnp.concatenate([x[0::2], x[1::2]], axis=2).reshape(R * 128, PW)

    sent = trade([packed(cut(frames, b * LW, LW, 2)) for b in order])
    squares = jnp.sum(jnp.square(tap_dir.astype(F32)), axis=(1, 2))
    coef = tap_scale * lax.rsqrt(squares)
    w = build_w(own_taps(idx, coef, tap_dir))
    bias4 = jnp.tile(cut(conv_bias, own, LW, 0).reshape(4, 1, 48), (1, 4, 1)).reshape(4, 1, LW)
    first, pre, xs = conv_fwd(ends, idx, sent, w, bias4)
    firsts = gather_seq(first)

    def xor_rows(a):
        return jnp.stack([cut(a, b * LW, LW, 0) for b in order])

    def pad_to(a, axis, size):
        widths = [(0, 0)] * a.ndim
        widths[axis] = (0, size - a.shape[axis])
        return jnp.pad(a, widths)

    own_cols = [
        pad_to(cut(a, own, LW, 1), 1, 256)
        for a in (query_weight * jnp.asarray(0.125, BF), key_weight, value_weight)
    ]
    w_qkv = pad_to(xor_rows(jnp.concatenate(own_cols, axis=1)), 1, 256)
    b_qkv = jnp.concatenate(
        [
            pad_to(cut(query_bias, own, LW, 0) * 0.125, 0, 512),
            pad_to(cut(value_bias, own, LW, 0), 0, 256),
        ]
    )[None]
    gain_x = xor_rows(pos_gain)[:, None]
    shift_x = xor_rows(pos_shift)[:, None]
    q, k, v, mixed_low, stat = qkv(firsts, w_qkv, b_qkv, gain_x, shift_x)
    att, att_full, lse = attn(idx, ends, q, k, v)
    att_blocks = trade([att[m] for m in range(4)])

    vecs = jnp.stack([pos_gain, pos_shift, proj_bias, attend_gain, attend_shift, outer_bias, final_gain, final_shift])
    layer_out, act, d_inner, middle_low, d_outer, d_proj, attended, d_att, second_x, sums, inner_sums = ff(
        idx, firsts, att_blocks, out_grad.reshape(R * 256, 768), proj_weight, inner_weight, outer_weight,
        inner_bias.reshape(4, 1, 768), vecs,
    )
    dos = trade_out(d_att)
    keep, send = ffw(idx, act, d_inner, middle_low, d_outer, d_proj, attended, sums, inner_sums)

    heads = attn_bwd(0, idx, ends, q, k, v, att_full, dos, lse)
    bulk = RowSum((late(keep, heads[0]).astype(F32) + swap(send, "seq", 1).astype(F32)).astype(BF), 1)
    heads += attn_bwd(1, idx, ends, q, k, v, att_full, dos, lse, tuple(bulk.sends))
    keep, send, moments = dmix(idx, heads, w_qkv, second_x, firsts, stat, gain_x)
    e_near, e_far = scatter_pair(keep, send)
    bulk.step(send)
    g_qkv, b_grads = qkvw(heads, mixed_low, (e_far, *bulk.sends))
    e_far = swap(e_far, "seq", 2)
    m1 = moments + swap(moments, "seq", 1)
    moments = (m1 + swap(m1, "seq", 2)).reshape(R * 4, 8, 256)

    tap_part, ds, d4, conv_b, vec = tap_grads(
        ends, e_near, e_far, first, stat.reshape(R * 1024, 128), moments, cut(pos_gain, own, LW, 0)[None], pre, xs, g_qkv,
    )
    if R > 2:
        tap_part = jnp.sum(tap_part.astype(F32), axis=0, keepdims=True).astype(BF)
    tap_part = tap_part[0]
    tap_sum = RowSum(tap_part.reshape(11 * LW, 768))
    bulk.step(tap_part)
    part = conv_back(0, ends, idx, ds, d4, w, None, tuple(tap_sum.sends + bulk.sends))
    tap_sum.step(part)
    back = conv_back(2, ends, idx, ds, d4, w, part, tuple(tap_sum.sends))
    tap_sum.step(back)
    bulk.step(back)
    dir_own = own_taps(idx, jnp.ones((128,), F32), tap_dir, tuple(tap_sum.sends + bulk.parts))
    dir_turned = jnp.transpose(dir_own.reshape(128, 48, LW), (1, 2, 0))
    dots = all_sum(tap_dots(tap_part, dir_own)[:, :, 0], "seq")
    back = trade_out(back)
    back = jnp.concatenate([b.reshape(R // 2, 1, 256, PW) for b in assemble(back, index)], axis=1)
    back = back.reshape(R // 2, 4, 256, 2, LW)
    frames_grad = jnp.transpose(back, (0, 3, 2, 1, 4)).reshape(R, 256, 768)
    bulk_sum = bulk.finish()
    t_inner = bulk_sum[:768].astype(F32)
    t_outer = jnp.concatenate([bulk_sum[768 + LW * i : 768 + LW * i + LW] for i in range(4)], axis=1).astype(F32).T
    t_proj = bulk_sum[1536:1728].astype(F32).T
    small = bulk_sum[1728:1744].astype(F32)
    tap_total = tap_sum.finish().reshape(11, LW, 768)
    qkv_std = assemble([tap_total[8:, :, LW * m : LW * m + LW] for m in range(4)], index)
    t_qkv = jnp.concatenate(qkv_std, axis=2).astype(F32)
    lates = jnp.concatenate(
        [
            jnp.sum(conv_b, axis=(0, 2)).reshape(4, 4, 48).sum(1).reshape(LW),
            jnp.sum(vec[:, 0], axis=0),
            jnp.sum(vec[:, 1], axis=0),
            b_grads[0, 0:LW] * 0.125,
            b_grads[0, 512 : 512 + LW],
            dots.reshape(128),
            jnp.zeros((2048 - 1088,), F32),
        ]
    )
    lates = all_sum(lates.reshape(16, 128), "rows").reshape(2048)
    dots = lates[5 * LW : 5 * LW + 128]
    inverse = lax.rsqrt(squares)
    g_tap_dir = jnp.transpose(last_taps(coef, coef * dots * inverse * inverse, tap_total, dir_turned), (2, 0, 1))
    g_tap_scale = cut(dots * inverse, index * 32, 32, 0)

    return (
        layer_out.reshape(R, 256, 768),
        frames_grad,
        g_tap_dir,
        g_tap_scale,
        lates[0:LW],
        lates[LW : 2 * LW],
        lates[2 * LW : 3 * LW],
        t_qkv[0].T * 0.125,
        lates[3 * LW : 4 * LW],
        t_qkv[1].T,
        t_qkv[2].T,
        lates[4 * LW : 5 * LW],
        t_proj,
        small[5, :LW],
        small[3, :LW],
        small[4, :LW],
        t_inner,
        small[8],
        t_outer,
        small[2, :LW],
        small[0, :LW],
        small[1, :LW],
    )


def trade_out(x):
    return trade([x[m] for m in range(4)])


def solution(mesh):
    split = P("rows", "seq", None)
    col = P(None, "seq")
    one = P("seq")
    return jax.shard_map(
        local,
        mesh=mesh,
        in_specs=(split, P("rows", None)) + (P(),) * 20 + (split,),
        out_specs=(split, split, P(None, None, "seq"), one, one, one, one)
        + (col, one, col, col, one, col, one, one, one, col, one, col, one, one, one),
        check_vma=False,
    )
```

```python
import jax, jax.numpy as jnp
from jax import lax
from jax.sharding import PartitionSpec as P
from jax.experimental import pallas as pl
from jax.experimental.pallas import tpu as pltpu
F32=jnp.float32; BF=jnp.bfloat16
CH=48; PH=4; LW=PH*CH
NJ=33; SEGL=48; XROWS=(SEGL+NJ-1)*16; MROWS=SEGL*16
VM=60*1024*1024

def cost(us):
    return pl.CostEstimate(flops=int(us*1.0e9),bytes_accessed=int(us*3.0e6),transcendentals=0)

ANY=pl.BlockSpec(memory_space=pl.ANY)
PW=2*LW

def skip(kernel,at,count):
    if not count:
        return kernel
    return lambda *refs: kernel(*refs[:at],*refs[at+count:])

def dot(a,b): return jnp.dot(a,b,preferred_element_type=F32)
def dot_nt(a,b): return lax.dot_general(a,b,(((1,),(1,)),((),())),preferred_element_type=F32)
def dot_tn(a,b): return lax.dot_general(a,b,(((0,),(0,)),((),())),preferred_element_type=F32)

def erf_gelu_parts(v):
    phi=0.5*(1.0+lax.erf(v*0.7071067811865476))
    return phi

WROWS=6400
def build_w_kernel(t_ref, w_ref, tp, rs):
    g=pl.program_id(0)
    rows=t_ref.shape[0]
    @pl.when(g==0)
    def _():
        tp[0:144,:]=jnp.zeros((144,LW),BF)
        tp[144:144+rows,:]=t_ref[...]
        tp[144+rows:,:]=jnp.zeros((256,LW),BF)
    src=lax.broadcasted_iota(jnp.int32,(LW,256),0); l=lax.broadcasted_iota(jnp.int32,(LW,256),1)
    pick=((src==48*g+lax.rem(l,48))&(l<LW)).astype(F32).astype(BF)
    n=640
    lane=lax.broadcasted_iota(jnp.int32,(n,256),1)
    for i in range(WROWS//n):
        r0=i*n
        R=dot(tp[r0:r0+n+144,:],pick).astype(BF)
        lo=jnp.where(lane[:,:128]<96,jnp.where(lane[:,:128]<48,R[144:144+n,:128],R[96:96+n,:128]),R[48:48+n,:128])
        hi=jnp.where(lane[:,128:]<144,R[48:48+n,128:],R[0:n,128:])
        w_ref[0,r0:r0+n,:128]=lo
        w_ref[0,r0:r0+n,128:]=hi

def build_w(taps2):
    rows=taps2.shape[0]
    return pl.pallas_call(build_w_kernel,grid=(4,),
        in_specs=[pl.BlockSpec((rows,LW),lambda g:(0,0))],
        out_specs=pl.BlockSpec((1,WROWS,256),lambda g:(g,0,0)),
        out_shape=jax.ShapeDtypeStruct((4,WROWS,256),BF),
        scratch_shapes=[pltpu.VMEM((rows+144+256,LW),BF),pltpu.VMEM((640+144,256),BF)],
        cost_estimate=cost(10),
        compiler_params=pltpu.CompilerParams(vmem_limit_bytes=VM))(taps2)

def sload(ref,start,n,stride):
    return jnp.concatenate([ref[0,pl.ds(start,n,stride=stride),:],ref[1,pl.ds(start,n,stride=stride),:]],axis=1)[:,:LW]
def sstore(ref,start,n,stride,v):
    ref[0,pl.ds(start,n,stride=stride),:]=v[:,:128]
    ref[1,pl.ds(start,n,stride=stride),:]=jnp.concatenate([v[:,128:],jnp.zeros((n,64),v.dtype)],axis=1)
def fload(ref,start,n):
    return jnp.concatenate([ref[0,pl.ds(start,n),:],ref[1,pl.ds(start,n),:]],axis=1)[:,:LW]
def fstore(ref,start,n,v):
    ref[0,pl.ds(start,n),:]=v[:,:128]
    ref[1,pl.ds(start,n),:]=jnp.concatenate([v[:,128:],jnp.zeros((n,64),v.dtype)],axis=1)

def pick_matrix(g,a):
    ch=lax.broadcasted_iota(jnp.int32,(LW,256),0); l=lax.broadcasted_iota(jnp.int32,(LW,256),1)
    return ((ch==48*g+(l-48*a))&(l>=48*a)&(l<48*a+48)).astype(F32).astype(BF)

def pick_back(g,a):
    l=lax.broadcasted_iota(jnp.int32,(LW,256),0); ch=lax.broadcasted_iota(jnp.int32,(LW,256),1)
    return ((ch==48*g+(l-48*a))&(l>=48*a)&(l<48*a+48)).astype(F32).astype(BF)

def fill_ids(seg_ref,pair,sid):
    sub=lax.broadcasted_iota(jnp.int32,(256,LW),0); l=lax.broadcasted_iota(jnp.int32,(256,LW),1)
    t=4*sub+(l>=48).astype(jnp.int32)+(l>=96).astype(jnp.int32)+(l>=144).astype(jnp.int32)
    for r in range(2):
        v=jnp.zeros((256,LW),jnp.int32)
        for q in range(7):
            v=v+(t>=seg_ref[pair*2+r,q]).astype(jnp.int32)
        sid[pl.ds(256*r,256),:]=v

TAIL=48
def respace(sid,src,xr,xsf):
    xsf[0,1280:1280+TAIL,:]=jnp.zeros((TAIL,128),F32); xsf[1,1280:1280+TAIL,:]=jnp.zeros((TAIL,128),F32)
    for r in range(2):
        for B in range(26):
            v=jnp.zeros((16,LW),F32)
            for q in range(8):
                bb=B-1-q
                if 0<=bb<16:
                    rows=pl.ds(r*256+16*bb,16)
                    v=jnp.where(sid[rows,:]==q,src[rows,:],v)
            xr[r,pl.ds(16*B,16),:]=v
        for sp in range(8):
            sstore(xsf,r*8+sp,80,16,xr[r,pl.ds(48*sp,80),:])

def unspace(sid,acc,yr,emit):
    for r in range(2):
        for sp in range(8):
            yr[r,pl.ds(48*sp,48),:]=sload(acc,r*8+sp,48,16)
        for bb in range(16):
            v=jnp.zeros((16,LW),F32)
            ids=sid[pl.ds(r*256+16*bb,16),:]
            for q in range(8):
                v=jnp.where(ids==q,yr[r,pl.ds(16*(bb+q),16),:],v)
            emit(r*256+16*bb,v)

def conv_fwd_kernel(seg_ref,idx_ref,x0_ref,x1_ref,x2_ref,x3_ref,w_ref,bias_ref,first_ref,pre_ref,xs_ref,xt,xa,x4,xr,xsf,acc,yr,facc,sid):
    pair=pl.program_id(0); g=pl.program_id(1)
    @pl.when(g==0)
    def _():
        fill_ids(seg_ref,pair,sid)
        for m,x_ref in enumerate((x0_ref,x1_ref,x2_ref,x3_ref)):
            k=pl.multiple_of((idx_ref[0]^m)*256,256)
            for r in range(2):
                fstore(xt,r*1024+k,256,x_ref[...].astype(F32)[:,LW*r:LW*r+LW])
        for a in range(4):
            xa[a]=sload(xt,a,512,4).astype(BF)
    v=dot(xa[0],pick_matrix(g,0))
    for a in range(1,4):
        v=v+dot(xa[a],pick_matrix(g,a))
    x4[...]=v[:,:LW]
    respace(sid,x4,xr,xsf)
    n=XROWS+32
    zt=jnp.zeros((n+16,64),F32)
    va=xsf[0,0:n+16,:]; vb=xsf[1,0:n+16,:]
    z0=jnp.concatenate([zt,va[:,:64]],axis=1); z1=jnp.concatenate([va[:,64:],vb[:,:64]],axis=1)
    for at,piece in enumerate((va[0:n].astype(BF),(vb[0:n]+z0[16:]).astype(BF),z1[16:].astype(BF))):
        xs_ref[0,0,:,128*at:128*at+128]=piece[:XROWS]
        xs_ref[0,0,:,384+128*at:512+128*at]=piece[32:]
    s=dot(xs_ref[0,0,512:512+MROWS,0:256],w_ref[0,6144:6400,:])
    for J in range(8):
        s=s+dot(xs_ref[0,0,64*J:64*J+MROWS,:],w_ref[0,768*J:768*J+768,:])
    acc[0]=s[:,:128]; acc[1]=s[:,128:]
    bias=bias_ref[0]
    def emit(row,v):
        pre_ref[0,0,pl.ds(row,16),:]=v+bias
    unspace(sid,acc,yr,emit)
    pre=pre_ref[0,0]
    fs=(x4[...]+pre*erf_gelu_parts(pre)).astype(BF)
    for a in range(4):
        f=dot(fs,pick_back(g,a))[:,:LW]
        @pl.when(g==0)
        def _(): facc[a]=f
        @pl.when(g>0)
        def _(): facc[a]=facc[a]+f
    @pl.when(g==3)
    def _():
        for a in range(4):
            sstore(xt,a,512,4,facc[a])
        first_ref[...]=jnp.concatenate([fload(xt,0,1024),fload(xt,1024,1024)],axis=1).astype(BF)

def conv_fwd(ends,idx,xs4,w,bias4):
    pairs=xs4[0].shape[0]//256
    return pl.pallas_call(conv_fwd_kernel,grid=(pairs,4),
        in_specs=[pl.BlockSpec(memory_space=pltpu.SMEM)]*2+[pl.BlockSpec((256,PW),lambda p,g:(p,0))]*4+[
                  pl.BlockSpec((1,WROWS,256),lambda p,g:(g,0,0)),
                  pl.BlockSpec((1,1,LW),lambda p,g:(g,0,0))],
        out_specs=[pl.BlockSpec((1024,PW),lambda p,g:(p,0)),
                   pl.BlockSpec((1,1,512,LW),lambda p,g:(p,g,0,0)),
                   pl.BlockSpec((1,1,XROWS,768),lambda p,g:(p,g,0,0))],
        out_shape=[jax.ShapeDtypeStruct((pairs*1024,PW),BF),
                   jax.ShapeDtypeStruct((pairs,4,512,LW),F32),
                   jax.ShapeDtypeStruct((pairs,4,XROWS,768),BF)],
        scratch_shapes=[pltpu.VMEM((2,2048,128),F32),pltpu.VMEM((4,512,LW),BF),pltpu.VMEM((512,LW),F32),
            pltpu.VMEM((2,416,LW),F32),pltpu.VMEM((2,XROWS+TAIL,128),F32),pltpu.VMEM((2,MROWS,128),F32),pltpu.VMEM((2,384,LW),F32),
            pltpu.VMEM((4,512,LW),F32),pltpu.VMEM((512,LW),jnp.int32)],
        cost_estimate=cost(35),
        compiler_params=pltpu.CompilerParams(vmem_limit_bytes=VM))(ends,idx,*xs4,w,bias4)

def tap_kernel(seg_ref,e0_ref,e1_ref,first_ref,stat_ref,mom_ref,mox_ref,gain_ref,pre_ref,xs_ref,qkv_ref,tap_ref,ds_ref,d4_ref,bias_ref,vec_ref,xt,xa,dc,xr,xsf,A,sid):
    pair=pl.program_id(0); g=pl.program_id(1)
    @pl.when(g==0)
    def _():
        fill_ids(seg_ref,pair,sid)
        gain=gain_ref[...]
        sg=jnp.zeros((1,LW),F32); sh=jnp.zeros((1,LW),F32)
        for t in range(8):
            r,k=t//4,t%4
            rows=slice(256*k,256*k+256); cols=slice(LW*r,LW*r+LW)
            e=(e0_ref[rows]+e1_ref[rows].astype(F32))[:,cols]
            st=stat_ref[256*t:256*t+256]
            mean=st[:,0:1]; rstd=st[:,1:2]
            mom=jnp.concatenate([mom_ref[t,0:2]+mox_ref[2*t:2*t+2].astype(F32)[:,:256],jnp.zeros((126,256),F32)],axis=0).T*(1.0/768)
            xhat=(first_ref[rows].astype(F32)[:,cols]-mean)*rstd
            sg=sg+jnp.sum(e*xhat,axis=0,keepdims=True); sh=sh+jnp.sum(e,axis=0,keepdims=True)
            fstore(xt,256*t,256,rstd*(e*gain-mom[:,0:1]-xhat*mom[:,1:2]))
        vec_ref[0,0:1]=sg; vec_ref[0,1:2]=sh; vec_ref[0,2:8]=jnp.zeros((6,LW),F32)
        for a in range(4):
            xa[a]=sload(xt,a,512,4).astype(BF)
    v=dot(xa[0],pick_matrix(g,0))
    for a in range(1,4):
        v=v+dot(xa[a],pick_matrix(g,a))
    v=v[:,:LW]
    d4_ref[0,0]=v.astype(BF)
    pre=pre_ref[0,0]
    cdf=erf_gelu_parts(pre)
    slope=cdf+pre*(jnp.exp(-0.5*pre*pre)*0.3989422804014327)
    d=v*slope
    dc[...]=d
    bias_ref[0,0]=jnp.sum(d,axis=0,keepdims=True)
    respace(sid,dc,xr,xsf)
    ds_ref[0,0,:,0:128]=xsf[0,0:XROWS].astype(BF); ds_ref[0,0,:,128:256]=xsf[1,0:XROWS].astype(BF)
    DT=fload(xsf,256,MROWS).astype(BF).T
    for J in range(8):
        A[:,768*J:768*J+768]=dot(DT,xs_ref[0,0,64*J:64*J+MROWS,:])
    A[:,6144:6400]=dot(DT,xs_ref[0,0,512:512+MROWS,0:256])
    n=6144
    o=A[0:48,0:n]
    for b in range(1,4):
        o=o+A[48*b:48*b+48,48*b:48*b+n]
    for J in range(8):
        tap_ref[0,J]=o[:,768*J:768*J+768].astype(BF)
    tap_ref[0,8:11]=jnp.where(pair==0,qkv_ref[...],jnp.zeros((3,48,768),BF))

def tap_grads(ends,e0,e1,first,stat,mom,gain,pre,xs,g_qkv,deps=()):
    pairs=e0.shape[0]//1024
    return pl.pallas_call(skip(tap_kernel,11,len(deps)),grid=(pairs,4),
        in_specs=[pl.BlockSpec(memory_space=pltpu.SMEM),
                  pl.BlockSpec((1024,PW),lambda p,g:(p,0)),
                  pl.BlockSpec((1024,PW),lambda p,g:(p,0)),
                  pl.BlockSpec((1024,PW),lambda p,g:(p,0)),
                  pl.BlockSpec((2048,128),lambda p,g:(p,0)),
                  pl.BlockSpec((8,8,256),lambda p,g:(p,0,0)),
                  pl.BlockSpec((16,PW),lambda p,g:(64*pairs+p,0)),
                  pl.BlockSpec((1,LW),lambda p,g:(0,0)),
                  pl.BlockSpec((1,1,512,LW),lambda p,g:(p,g,0,0)),
                  pl.BlockSpec((1,1,XROWS,768),lambda p,g:(p,g,0,0)),
                  pl.BlockSpec((3,48,768),lambda p,g:(0,g,0))]+[ANY]*len(deps),
        out_specs=[pl.BlockSpec((1,11,48,768),lambda p,g:(p,0,g,0)),
                   pl.BlockSpec((1,1,XROWS,256),lambda p,g:(p,g,0,0)),
                   pl.BlockSpec((1,1,512,LW),lambda p,g:(p,g,0,0)),
                   pl.BlockSpec((1,1,1,LW),lambda p,g:(p,g,0,0)),
                   pl.BlockSpec((1,8,LW),lambda p,g:(p,0,0))],
        out_shape=[jax.ShapeDtypeStruct((pairs,11,LW,768),BF),
                   jax.ShapeDtypeStruct((pairs,4,XROWS,256),BF),
                   jax.ShapeDtypeStruct((pairs,4,512,LW),BF),
                   jax.ShapeDtypeStruct((pairs,4,1,LW),F32),jax.ShapeDtypeStruct((pairs,8,LW),F32)],
        scratch_shapes=[pltpu.VMEM((2,2048,128),F32),pltpu.VMEM((4,512,LW),BF),pltpu.VMEM((512,LW),F32),
            pltpu.VMEM((2,416,LW),F32),pltpu.VMEM((2,XROWS+TAIL,128),F32),pltpu.VMEM((LW,6400),F32),pltpu.VMEM((512,LW),jnp.int32)],
        cost_estimate=cost(24),
        compiler_params=pltpu.CompilerParams(vmem_limit_bytes=VM))(ends,e0,e1,first,stat,mom,e1,gain,pre,xs,g_qkv,*deps)

def back_kernel(at,seg_ref,idx_ref,ds_ref,d4_ref,w_ref,*rest):
    if at:
        part_ref,out_ref,xt,acc,yr,fs,sid=rest
    else:
        facc,acc,yr,fs,sid=rest
    pair=pl.program_id(0); i=pl.program_id(1); g=i+at
    @pl.when(i==0)
    def _(): fill_ids(seg_ref,pair,sid)
    s=None
    for j in range(NJ):
        p=dot_nt(ds_ref[0,0,16*(NJ-1-j):16*(NJ-1-j)+MROWS,:],w_ref[0,LW*j:LW*j+256,:])
        s=p if s is None else s+p
    def emit(row,v):
        fs[pl.ds(row,16),:]=(v+d4_ref[0,0,pl.ds(row,16),:].astype(F32)).astype(BF)
    acc[0]=s[:,:128]; acc[1]=s[:,128:]
    unspace(sid,acc,yr,emit)
    if at:
        for a in range(4):
            f=dot(fs[...],pick_back(g,a))[:,:LW]
            @pl.when(i==0)
            def _(): sstore(xt,a,512,4,f+part_ref[0,a])
            @pl.when(i>0)
            def _(): sstore(xt,a,512,4,f+sload(xt,a,512,4))
        @pl.when(i==1)
        def _():
            for k in range(4):
                out_ref[idx_ref[0]^k]=jnp.concatenate([fload(xt,k*256,256),fload(xt,1024+k*256,256)],axis=1).astype(BF)
    else:
        for a in range(4):
            f=dot(fs[...],pick_back(g,a))[:,:LW]
            @pl.when(i==0)
            def _(): facc[0,a]=f
            @pl.when(i>0)
            def _(): facc[0,a]=facc[0,a]+f

def conv_back(at,ends,idx,ds,d4,w,part=None,deps=()):
    pairs=ds.shape[0]
    parts=() if part is None else (part,)
    facc=pl.BlockSpec((1,4,512,LW),lambda p,g:(p,0,0,0))
    scratch=[pltpu.VMEM((2,2048,128),F32)] if at else []
    return pl.pallas_call(skip(lambda *refs: back_kernel(at,*refs),5+len(parts),len(deps)),grid=(pairs,2),
        in_specs=[pl.BlockSpec(memory_space=pltpu.SMEM),pl.BlockSpec(memory_space=pltpu.SMEM),
                  pl.BlockSpec((1,1,XROWS,256),lambda p,g:(p,g+at,0,0)),
                  pl.BlockSpec((1,1,512,LW),lambda p,g:(p,g+at,0,0)),
                  pl.BlockSpec((1,WROWS,256),lambda p,g:(g+at,0,0))]+[facc]*len(parts)+[ANY]*len(deps),
        out_specs=pl.BlockSpec((4,256,PW),lambda p,g:(0,p,0)) if at else facc,
        out_shape=jax.ShapeDtypeStruct((4,pairs*256,PW),BF) if at else jax.ShapeDtypeStruct((pairs,4,512,LW),F32),
        scratch_shapes=scratch+[pltpu.VMEM((2,MROWS,128),F32),pltpu.VMEM((2,384,LW),F32),
            pltpu.VMEM((512,LW),BF),pltpu.VMEM((512,LW),jnp.int32)],
        cost_estimate=cost(100),
        compiler_params=pltpu.CompilerParams(vmem_limit_bytes=VM))(ends,idx,ds,d4,w,*parts,*deps)


def qkv_kernel(f0,f1,f2,f3,w_ref,bias_ref,gain_ref,shift_ref,q_ref,k_ref,v_ref,ml_ref,stat_ref):
    fs=[f[...].astype(F32) for f in (f0,f1,f2,f3)]
    fs=[jnp.concatenate([f[:,:LW],f[:,LW:]],axis=0) for f in fs]
    mean=sum(jnp.sum(f,axis=1,keepdims=True) for f in fs)*(1.0/768)
    cs=[f-mean for f in fs]
    var=sum(jnp.sum(c*c,axis=1,keepdims=True) for c in cs)*(1.0/768)
    rstd=lax.rsqrt(var+1e-5)
    n=mean.shape[0]
    pad=jnp.zeros((n,64),BF)
    out=None
    for m in range(4):
        ml=(cs[m]*rstd*gain_ref[m]+shift_ref[m]).astype(BF)
        ml_ref[m]=ml.reshape(2,256,LW)
        p=dot(jnp.concatenate([ml,pad],axis=1),w_ref[m])
        out=p if out is None else out+p
    out=(out+bias_ref[...]).astype(BF)
    out=out.reshape(2,256,768)
    q_ref[...]=out[:,:,0:192]; k_ref[...]=out[:,:,256:448]; v_ref[...]=out[:,:,512:704]
    lane=lax.broadcasted_iota(jnp.int32,(n,128),1)
    stat_ref[...]=jnp.where(lane==0,mean,jnp.where(lane==1,rstd,0.0)).reshape(2,256,128)

def qkv(fs,w,bias,gain,shift):
    pairs=fs[0].shape[0]//1024; R=2*pairs
    row=pl.BlockSpec((2,256,LW),lambda p,k:(p,k,0))
    full=lambda a: pl.BlockSpec(a.shape,lambda p,k:(0,)*a.ndim)
    return pl.pallas_call(qkv_kernel,grid=(pairs,4),
        in_specs=[pl.BlockSpec((256,PW),lambda p,k:(4*p+k,0))]*4+[full(w),full(bias),full(gain),full(shift)],
        out_specs=[row]*3+[pl.BlockSpec((4,2,256,LW),lambda p,k:(0,p,k,0)),pl.BlockSpec((2,256,128),lambda p,k:(p,k,0))],
        out_shape=[jax.ShapeDtypeStruct((R,1024,LW),BF)]*3+[jax.ShapeDtypeStruct((4,R,1024,LW),BF),jax.ShapeDtypeStruct((R,1024,128),F32)],
        cost_estimate=cost(10),
        compiler_params=pltpu.CompilerParams(vmem_limit_bytes=VM))(*fs,w,bias,gain,shift)

def seg_vec(seg_ref,r,shape,axis,start):
    t=lax.broadcasted_iota(jnp.int32,shape,axis)+start
    v=jnp.zeros(shape,jnp.int32)
    for i in range(8):
        v=v+(t>=seg_ref[r,i]).astype(jnp.int32)
    return v

def attn_kernel(idx_ref,seg_ref,q_ref,k_ref,v_ref,o_ref,of_ref,lse_ref):
    pair=pl.program_id(0); kb=pl.program_id(1)
    for r in range(2):
        sq=seg_vec(seg_ref,2*pair+r,(256,1),0,kb*256); sk=seg_vec(seg_ref,2*pair+r,(1,1024),1,0)
        same=sq==sk
        outs=[]; rows=[]
        for h in range(3):
            c=slice(64*h,64*h+64)
            s=jnp.where(same,dot_nt(q_ref[r,:,c],k_ref[r,:,c]),-1e30)
            mx=jnp.max(s,axis=1,keepdims=True)
            p=jnp.exp(s-mx)
            tot=jnp.sum(p,axis=1,keepdims=True)
            outs.append(dot(p.astype(BF),v_ref[r,:,c])/tot)
            rows.append(jnp.broadcast_to(mx+jnp.log(tot),(256,128)).T[0:1,:])
        o=jnp.concatenate(outs,axis=1)
        of_ref[r]=o
        o_ref[0,:,LW*r:LW*r+LW]=o.astype(BF)
        lse_ref[r,0]=jnp.concatenate(rows+[jnp.zeros((5,256),F32)],axis=0)

def attn(idx,ends,q,k,v):
    R=ends.shape[0]; pairs=R//2
    blk=pl.BlockSpec((2,256,LW),lambda p,b,i,s:(p,b,0)); full=pl.BlockSpec((2,1024,LW),lambda p,b,i,s:(p,0,0))
    return pl.pallas_call(attn_kernel,
        grid_spec=pltpu.PrefetchScalarGridSpec(num_scalar_prefetch=2,grid=(pairs,4),
        in_specs=[blk,full,full],
        out_specs=[pl.BlockSpec((1,256,PW),lambda p,b,i,s:(b^i[0],p,0)),blk,pl.BlockSpec((2,1,8,256),lambda p,b,i,s:(p,b,0,0))]),
        out_shape=[jax.ShapeDtypeStruct((4,pairs*256,PW),BF),jax.ShapeDtypeStruct((R,1024,LW),F32),jax.ShapeDtypeStruct((R,4,8,256),F32)],
        cost_estimate=cost(18),
        compiler_params=pltpu.CompilerParams(vmem_limit_bytes=VM))(idx,ends,q,k,v)

def attn_bwd_kernel(r,idx_ref,seg_ref,q_ref,k_ref,v_ref,o_ref,d0,d1,d2,d3,lse_ref,dq_ref,dk_ref,dv_ref,dks,dvs):
    pair=pl.program_id(0); kb=pl.program_id(1)
    m=kb^idx_ref[0]
    mine=slice(LW*r,LW*r+LW)
    dod=jnp.where(m<2,jnp.where(m==0,d0[...],d1[...]),jnp.where(m==2,d2[...],d3[...])).astype(F32)[:,mine].astype(BF)
    @pl.when(kb==0)
    def _():
        dks[...]=jnp.zeros_like(dks); dvs[...]=jnp.zeros_like(dvs)
    sq=seg_vec(seg_ref,2*pair+r,(1,256),1,kb*256); sk=seg_vec(seg_ref,2*pair+r,(1024,1),0,0)
    same=sk==sq
    dqs=[]; ks=[]; vs=[]
    for h in range(3):
        c=slice(64*h,64*h+64)
        q=q_ref[0,:,c]; k=k_ref[0,:,c]; do=dod[:,c]
        delta=jnp.sum(do.astype(F32)*o_ref[0,:,c],axis=1,keepdims=True)
        delta=jnp.broadcast_to(delta,(256,128)).T[0:1,:]
        st=jnp.where(same,dot_nt(k,q)-lse_ref[0,0,h:h+1,:],-1e30)
        p=jnp.exp(st)
        dp=dot_nt(v_ref[0,:,c],do)
        ds=(p*(dp-delta)).astype(BF)
        vs.append(dot(p.astype(BF),do)); ks.append(dot(ds,q)); dqs.append(dot_tn(ds,k))
    dks[...]+=jnp.concatenate(ks,axis=1); dvs[...]+=jnp.concatenate(vs,axis=1)
    dq_ref[0]=jnp.concatenate(dqs,axis=1).astype(BF)
    @pl.when(kb==3)
    def _():
        dk_ref[0]=dks[...].astype(BF); dv_ref[0]=dvs[...].astype(BF)

def attn_bwd(r,idx,ends,q,k,v,o,dos,lse,deps=()):
    pairs=ends.shape[0]//2
    blk=pl.BlockSpec((1,256,LW),lambda p,b,i,s:(2*p+r,b,0)); full=pl.BlockSpec((1,1024,LW),lambda p,b,i,s:(2*p+r,0,0))
    out=pl.BlockSpec((1,256,LW),lambda p,b,i,s:(p,b,0)); outs=pl.BlockSpec((1,1024,LW),lambda p,b,i,s:(p,0,0))
    return pl.pallas_call(skip(lambda *refs: attn_bwd_kernel(r,*refs),11,len(deps)),
        grid_spec=pltpu.PrefetchScalarGridSpec(num_scalar_prefetch=2,grid=(pairs,4),
        in_specs=[blk,full,full,blk]+[pl.BlockSpec((256,PW),lambda p,b,i,s:(p,0))]*4+[pl.BlockSpec((1,1,8,256),lambda p,b,i,s:(2*p+r,b,0,0))]+[ANY]*len(deps),
        out_specs=[out,outs,outs],scratch_shapes=[pltpu.VMEM((1024,LW),F32)]*2),
        out_shape=[jax.ShapeDtypeStruct((pairs,1024,LW),BF)]*3,
        cost_estimate=cost(60),
        compiler_params=pltpu.CompilerParams(vmem_limit_bytes=VM))(idx,ends,q,k,v,o,*dos,lse,*deps)

def pad3(a,b,c):
    z=jnp.zeros((a.shape[0],64),BF)
    return jnp.concatenate([a,z,b,z,c,z],axis=1)

def dmix_kernel(idx_ref,q0,k0,v0,q1,k1,v1,w_ref,sec_ref,f0,f1,f2,f3,stat_ref,gain_ref,keep_ref,send_ref,mom_ref):
    kb=pl.program_id(1)
    flat=lambda x: x[...].reshape(512,x.shape[-1])
    d=jnp.concatenate([pad3(q0[0],k0[0],v0[0]),pad3(q1[0],k1[0],v1[0])],axis=0)
    st=flat(stat_ref); mean=st[:,0:1]; rstd=st[:,1:2]
    mine=(kb==idx_ref[0]).astype(F32)
    m1=None
    for m,f in enumerate((f0,f1,f2,f3)):
        part=dot_nt(d,w_ref[m])[:,:LW]
        part=part+mine*sec_ref[m].reshape(512,LW)
        both=jnp.concatenate([part[:256],part[256:]],axis=1)
        if m%2: send_ref[m//2]=both.astype(BF)
        else: keep_ref[m//2]=both
        eg=part*gain_ref[m]
        f=f[...].astype(F32)
        xh=(jnp.concatenate([f[:,:LW],f[:,LW:]],axis=0)-mean)*rstd
        a=jnp.sum(eg,axis=1,keepdims=True); b=jnp.sum(eg*xh,axis=1,keepdims=True)
        m1=(a,b) if m1 is None else (m1[0]+a,m1[1]+b)
    lane=lax.broadcasted_iota(jnp.int32,(512,128),1)
    t=jnp.where(lane==0,m1[0],jnp.where(lane==1,m1[1],0.0)).T[0:8,:]
    mom_ref[0,0]=t[:,:256]; mom_ref[1,0]=t[:,256:]

def dmix(idx,heads,w,sec,fs,stat,gain,deps=()):
    pairs=heads[0].shape[0]; R=2*pairs
    blk=pl.BlockSpec((1,256,LW),lambda p,b,i:(p,b,0))
    full=lambda a: pl.BlockSpec(a.shape,lambda p,b,i:(0,)*a.ndim)
    pack=pl.BlockSpec((2,256,PW),lambda p,b,i:(0,4*p+b,0))
    return pl.pallas_call(skip(dmix_kernel,15,len(deps)),
        grid_spec=pltpu.PrefetchScalarGridSpec(num_scalar_prefetch=1,grid=(pairs,4),
        in_specs=[blk]*6+[full(w),pl.BlockSpec((4,2,256,LW),lambda p,b,i:(0,p,0,0))]+[pl.BlockSpec((256,PW),lambda p,b,i:(4*p+b,0))]*4
            +[pl.BlockSpec((2,256,128),lambda p,b,i:(p,b,0)),full(gain)]+[ANY]*len(deps),
        out_specs=[pack,pack,pl.BlockSpec((2,1,8,256),lambda p,b,i:(p,b,0,0))]),
        out_shape=[jax.ShapeDtypeStruct((2,pairs*1024,PW),F32),jax.ShapeDtypeStruct((2,pairs*1024,PW),BF),jax.ShapeDtypeStruct((R,4,8,256),F32)],
        cost_estimate=cost(0.1),
        compiler_params=pltpu.CompilerParams(vmem_limit_bytes=VM))(idx,*heads,w,sec,*fs,stat,gain,*deps)

def qkvw_kernel(q0,k0,v0,q1,k1,v1,ml_ref,out_ref,bias_ref,acc):
    i=pl.program_id(0)*2+pl.program_id(1)
    @pl.when(i==0)
    def _(): acc[...]=jnp.zeros_like(acc); bias_ref[...]=jnp.zeros_like(bias_ref)
    d=jnp.concatenate([pad3(q0[0],k0[0],v0[0]),pad3(q1[0],k1[0],v1[0])],axis=0)
    dt=d.T
    bias_ref[...]+=jnp.broadcast_to(jnp.sum(d.astype(F32),axis=0,keepdims=True),bias_ref.shape)
    pad=jnp.zeros((d.shape[0],64),BF)
    for m in range(4):
        acc[m]+=dot(dt,jnp.concatenate([ml_ref[m].reshape(d.shape[0],LW),pad],axis=1))
    @pl.when(i==2*pl.num_programs(0)-1)
    def _():
        for t in range(3):
            out_ref[t]=jnp.concatenate([acc[m,256*t:256*t+192,:LW] for m in range(4)],axis=1).astype(BF)

def qkvw(heads,ml,deps=()):
    pairs=heads[0].shape[0]
    row=pl.BlockSpec((1,512,LW),lambda p,i:(p,i,0))
    return pl.pallas_call(skip(qkvw_kernel,7,len(deps)),grid=(pairs,2),
        in_specs=[row]*6+[pl.BlockSpec((4,2,512,LW),lambda p,i:(0,p,i,0))]+[ANY]*len(deps),
        out_specs=[pl.BlockSpec((3,LW,768),lambda p,i:(0,0,0)),pl.BlockSpec((8,768),lambda p,i:(0,0))],
        out_shape=[jax.ShapeDtypeStruct((3,LW,768),BF),jax.ShapeDtypeStruct((8,768),F32)],
        scratch_shapes=[pltpu.VMEM((4,768,256),F32)],
        cost_estimate=cost(8),
        compiler_params=pltpu.CompilerParams(vmem_limit_bytes=VM))(*heads,ml,*deps)


def row_sum(x):
    return jnp.sum(x, axis=0, keepdims=True)


def norm_parts(x):
    c = x - jnp.mean(x, axis=1, keepdims=True)
    rstd = lax.rsqrt(jnp.mean(c * c, axis=1, keepdims=True) + 1e-5)
    return c * rstd, rstd


def norm_back(e, xhat, rstd, gain):
    eg = e * gain
    return rstd * (eg - jnp.mean(eg, axis=1, keepdims=True) - xhat * jnp.mean(eg * xhat, axis=1, keepdims=True))


def in_order(blocks, index):
    low = (index & 1) != 0
    high = (index & 2) != 0
    b = [jnp.where(low, blocks[m ^ 1], blocks[m]) for m in range(4)]
    return jnp.concatenate([jnp.where(high, b[m ^ 2], b[m]) for m in range(4)], axis=1)


def half(r):
    return slice(LW * (r % 2), LW * (r % 2) + LW)


def ff_kernel(
    idx_ref, f0, f1, f2, f3, a0, a1, a2, a3, og_ref, pw_ref, iw_ref, ow_ref, ib_ref, vec_ref,
    out_ref, act_ref, din_ref, ml_ref, do_ref, dp_ref, att_ref, datt_ref, sec_ref, sums_ref, ibg_ref,
    mid, xh2, rs2, acc, slopes,
):
    i = pl.program_id(0)
    index = idx_ref[0]
    R = 2 * f0.shape[0]
    M = R * 256
    pos_gain, pos_shift, proj_bias, gain2, shift2, outer_bias, gain3, shift3 = [vec_ref[j : j + 1, :] for j in range(8)]

    @pl.when(i == 0)
    def _():
        for r in range(R):
            rows = pl.ds(256 * r, 256)
            xhat, _ = norm_parts(in_order([f[r // 2, 0].astype(F32)[:, half(r)] for f in (f0, f1, f2, f3)], index))
            att_ref[rows] = in_order([a[pl.ds(256 * (r // 2), 256)].astype(F32)[:, half(r)] for a in (a0, a1, a2, a3)], index).astype(BF)
            second = xhat * pos_gain + pos_shift + dot(att_ref[rows], pw_ref[...]) + proj_bias
            xhat, rstd = norm_parts(second)
            xh2[rows] = xhat
            rs2[rows] = jnp.broadcast_to(rstd, (256, 128))
            middle = xhat * gain2 + shift2
            mid[rows] = middle
            ml_ref[rows] = middle.astype(BF)
        acc[...] = jnp.zeros_like(acc)

    @pl.when(i < 4)
    def _():
        for r in range(R):
            rows = pl.ds(256 * r, 256)
            inner = dot(ml_ref[rows], iw_ref[...]) + ib_ref[0]
            phi = erf_gelu_parts(inner)
            slopes[i, rows] = (phi + inner * (jnp.exp(-0.5 * inner * inner) * 0.3989422804014327)).astype(BF)
            act_ref[rows] = (inner * phi).astype(BF)
            acc[rows] += dot(act_ref[rows], ow_ref[...])

    @pl.when(i == 3)
    def _():
        g1 = g2 = g3 = jnp.zeros((1, 768), F32)
        for r in range(R):
            rows = pl.ds(256 * r, 256)
            xhat, rstd = norm_parts(mid[rows] + acc[rows] + outer_bias)
            out_ref[rows] = (xhat * gain3 + shift3).astype(BF)
            e = og_ref[rows].astype(F32)
            d = norm_back(e, xhat, rstd, gain3)
            low = d.astype(BF)
            do_ref[rows] = low
            mid[rows] = d
            g1, g2, g3 = g1 + row_sum(e * xhat), g2 + row_sum(e), g3 + row_sum(low.astype(F32))
        sums_ref[0:1] = g1
        sums_ref[1:2] = g2
        sums_ref[2:3] = g3
        sums_ref[3:8] = jnp.zeros((5, 768), F32)

    @pl.when(i >= 4)
    def _():
        g = jnp.zeros((1, 768), F32)
        for r in range(R):
            rows = pl.ds(256 * r, 256)
            d = dot_nt(do_ref[rows], ow_ref[...]) * slopes[7 - i, rows].astype(F32)
            low = d.astype(BF)
            din_ref[rows] = low
            g = g + row_sum(low.astype(F32))
            mid[rows] += dot_nt(low, iw_ref[...])
        ibg_ref[0] = g

    @pl.when(i == 7)
    def _():
        g1 = g2 = g3 = jnp.zeros((1, 768), F32)
        for r in range(R):
            rows = pl.ds(256 * r, 256)
            e = mid[rows]
            xhat = xh2[rows]
            d = norm_back(e, xhat, rs2[rows, 0:1], gain2)
            low = d.astype(BF)
            dp_ref[rows] = low
            datt = dot_nt(low, pw_ref[...]).astype(BF)
            for b in range(4):
                datt_ref[index ^ b, pl.ds(256 * (r // 2), 256), half(r)] = datt[:, LW * b : LW * b + LW]
                sec_ref[index ^ b, r] = d[:, LW * b : LW * b + LW]
            g1, g2, g3 = g1 + row_sum(e * xhat), g2 + row_sum(e), g3 + row_sum(low.astype(F32))
        sums_ref[3:4] = g1
        sums_ref[4:5] = g2
        sums_ref[5:6] = g3


def ff(idx, firsts, atts, out_grad, pw, iw, ow, ib, vec):
    pairs = atts[0].shape[0] // 256
    R = 2 * pairs
    M = R * 256
    chunk = lambda i: jnp.where(i < 4, i, 7 - i)
    whole = lambda *s: pl.BlockSpec(s, lambda i, x: (0,) * len(s))
    return pl.pallas_call(
        ff_kernel,
        grid_spec=pltpu.PrefetchScalarGridSpec(
            num_scalar_prefetch=1,
            grid=(8,),
            in_specs=[pl.BlockSpec((pairs, 1, 256, PW), lambda i, x: (0, x[0], 0, 0))] * 4
            + [whole(pairs * 256, PW)] * 4
            + [
                whole(M, 768),
                whole(768, 768),
                pl.BlockSpec((768, 768), lambda i, x: (0, chunk(i))),
                pl.BlockSpec((768, 768), lambda i, x: (chunk(i), 0)),
                pl.BlockSpec((1, 1, 768), lambda i, x: (chunk(i), 0, 0)),
                whole(8, 768),
            ],
            out_specs=[
                whole(M, 768),
                pl.BlockSpec((M, 768), lambda i, x: (0, jnp.minimum(i, 3))),
                pl.BlockSpec((M, 768), lambda i, x: (0, jnp.minimum(7 - i, 3))),
            ]
            + [whole(M, 768)] * 4
            + [
                whole(4, pairs * 256, PW),
                whole(4, R, 256, LW),
                whole(8, 768),
                pl.BlockSpec((1, 1, 768), lambda i, x: (jnp.minimum(7 - i, 3), 0, 0)),
            ],
            scratch_shapes=[
                pltpu.VMEM((M, 768), F32),
                pltpu.VMEM((M, 768), F32),
                pltpu.VMEM((M, 128), F32),
                pltpu.VMEM((M, 768), F32),
                pltpu.VMEM((4, M, 768), BF),
            ],
        ),
        out_shape=[
            jax.ShapeDtypeStruct((M, 768), BF),
            jax.ShapeDtypeStruct((M, 3072), BF),
            jax.ShapeDtypeStruct((M, 3072), BF),
        ]
        + [jax.ShapeDtypeStruct((M, 768), BF)] * 4
        + [
            jax.ShapeDtypeStruct((4, pairs * 256, PW), BF),
            jax.ShapeDtypeStruct((4, R, 256, LW), F32),
            jax.ShapeDtypeStruct((8, 768), F32),
            jax.ShapeDtypeStruct((4, 1, 768), F32),
        ],
        cost_estimate=cost(40),
        compiler_params=pltpu.CompilerParams(vmem_limit_bytes=VM),
    )(idx, *[f.reshape(pairs, 4, 256, PW) for f in firsts], *atts, out_grad, pw, iw, ow, ib, vec)


def put(index, keep, send, b, rows, value):
    m = index ^ b

    @pl.when((m & 1) == 0)
    def _():
        keep[m >> 1, rows] = value

    @pl.when((m & 1) == 1)
    def _():
        send[m >> 1, rows] = value


def outer_kernel(idx_ref, act_ref, do_ref, sums_ref, ibg_ref, dp_ref, att_ref, keep_ref, send_ref):
    c = pl.program_id(0)
    index = idx_ref[0]
    outer = dot_tn(do_ref[...], act_ref[...]).astype(BF)
    for b in range(4):
        put(index, keep_ref, send_ref, b, pl.ds(pl.multiple_of(LW * c, LW), LW), outer[LW * b : LW * b + LW])

    @pl.when(c == 0)
    def _():
        proj = dot_tn(dp_ref[...], att_ref[...]).astype(BF)
        for b in range(4):
            put(index, keep_ref, send_ref, b, pl.ds(768, LW), proj[LW * b : LW * b + LW])
            small = jnp.concatenate([sums_ref[:, LW * b : LW * b + LW], jnp.zeros((8, 576), F32)], axis=1)
            small = jnp.concatenate([small, ibg_ref[b], jnp.zeros((7, 768), F32)], axis=0)
            put(index, keep_ref, send_ref, b, pl.ds(960, 16), small.astype(BF))
            put(index, keep_ref, send_ref, b, pl.ds(976, 48), jnp.zeros((48, 768), BF))


def inner_kernel(idx_ref, din_ref, ml_ref, keep_ref, send_ref):
    put(idx_ref[0], keep_ref, send_ref, pl.program_id(0), pl.ds(0, 768), dot_tn(ml_ref[...], din_ref[...]).astype(BF))


def weight_grads(kernel, rows, idx, wide, others, deps=()):
    M = wide.shape[0]
    whole = lambda a: pl.BlockSpec(a.shape, lambda i, x: (0,) * a.ndim)
    out = pl.BlockSpec((2, rows, 768), lambda i, x: (0, 0, 0))
    return pl.pallas_call(
        skip(kernel, 2 + len(others), len(deps)),
        grid_spec=pltpu.PrefetchScalarGridSpec(
            num_scalar_prefetch=1,
            grid=(4,),
            in_specs=[pl.BlockSpec((M, 768), lambda i, x: (0, i))] + [whole(a) for a in others] + [ANY] * len(deps),
            out_specs=[out, out],
        ),
        out_shape=[jax.ShapeDtypeStruct((2, rows, 768), BF)] * 2,
        cost_estimate=cost(8),
        compiler_params=pltpu.CompilerParams(vmem_limit_bytes=VM),
    )(idx, wide, *others, *deps)


def far_kernel(keep_ref, got_ref, out_ref):
    out_ref[...] = (keep_ref[0].astype(F32) + got_ref[0].astype(F32)).astype(BF)


def far_sum(keep, got, deps=()):
    n = keep.shape[1]
    block = pl.BlockSpec((1, n // 2, 768), lambda i: (1, i, 0))
    return pl.pallas_call(
        skip(far_kernel, 2, len(deps)),
        grid=(2,),
        in_specs=[block] * 2 + [ANY] * len(deps),
        out_specs=pl.BlockSpec((n // 2, 768), lambda i: (i, 0)),
        out_shape=jax.ShapeDtypeStruct((n, 768), BF),
        cost_estimate=cost(1),
        compiler_params=pltpu.CompilerParams(vmem_limit_bytes=VM),
    )(keep, got, *deps)


def own_kernel(keep_ref, got_ref, far_ref, out_ref):
    x = keep_ref[0].astype(F32) + got_ref[0].astype(F32) + far_ref[...].astype(F32)
    out_ref[...] = x.astype(BF).reshape(out_ref.shape)


def own_sum(keep, got, far, deps=()):
    n = keep.shape[1]
    block = pl.BlockSpec((1, n // 2, 768), lambda i: (0, i, 0))
    one = pl.BlockSpec((n // 2, 768), lambda i: (i, 0))
    return pl.pallas_call(
        skip(own_kernel, 3, len(deps)),
        grid=(2,),
        in_specs=[block] * 2 + [one] + [ANY] * len(deps),
        out_specs=one,
        out_shape=jax.ShapeDtypeStruct((n, 768), BF),
        cost_estimate=cost(1),
        compiler_params=pltpu.CompilerParams(vmem_limit_bytes=VM),
    )(keep, got, far, *deps)


def finish_kernel(in_ref, proj_ref, outer_ref, small_ref):
    proj_ref[...] = in_ref[768:960].astype(F32)
    for i in range(4):
        outer_ref[:, 768 * i : 768 * i + 768] = in_ref[LW * i : LW * i + LW].astype(F32)
    small_ref[...] = in_ref[960:976].astype(F32)


def finish(grads, deps=()):
    whole = lambda *s: pl.BlockSpec(s, lambda: (0, 0))
    shapes = (LW, 768), (LW, 3072), (16, 768)
    return pl.pallas_call(
        skip(finish_kernel, 1, len(deps)),
        in_specs=[whole(1024, 768)] + [ANY] * len(deps),
        out_specs=[whole(*s) for s in shapes],
        out_shape=[jax.ShapeDtypeStruct(s, F32) for s in shapes],
        cost_estimate=cost(6),
        compiler_params=pltpu.CompilerParams(vmem_limit_bytes=VM),
    )(grads, *deps)


def widen_kernel(in_ref, out_ref):
    out_ref[...] = in_ref[...].astype(F32)


def widen(x, deps=()):
    block = pl.BlockSpec((x.shape[0] // 2, x.shape[1]), lambda i: (i, 0))
    return pl.pallas_call(
        skip(widen_kernel, 1, len(deps)),
        grid=(2,),
        in_specs=[block] + [ANY] * len(deps),
        out_specs=block,
        out_shape=jax.ShapeDtypeStruct(x.shape, F32),
        cost_estimate=cost(3),
        compiler_params=pltpu.CompilerParams(vmem_limit_bytes=VM),
    )(x, *deps)


def taps_kernel(own_ref, scale_ref, dir_ref, out_ref, square_ref, tmp):
    n = dir_ref.shape[0]
    at = pl.program_id(0) * n
    side = own_ref[0] // 2
    for k in range(n):
        x = dir_ref[k].astype(F32)
        total = jnp.sum(jnp.sum(x * x, axis=0, keepdims=True), axis=1, keepdims=True)
        square_ref[k : k + 1] = jnp.broadcast_to(total, (1, 128))
        x = jnp.where(side != 0, x[:, PW:], x[:, :PW])
        tmp[48 * k : 48 * k + 48] = (x * (scale_ref[at + k] * lax.rsqrt(total))).astype(BF)
    out_ref[...] = dot(tmp[...], own_pick(own_ref[0]))[:, :LW].astype(BF)


def own_pick(index):
    row = lax.broadcasted_iota(jnp.int32, (PW, 256), 0)
    lane = lax.broadcasted_iota(jnp.int32, (PW, 256), 1)
    return ((row == lane + LW * (index & 1)) & (lane < LW)).astype(F32).astype(BF)


def own_taps(idx, scale, tap_dir):
    return pl.pallas_call(
        taps_kernel,
        grid_spec=pltpu.PrefetchScalarGridSpec(
            num_scalar_prefetch=2,
            grid=(8,),
            in_specs=[pl.BlockSpec((16, 48, 768), lambda i, x, c: (i, 0, 0))],
            out_specs=[pl.BlockSpec((768, LW), lambda i, x, c: (i, 0)), pl.BlockSpec((16, 128), lambda i, x, c: (i, 0))],
            scratch_shapes=[pltpu.VMEM((768, PW), BF)],
        ),
        out_shape=[jax.ShapeDtypeStruct((6144, LW), BF), jax.ShapeDtypeStruct((128, 128), F32)],
        cost_estimate=cost(10),
        compiler_params=pltpu.CompilerParams(vmem_limit_bytes=VM),
    )(idx, scale, tap_dir)


def raw_kernel(own_ref, dir_ref, out_ref):
    out_ref[...] = dot(dir_ref[...], own_pick(own_ref[0]))[:, :LW].astype(BF)


def own_dirs(idx, tap_dir, deps=()):
    return pl.pallas_call(
        skip(raw_kernel, 2, len(deps)),
        grid_spec=pltpu.PrefetchScalarGridSpec(
            num_scalar_prefetch=1,
            grid=(4,),
            in_specs=[pl.BlockSpec((1536, PW), lambda i, x: (i, x[0] // 2))] + [ANY] * len(deps),
            out_specs=pl.BlockSpec((1536, LW), lambda i, x: (i, 0)),
        ),
        out_shape=jax.ShapeDtypeStruct((6144, LW), BF),
        cost_estimate=cost(5),
        compiler_params=pltpu.CompilerParams(vmem_limit_bytes=VM),
    )(idx, tap_dir.reshape(6144, 768), *deps)


def dots_kernel(tap_ref, dir_ref, out_ref):
    g = tap_ref[0].astype(F32).T
    p = g * dir_ref[...].astype(F32)
    rows = [jnp.sum(p[48 * t : 48 * t + 48], axis=0, keepdims=True) for t in range(16)]
    s = jnp.sum(jnp.concatenate(rows, axis=0), axis=1, keepdims=True)
    out_ref[0] = jnp.broadcast_to(s, (16, 128))


def tap_dots(tap, dirs, deps=()):
    return pl.pallas_call(
        skip(dots_kernel, 2, len(deps)),
        grid=(8,),
        in_specs=[pl.BlockSpec((1, LW, 768), lambda i: (i, 0, 0)), pl.BlockSpec((768, LW), lambda i: (i, 0))] + [ANY] * len(deps),
        out_specs=pl.BlockSpec((1, 16, 128), lambda i: (i, 0, 0)),
        out_shape=jax.ShapeDtypeStruct((8, 16, 128), F32),
        cost_estimate=cost(6),
        compiler_params=pltpu.CompilerParams(vmem_limit_bytes=VM),
    )(tap, dirs, *deps)


def last_kernel(left_ref, right_ref, dir_ref, coef_ref, beta_ref, out_ref, turned):
    i = pl.program_id(0)

    @pl.when(i == 0)
    def _():
        for J in range(8):
            for p, ref in enumerate((left_ref, right_ref)):
                t = ref[J].astype(F32).T
                at = 768 * J + 384 * p
                turned[0, at : at + 384] = t[:, :128]
                turned[1, at : at + 384, :64] = t[:, 128:]

    for c in range(8):
        at = pl.ds(8 * i + c, 128, stride=48)
        g = jnp.concatenate([turned[0, at].T, turned[1, at].T[:64]], axis=0)
        out_ref[c] = g * coef_ref[...] - dir_ref[c].astype(F32) * beta_ref[...]


def last_taps(coef, beta, left, right, dirs, deps=()):
    row = pl.BlockSpec((1, 128), lambda i: (0, 0))
    block = pl.BlockSpec((8, LW, 128), lambda i: (i, 0, 0))
    return pl.pallas_call(
        skip(last_kernel, 5, len(deps)),
        grid=(6,),
        in_specs=[pl.BlockSpec((8, LW, 384), lambda i: (0, 0, 0))] * 2 + [block, row, row] + [ANY] * len(deps),
        out_specs=block,
        out_shape=jax.ShapeDtypeStruct((48, LW, 128), F32),
        scratch_shapes=[pltpu.VMEM((2, 6144, 128), F32)],
        cost_estimate=cost(8),
        compiler_params=pltpu.CompilerParams(vmem_limit_bytes=VM),
    )(left, right, dirs, coef[None], beta[None], *deps)


def near_kernel(keep_ref, got_ref, mom_ref, mom_got, near_ref, far_ref, mom_out):
    N = keep_ref.shape[1]
    near_ref[...] = keep_ref[0] + got_ref[0].astype(F32)
    far_ref[:N] = (keep_ref[1] + got_ref[1].astype(F32)).astype(BF)
    mom = mom_ref[...] + mom_got[...]
    mom_out[...] = mom
    R = mom.shape[0]
    rows = jnp.concatenate([mom[r, k, 0:2] for r in range(R) for k in range(4)], axis=0)
    far_ref[N:] = jnp.concatenate([rows, jnp.zeros((8 * R, 128), F32)], axis=1).astype(BF)


def near_far(keep, got, moments, moments_got):
    N = keep.shape[1]
    R = moments.shape[0]
    whole = lambda a: pl.BlockSpec(a.shape, lambda: (0,) * a.ndim)
    shapes = [
        jax.ShapeDtypeStruct((N, PW), F32),
        jax.ShapeDtypeStruct((N + 8 * R, PW), BF),
        jax.ShapeDtypeStruct(moments.shape, F32),
    ]
    return pl.pallas_call(
        near_kernel,
        in_specs=[whole(a) for a in (keep, got, moments, moments_got)],
        out_specs=[whole(a) for a in shapes],
        out_shape=shapes,
        cost_estimate=cost(2),
        compiler_params=pltpu.CompilerParams(vmem_limit_bytes=VM),
    )(keep, got, moments, moments_got)


HALF = 384


def pick_kernel(bits_ref, a_ref, b_ref, sa_ref, sb_ref):
    sa_ref[...] = a_ref[...]
    sb_ref[...] = b_ref[...]


def first_sends(bits, x, deps=()):
    L, N, _ = x.shape
    n = N // 4
    out = pl.BlockSpec((L, n, HALF), lambda i, s: (0, i, 0))
    return pl.pallas_call(
        skip(pick_kernel, 3, len(deps)),
        grid_spec=pltpu.PrefetchScalarGridSpec(
            num_scalar_prefetch=1,
            grid=(2,),
            in_specs=[
                pl.BlockSpec((L, n, HALF), lambda i, s: (0, 2 - 2 * s[0] + i, 0)),
                pl.BlockSpec((L, n, HALF), lambda i, s: (0, 2 - 2 * s[1] + i, 1)),
            ]
            + [ANY] * len(deps),
            out_specs=[out, out],
        ),
        out_shape=[jax.ShapeDtypeStruct((L, N // 2, HALF), BF)] * 2,
        cost_estimate=cost(3),
        compiler_params=pltpu.CompilerParams(vmem_limit_bytes=VM),
    )(bits, x, x, *deps)


def stage_kernel(last, steps, bits_ref, ka, kb, ra, rb, *outs):
    i = pl.program_id(0)
    for p, (k, r) in enumerate(((ka, ra), (kb, rb))):
        y = k[...].reshape(r.shape).astype(F32) + r[...].astype(F32)
        if last:
            outs[p][...] = y.astype(BF)
            continue
        sum_ref, send_ref = outs[p], outs[2 + p]
        h = y.shape[1] * steps // 2
        halves = ((i, y),) if steps == 2 else ((0, y[:, :h]), (1, y[:, h:]))
        for at, half in halves:
            sum_ref[:, 0 if steps == 2 else at] = half.astype(BF)

            @pl.when(bits_ref[2 + p] != at)
            def _():
                send_ref[...] = half.astype(BF)


def stage(bits, a, b, ra, rb, last, deps=()):
    L, n, _ = ra.shape
    h = n // 2
    steps = 2 if not last and h % 16 == 0 else 1
    m = n // steps
    if a.ndim == 3:
        keep = lambda p: pl.BlockSpec((L, m, HALF), lambda i, s: (0, steps * s[p] + i, p))
    else:
        keep = lambda p: pl.BlockSpec((L, 1, m, HALF), lambda i, s: (0, s[p], i, 0))
    row = pl.BlockSpec((L, m, HALF), lambda i, s: (0, i, 0))
    if last:
        out_specs, out_shape = [row] * 2, [jax.ShapeDtypeStruct((L, n, HALF), BF)] * 2
    else:
        out_specs = [pl.BlockSpec((L, 2 // steps, h, HALF), lambda i, s: (0, i, 0, 0))] * 2
        out_specs += [pl.BlockSpec((L, h, HALF), lambda i, s: (0, 0, 0))] * 2
        out_shape = [jax.ShapeDtypeStruct((L, 2, h, HALF), BF)] * 2 + [jax.ShapeDtypeStruct((L, h, HALF), BF)] * 2
    return pl.pallas_call(
        skip(lambda *refs: stage_kernel(last, steps, *refs), 5, len(deps)),
        grid_spec=pltpu.PrefetchScalarGridSpec(
            num_scalar_prefetch=1,
            grid=(steps,),
            in_specs=[keep(0), keep(1), row, row] + [ANY] * len(deps),
            out_specs=out_specs,
        ),
        out_shape=out_shape,
        cost_estimate=cost(3),
        compiler_params=pltpu.CompilerParams(vmem_limit_bytes=VM),
    )(bits, a, b, ra, rb, *deps)


def join_kernel(bits_ref, a, b, ra, rb, oa, ob):
    for p, (k, r, o) in enumerate(((a, ra, oa), (b, rb, ob))):
        on = bits_ref[p]
        o[on] = k[...]
        o[1 - on] = r[...]


def join(bits, a, b, ra, rb, deps=()):
    shape = a.shape
    block = pl.BlockSpec(shape, lambda i, s: (0,) * len(shape))
    out = pl.BlockSpec((2,) + shape, lambda i, s: (0,) * (len(shape) + 1))
    oa, ob = pl.pallas_call(
        skip(join_kernel, 5, len(deps)),
        grid_spec=pltpu.PrefetchScalarGridSpec(
            num_scalar_prefetch=1,
            grid=(1,),
            in_specs=[block] * 4 + [ANY] * len(deps),
            out_specs=[out] * 2,
        ),
        out_shape=[jax.ShapeDtypeStruct((2,) + shape, BF)] * 2,
        cost_estimate=cost(2),
        compiler_params=pltpu.CompilerParams(vmem_limit_bytes=VM),
    )(bits, a, b, ra, rb, *deps)
    flat = (2 * shape[0],) + shape[1:]
    return oa.reshape(flat), ob.reshape(flat)


class RowSum:
    def __init__(self, x, deps=()):
        n = lax.axis_size("rows")
        bits = [1 << i for i in range(n.bit_length() - 1)]
        self.orders = (bits, bits[1::-1] + bits[2:])
        self.count = x.shape[1]
        full = -(-self.count // (16 * n)) * (16 * n) if n > 8 else self.count
        if full != self.count:
            x = jnp.pad(x, ((0, 0), (0, full - self.count), (0, 0)))
        self.parts = [x, x]
        self.at = 0
        self.got = None
        self.steps = len(bits)
        self.sends = first_sends(self.bits(0), x, deps)

    def bits(self, s):
        place = lax.axis_index("rows")
        pick = lambda o, i: (place // o[min(i, self.steps - 1)]) % 2
        return jnp.stack([pick(o, i) for i in (s, s + 1) for o in self.orders]).astype(jnp.int32)

    def go(self):
        self.got = [swap(s, "rows", o[self.at]) for s, o in zip(self.sends, self.orders)]

    def step(self, *deps):
        if self.got is None:
            self.go()
        got, self.got = self.got, None
        last = self.at == self.steps - 1
        outs = stage(self.bits(self.at), *self.parts, *got, last, deps)
        self.parts, self.sends = outs[:2], outs[2:]
        self.at += 1
        return self.parts[0]

    def back(self, *deps):
        self.at -= 1
        got = [swap(p, "rows", o[self.at]) for p, o in zip(self.parts, self.orders)]
        self.parts = join(self.bits(self.at), *self.parts, *got, deps)
        return self.parts[0]

    def result(self):
        return [p.reshape(-1, HALF)[: self.count] for p in self.parts]


def swap(x, axis, bit):
    return lax.ppermute(x, axis, [(i, i ^ bit) for i in range(lax.axis_size(axis))])


def gather_seq(x):
    far = swap(x, "seq", 2)
    near = swap(x, "seq", 1)
    return [x, near, far, swap(far, "seq", 1)]


def trade(blocks):
    return [blocks[0], swap(blocks[1], "seq", 1), swap(blocks[2], "seq", 2), swap(blocks[3], "seq", 3)]


def all_sum(x, axis):
    for i in range(lax.axis_size(axis).bit_length() - 1):
        x = x + swap(x, axis, 1 << i)
    return x


def assemble(blocks, index):
    low = (index & 1) != 0
    high = (index & 2) != 0
    b = [jnp.where(low, blocks[m ^ 1], blocks[m]) for m in range(4)]
    return [jnp.where(high, b[m ^ 2], b[m]) for m in range(4)]


def cut(x, start, size, axis):
    return lax.dynamic_slice_in_dim(x, start, size, axis)


def local(
    frames,
    utterance_lengths,
    tap_dir,
    tap_scale,
    conv_bias,
    pos_gain,
    pos_shift,
    query_weight,
    query_bias,
    key_weight,
    value_weight,
    value_bias,
    proj_weight,
    proj_bias,
    attend_gain,
    attend_shift,
    inner_weight,
    inner_bias,
    outer_weight,
    outer_bias,
    final_gain,
    final_shift,
    out_grad,
):
    R = frames.shape[0]
    index = lax.axis_index("seq")
    idx = jnp.full((1,), index, jnp.int32)
    ends = jnp.cumsum(utterance_lengths, axis=1, dtype=jnp.int32)
    order = [index ^ m for m in range(4)]
    own = index * LW

    def packed(x):
        return jnp.concatenate([x[0::2], x[1::2]], axis=2).reshape(R * 128, PW)

    sent = trade([packed(cut(frames, b * LW, LW, 2)) for b in order])
    taps, squares = own_taps(idx, tap_scale, tap_dir)
    w = build_w(taps)
    bias4 = jnp.tile(cut(conv_bias, own, LW, 0).reshape(4, 1, 48), (1, 4, 1)).reshape(4, 1, LW)
    first, pre, xs = conv_fwd(ends, idx, sent, w, bias4)
    firsts = gather_seq(first)

    def xor_rows(a):
        return jnp.stack([cut(a, b * LW, LW, 0) for b in order])

    def pad_to(a, axis, size):
        widths = [(0, 0)] * a.ndim
        widths[axis] = (0, size - a.shape[axis])
        return jnp.pad(a, widths)

    own_cols = [
        pad_to(cut(a, own, LW, 1), 1, 256)
        for a in (query_weight * jnp.asarray(0.125, BF), key_weight, value_weight)
    ]
    w_qkv = pad_to(xor_rows(jnp.concatenate(own_cols, axis=1)), 1, 256)
    b_qkv = jnp.concatenate(
        [
            pad_to(cut(query_bias, own, LW, 0) * 0.125, 0, 512),
            pad_to(cut(value_bias, own, LW, 0), 0, 256),
        ]
    )[None]
    gain_x = xor_rows(pos_gain)[:, None]
    shift_x = xor_rows(pos_shift)[:, None]
    q, k, v, mixed_low, stat = qkv(firsts, w_qkv, b_qkv, gain_x, shift_x)
    att, att_full, lse = attn(idx, ends, q, k, v)
    att_blocks = trade([att[m] for m in range(4)])

    vecs = jnp.stack([pos_gain, pos_shift, proj_bias, attend_gain, attend_shift, outer_bias, final_gain, final_shift])
    layer_out, act, d_inner, middle_low, d_outer, d_proj, attended, d_att, second_x, sums, inner_sums = ff(
        idx, firsts, att_blocks, out_grad.reshape(R * 256, 768), proj_weight, inner_weight, outer_weight,
        inner_bias.reshape(4, 1, 768), vecs,
    )
    dos = trade_out(d_att)
    keep_out, send_out = weight_grads(outer_kernel, 1024, idx, act, (d_outer, sums, inner_sums, d_proj, attended))
    got_out = swap(send_out, "seq", 1)
    keep_in, send_in = weight_grads(inner_kernel, 768, idx, d_inner, (middle_low,), (send_out,))
    far = far_sum(keep_out, got_out, (send_in,))
    got_in = swap(send_in, "seq", 1)

    heads = attn_bwd(0, idx, ends, q, k, v, att_full, dos, lse, (far,))
    heads += attn_bwd(1, idx, ends, q, k, v, att_full, dos, lse, (heads[0],))
    grads = own_sum(keep_out, got_out, swap(far, "seq", 2), (heads[3],))
    keep, send, moments = dmix(idx, heads, w_qkv, second_x, firsts, stat, gain_x, (grads,))
    grads_out = lax.psum(grads, "rows")
    e_near, e_far, moments = near_far(keep, swap(send, "seq", 1), moments, swap(moments, "seq", 1))
    g_qkv, b_grads = qkvw(heads, mixed_low, (e_far,))
    e_sent = e_far
    e_far = swap(e_far, "seq", 2)
    far = swap(far_sum(keep_in, got_in, (e_sent, g_qkv)), "seq", 2)
    dir_own = own_dirs(idx, tap_dir, (e_sent, g_qkv))
    dir_turned = jnp.transpose(dir_own.reshape(128, 48, LW), (1, 2, 0))
    moments = moments.reshape(R * 4, 8, 256)

    tap_part, ds, d4, conv_b, vec = tap_grads(
        ends, e_near, e_far, first, stat.reshape(R * 1024, 128), moments, cut(pos_gain, own, LW, 0)[None], pre, xs, g_qkv, (dir_own,),
    )
    if R > 2:
        tap_part = jnp.sum(tap_part.astype(F32), axis=0, keepdims=True).astype(BF)
    tap_part = tap_part[0]
    tap_sum = RowSum(tap_part.reshape(1, 11 * LW, 768))
    part = conv_back(0, ends, idx, ds, d4, w, None, tuple(tap_sum.sends))
    tap_sum.step(part)
    grads_in = lax.psum(own_sum(keep_in, got_in, far, (part, grads_out)), "rows")
    back = conv_back(2, ends, idx, ds, d4, w, part, tuple(tap_sum.sends))
    tap_sum.step(back)
    dots = tap_dots(tap_part, dir_own, tuple(tap_sum.sends))
    tap_sum.step(dots)
    dots = all_sum(dots[:, :, 0], "seq")
    back = trade_out(back)
    back = jnp.concatenate([b.reshape(R // 2, 1, 256, PW) for b in assemble(back, index)], axis=1)
    back = back.reshape(R // 2, 4, 256, 2, LW)
    frames_grad = jnp.transpose(back, (0, 3, 2, 1, 4)).reshape(R, 256, 768)
    while tap_sum.at:
        tap_sum.back()
    tap_left, tap_right = [p.reshape(11, LW, HALF) for p in tap_sum.result()]
    qkv_std = assemble([x[8:11, :, LW * m : LW * m + LW] for x in (tap_left, tap_right) for m in range(2)], index)
    t_qkv = jnp.concatenate(qkv_std, axis=2).astype(F32)
    t_proj, t_outer, small = finish(grads_out, (tap_sum.parts[0],))
    lates = jnp.concatenate(
        [
            jnp.sum(conv_b, axis=(0, 2)).reshape(4, 4, 48).sum(1).reshape(LW),
            jnp.sum(vec[:, 0], axis=0),
            jnp.sum(vec[:, 1], axis=0),
            b_grads[0, 0:LW] * 0.125,
            b_grads[0, 512 : 512 + LW],
            dots.reshape(128),
            jnp.zeros((2048 - 1088,), F32),
        ]
    )
    lates = all_sum(lates.reshape(16, 128), "rows").reshape(2048)
    dots = lates[5 * LW : 5 * LW + 128]
    inverse = lax.rsqrt(squares[:, 0])
    coef = tap_scale * inverse
    turned = last_taps(coef, coef * dots * inverse * inverse, tap_left, tap_right, dir_turned, (frames_grad, t_outer))
    g_tap_dir = jnp.transpose(turned, (2, 0, 1))
    t_inner = widen(grads_in, (turned,))
    g_tap_scale = cut(dots * inverse, index * 32, 32, 0)

    return (
        layer_out.reshape(R, 256, 768),
        frames_grad,
        g_tap_dir,
        g_tap_scale,
        lates[0:LW],
        lates[LW : 2 * LW],
        lates[2 * LW : 3 * LW],
        t_qkv[0].T * 0.125,
        lates[3 * LW : 4 * LW],
        t_qkv[1].T,
        t_qkv[2].T,
        lates[4 * LW : 5 * LW],
        t_proj.T,
        small[5, :LW],
        small[3, :LW],
        small[4, :LW],
        t_inner,
        small[8],
        t_outer.T,
        small[2, :LW],
        small[0, :LW],
        small[1, :LW],
    )


def trade_out(x):
    return trade([x[m] for m in range(4)])


def solution(mesh):
    split = P("rows", "seq", None)
    col = P(None, "seq")
    one = P("seq")
    return jax.shard_map(
        local,
        mesh=mesh,
        in_specs=(split, P("rows", None)) + (P(),) * 20 + (split,),
        out_specs=(split, split, P(None, None, "seq"), one, one, one, one)
        + (col, one, col, col, one, col, one, one, one, col, one, col, one, one, one),
        check_vma=False,
    )
```

```python
import jax, jax.numpy as jnp
from jax import lax
from jax.sharding import PartitionSpec as P
from jax.experimental import pallas as pl
from jax.experimental.pallas import tpu as pltpu
F32=jnp.float32; BF=jnp.bfloat16
CH=48; PH=4; LW=PH*CH
NJ=33; SEGL=48; XROWS=(SEGL+NJ-1)*16; MROWS=SEGL*16
VM=60*1024*1024

def cost(us):
    return pl.CostEstimate(flops=int(us*1.0e9),bytes_accessed=int(us*3.0e6),transcendentals=0)

ANY=pl.BlockSpec(memory_space=pl.ANY)
PW=2*LW

def skip(kernel,at,count):
    if not count:
        return kernel
    return lambda *refs: kernel(*refs[:at],*refs[at+count:])

def dot(a,b): return jnp.dot(a,b,preferred_element_type=F32)
def dot_nt(a,b): return lax.dot_general(a,b,(((1,),(1,)),((),())),preferred_element_type=F32)
def dot_tn(a,b): return lax.dot_general(a,b,(((0,),(0,)),((),())),preferred_element_type=F32)

def erf_gelu_parts(v):
    phi=0.5*(1.0+lax.erf(v*0.7071067811865476))
    return phi

WROWS=6400
def build_w_kernel(t_ref, w_ref, tp, rs):
    g=pl.program_id(0)
    rows=t_ref.shape[0]
    @pl.when(g==0)
    def _():
        tp[0:144,:]=jnp.zeros((144,LW),BF)
        tp[144:144+rows,:]=t_ref[...]
        tp[144+rows:,:]=jnp.zeros((256,LW),BF)
    src=lax.broadcasted_iota(jnp.int32,(LW,256),0); l=lax.broadcasted_iota(jnp.int32,(LW,256),1)
    pick=((src==48*g+lax.rem(l,48))&(l<LW)).astype(F32).astype(BF)
    n=1600
    lane=lax.broadcasted_iota(jnp.int32,(n,256),1)
    for i in range(WROWS//n):
        r0=i*n
        R=dot(tp[r0:r0+n+144,:],pick).astype(BF)
        lo=jnp.where(lane[:,:128]<96,jnp.where(lane[:,:128]<48,R[144:144+n,:128],R[96:96+n,:128]),R[48:48+n,:128])
        hi=jnp.where(lane[:,128:]<144,R[48:48+n,128:],R[0:n,128:])
        w_ref[0,r0:r0+n,:128]=lo
        w_ref[0,r0:r0+n,128:]=hi

def build_w(taps2):
    rows=taps2.shape[0]
    return pl.pallas_call(build_w_kernel,grid=(4,),
        in_specs=[pl.BlockSpec((rows,LW),lambda g:(0,0))],
        out_specs=pl.BlockSpec((1,WROWS,256),lambda g:(g,0,0)),
        out_shape=jax.ShapeDtypeStruct((4,WROWS,256),BF),
        scratch_shapes=[pltpu.VMEM((rows+144+256,LW),BF),pltpu.VMEM((16,256),BF)],
        cost_estimate=cost(10),
        compiler_params=pltpu.CompilerParams(vmem_limit_bytes=VM))(taps2)

def sload(ref,start,n,stride):
    return jnp.concatenate([ref[0,pl.ds(start,n,stride=stride),:],ref[1,pl.ds(start,n,stride=stride),:]],axis=1)[:,:LW]
def sstore(ref,start,n,stride,v):
    ref[0,pl.ds(start,n,stride=stride),:]=v[:,:128]
    ref[1,pl.ds(start,n,stride=stride),:]=jnp.concatenate([v[:,128:],jnp.zeros((n,64),v.dtype)],axis=1)
def fload(ref,start,n):
    return jnp.concatenate([ref[0,pl.ds(start,n),:],ref[1,pl.ds(start,n),:]],axis=1)[:,:LW]
def fstore(ref,start,n,v):
    ref[0,pl.ds(start,n),:]=v[:,:128]
    ref[1,pl.ds(start,n),:]=jnp.concatenate([v[:,128:],jnp.zeros((n,64),v.dtype)],axis=1)

def pick_matrix(g,a):
    ch=lax.broadcasted_iota(jnp.int32,(LW,256),0); l=lax.broadcasted_iota(jnp.int32,(LW,256),1)
    return ((ch==48*g+(l-48*a))&(l>=48*a)&(l<48*a+48)).astype(F32).astype(BF)

def pick_back(g,a):
    l=lax.broadcasted_iota(jnp.int32,(LW,256),0); ch=lax.broadcasted_iota(jnp.int32,(LW,256),1)
    return ((ch==48*g+(l-48*a))&(l>=48*a)&(l<48*a+48)).astype(F32).astype(BF)

def fill_ids(seg_ref,pair,sid):
    sub=lax.broadcasted_iota(jnp.int32,(256,LW),0); l=lax.broadcasted_iota(jnp.int32,(256,LW),1)
    t=4*sub+(l>=48).astype(jnp.int32)+(l>=96).astype(jnp.int32)+(l>=144).astype(jnp.int32)
    for r in range(2):
        v=jnp.zeros((256,LW),jnp.int32)
        for q in range(7):
            v=v+(t>=seg_ref[pair*2+r,q]).astype(jnp.int32)
        sid[pl.ds(256*r,256),:]=v

TAIL=48
def respace(sid,src,xr,xsf):
    xsf[0,1280:1280+TAIL,:]=jnp.zeros((TAIL,128),F32); xsf[1,1280:1280+TAIL,:]=jnp.zeros((TAIL,128),F32)
    for r in range(2):
        for B in range(26):
            v=jnp.zeros((16,LW),F32)
            for q in range(8):
                bb=B-1-q
                if 0<=bb<16:
                    rows=pl.ds(r*256+16*bb,16)
                    v=jnp.where(sid[rows,:]==q,src[rows,:],v)
            xr[r,pl.ds(16*B,16),:]=v
        for sp in range(8):
            sstore(xsf,r*8+sp,80,16,xr[r,pl.ds(48*sp,80),:])

def unspace(sid,acc,yr,emit):
    for r in range(2):
        for sp in range(8):
            yr[r,pl.ds(48*sp,48),:]=sload(acc,r*8+sp,48,16)
        for bb in range(16):
            v=jnp.zeros((16,LW),F32)
            ids=sid[pl.ds(r*256+16*bb,16),:]
            for q in range(8):
                v=jnp.where(ids==q,yr[r,pl.ds(16*(bb+q),16),:],v)
            emit(r*256+16*bb,v)

def conv_fwd_kernel(seg_ref,idx_ref,x0_ref,x1_ref,x2_ref,x3_ref,w_ref,bias_ref,first_ref,pre_ref,xs_ref,xt,xa,x4,xr,xsf,acc,yr,facc,sid):
    pair=pl.program_id(0); g=pl.program_id(1)
    @pl.when(g==0)
    def _():
        fill_ids(seg_ref,pair,sid)
        for m,x_ref in enumerate((x0_ref,x1_ref,x2_ref,x3_ref)):
            k=pl.multiple_of((idx_ref[0]^m)*256,256)
            for r in range(2):
                fstore(xt,r*1024+k,256,x_ref[...].astype(F32)[:,LW*r:LW*r+LW])
        for a in range(4):
            xa[a]=sload(xt,a,512,4).astype(BF)
    v=dot(xa[0],pick_matrix(g,0))
    for a in range(1,4):
        v=v+dot(xa[a],pick_matrix(g,a))
    x4[...]=v[:,:LW]
    respace(sid,x4,xr,xsf)
    n=XROWS+32
    zt=jnp.zeros((n+16,64),F32)
    va=xsf[0,0:n+16,:]; vb=xsf[1,0:n+16,:]
    z0=jnp.concatenate([zt,va[:,:64]],axis=1); z1=jnp.concatenate([va[:,64:],vb[:,:64]],axis=1)
    for at,piece in enumerate((va[0:n].astype(BF),(vb[0:n]+z0[16:]).astype(BF),z1[16:].astype(BF))):
        xs_ref[0,0,:,128*at:128*at+128]=piece[:XROWS]
        xs_ref[0,0,:,384+128*at:512+128*at]=piece[32:]
    s=dot(xs_ref[0,0,512:512+MROWS,0:256],w_ref[0,6144:6400,:])
    for J in range(8):
        s=s+dot(xs_ref[0,0,64*J:64*J+MROWS,:],w_ref[0,768*J:768*J+768,:])
    acc[0]=s[:,:128]; acc[1]=s[:,128:]
    bias=bias_ref[0]
    def emit(row,v):
        pre_ref[0,0,pl.ds(row,16),:]=v+bias
    unspace(sid,acc,yr,emit)
    pre=pre_ref[0,0]
    fs=(x4[...]+pre*erf_gelu_parts(pre)).astype(BF)
    for a in range(4):
        f=dot(fs,pick_back(g,a))[:,:LW]
        @pl.when(g==0)
        def _(): facc[a]=f
        @pl.when(g>0)
        def _(): facc[a]=facc[a]+f
    @pl.when(g==3)
    def _():
        for a in range(4):
            sstore(xt,a,512,4,facc[a])
        first_ref[...]=jnp.concatenate([fload(xt,0,1024),fload(xt,1024,1024)],axis=1).astype(BF)

def conv_fwd(ends,idx,xs4,w,bias4):
    pairs=xs4[0].shape[0]//256
    return pl.pallas_call(conv_fwd_kernel,grid=(pairs,4),
        in_specs=[pl.BlockSpec(memory_space=pltpu.SMEM)]*2+[pl.BlockSpec((256,PW),lambda p,g:(p,0))]*4+[
                  pl.BlockSpec((1,WROWS,256),lambda p,g:(g,0,0)),
                  pl.BlockSpec((1,1,LW),lambda p,g:(g,0,0))],
        out_specs=[pl.BlockSpec((1024,PW),lambda p,g:(p,0)),
                   pl.BlockSpec((1,1,512,LW),lambda p,g:(p,g,0,0)),
                   pl.BlockSpec((1,1,XROWS,768),lambda p,g:(p,g,0,0))],
        out_shape=[jax.ShapeDtypeStruct((pairs*1024,PW),BF),
                   jax.ShapeDtypeStruct((pairs,4,512,LW),F32),
                   jax.ShapeDtypeStruct((pairs,4,XROWS,768),BF)],
        scratch_shapes=[pltpu.VMEM((2,2048,128),F32),pltpu.VMEM((4,512,LW),BF),pltpu.VMEM((512,LW),F32),
            pltpu.VMEM((2,416,LW),F32),pltpu.VMEM((2,XROWS+TAIL,128),F32),pltpu.VMEM((2,MROWS,128),F32),pltpu.VMEM((2,384,LW),F32),
            pltpu.VMEM((4,512,LW),F32),pltpu.VMEM((512,LW),jnp.int32)],
        cost_estimate=cost(35),
        compiler_params=pltpu.CompilerParams(vmem_limit_bytes=VM))(ends,idx,*xs4,w,bias4)

def tap_kernel(seg_ref,e0_ref,e1_ref,first_ref,stat_ref,mom_ref,mox_ref,gain_ref,pre_ref,xs_ref,qkv_ref,tap_ref,ds_ref,d4_ref,bias_ref,vec_ref,xt,xa,dc,xr,xsf,A,sid):
    pair=pl.program_id(0); g=pl.program_id(1)
    @pl.when(g==0)
    def _():
        fill_ids(seg_ref,pair,sid)
        gain=gain_ref[...]
        sg=jnp.zeros((1,LW),F32); sh=jnp.zeros((1,LW),F32)
        for t in range(8):
            r,k=t//4,t%4
            rows=slice(256*k,256*k+256); cols=slice(LW*r,LW*r+LW)
            e=(e0_ref[rows]+e1_ref[rows].astype(F32))[:,cols]
            st=stat_ref[256*t:256*t+256]
            mean=st[:,0:1]; rstd=st[:,1:2]
            mom=jnp.concatenate([mom_ref[t,0:2]+mox_ref[2*t:2*t+2].astype(F32)[:,:256],jnp.zeros((126,256),F32)],axis=0).T*(1.0/768)
            xhat=(first_ref[rows].astype(F32)[:,cols]-mean)*rstd
            sg=sg+jnp.sum(e*xhat,axis=0,keepdims=True); sh=sh+jnp.sum(e,axis=0,keepdims=True)
            fstore(xt,256*t,256,rstd*(e*gain-mom[:,0:1]-xhat*mom[:,1:2]))
        vec_ref[0,0:1]=sg; vec_ref[0,1:2]=sh; vec_ref[0,2:8]=jnp.zeros((6,LW),F32)
        for a in range(4):
            xa[a]=sload(xt,a,512,4).astype(BF)
    v=dot(xa[0],pick_matrix(g,0))
    for a in range(1,4):
        v=v+dot(xa[a],pick_matrix(g,a))
    v=v[:,:LW]
    d4_ref[0,0]=v.astype(BF)
    pre=pre_ref[0,0]
    cdf=erf_gelu_parts(pre)
    slope=cdf+pre*(jnp.exp(-0.5*pre*pre)*0.3989422804014327)
    d=v*slope
    dc[...]=d
    bias_ref[0,0]=jnp.sum(d,axis=0,keepdims=True)
    respace(sid,dc,xr,xsf)
    ds_ref[0,0,:,0:128]=xsf[0,0:XROWS].astype(BF); ds_ref[0,0,:,128:256]=xsf[1,0:XROWS].astype(BF)
    DT=fload(xsf,256,MROWS).astype(BF).T
    for J in range(8):
        A[:,768*J:768*J+768]=dot(DT,xs_ref[0,0,64*J:64*J+MROWS,:])
    A[:,6144:6400]=dot(DT,xs_ref[0,0,512:512+MROWS,0:256])
    n=6144
    o=A[0:48,0:n]
    for b in range(1,4):
        o=o+A[48*b:48*b+48,48*b:48*b+n]
    for J in range(8):
        tap_ref[0,J]=o[:,768*J:768*J+768].astype(BF)
    tap_ref[0,8:11]=jnp.where(pair==0,qkv_ref[...],jnp.zeros((3,48,768),BF))

def tap_grads(ends,e0,e1,first,stat,mom,gain,pre,xs,g_qkv,deps=()):
    pairs=e0.shape[0]//1024
    return pl.pallas_call(skip(tap_kernel,11,len(deps)),grid=(pairs,4),
        in_specs=[pl.BlockSpec(memory_space=pltpu.SMEM),
                  pl.BlockSpec((1024,PW),lambda p,g:(p,0)),
                  pl.BlockSpec((1024,PW),lambda p,g:(p,0)),
                  pl.BlockSpec((1024,PW),lambda p,g:(p,0)),
                  pl.BlockSpec((2048,128),lambda p,g:(p,0)),
                  pl.BlockSpec((8,8,256),lambda p,g:(p,0,0)),
                  pl.BlockSpec((16,PW),lambda p,g:(64*pairs+p,0)),
                  pl.BlockSpec((1,LW),lambda p,g:(0,0)),
                  pl.BlockSpec((1,1,512,LW),lambda p,g:(p,g,0,0)),
                  pl.BlockSpec((1,1,XROWS,768),lambda p,g:(p,g,0,0)),
                  pl.BlockSpec((3,48,768),lambda p,g:(0,g,0))]+[ANY]*len(deps),
        out_specs=[pl.BlockSpec((1,11,48,768),lambda p,g:(p,0,g,0)),
                   pl.BlockSpec((1,1,XROWS,256),lambda p,g:(p,g,0,0)),
                   pl.BlockSpec((1,1,512,LW),lambda p,g:(p,g,0,0)),
                   pl.BlockSpec((1,1,1,LW),lambda p,g:(p,g,0,0)),
                   pl.BlockSpec((1,8,LW),lambda p,g:(p,0,0))],
        out_shape=[jax.ShapeDtypeStruct((pairs,11,LW,768),BF),
                   jax.ShapeDtypeStruct((pairs,4,XROWS,256),BF),
                   jax.ShapeDtypeStruct((pairs,4,512,LW),BF),
                   jax.ShapeDtypeStruct((pairs,4,1,LW),F32),jax.ShapeDtypeStruct((pairs,8,LW),F32)],
        scratch_shapes=[pltpu.VMEM((2,2048,128),F32),pltpu.VMEM((4,512,LW),BF),pltpu.VMEM((512,LW),F32),
            pltpu.VMEM((2,416,LW),F32),pltpu.VMEM((2,XROWS+TAIL,128),F32),pltpu.VMEM((LW,6400),F32),pltpu.VMEM((512,LW),jnp.int32)],
        cost_estimate=cost(24),
        compiler_params=pltpu.CompilerParams(vmem_limit_bytes=VM))(ends,e0,e1,first,stat,mom,e1,gain,pre,xs,g_qkv,*deps)

def back_kernel(at,seg_ref,idx_ref,ds_ref,d4_ref,w_ref,*rest):
    if at:
        part_ref,out_ref,xt,acc,yr,fs,sid=rest
    else:
        facc,acc,yr,fs,sid=rest
    pair=pl.program_id(0); i=pl.program_id(1); g=i+at
    @pl.when(i==0)
    def _(): fill_ids(seg_ref,pair,sid)
    s=None
    for j in range(NJ):
        p=dot_nt(ds_ref[0,0,16*(NJ-1-j):16*(NJ-1-j)+MROWS,:],w_ref[0,LW*j:LW*j+256,:])
        s=p if s is None else s+p
    def emit(row,v):
        fs[pl.ds(row,16),:]=(v+d4_ref[0,0,pl.ds(row,16),:].astype(F32)).astype(BF)
    acc[0]=s[:,:128]; acc[1]=s[:,128:]
    unspace(sid,acc,yr,emit)
    if at:
        for a in range(4):
            f=dot(fs[...],pick_back(g,a))[:,:LW]
            @pl.when(i==0)
            def _(): sstore(xt,a,512,4,f+part_ref[0,a])
            @pl.when(i>0)
            def _(): sstore(xt,a,512,4,f+sload(xt,a,512,4))
        @pl.when(i==1)
        def _():
            for k in range(4):
                out_ref[idx_ref[0]^k]=jnp.concatenate([fload(xt,k*256,256),fload(xt,1024+k*256,256)],axis=1).astype(BF)
    else:
        for a in range(4):
            f=dot(fs[...],pick_back(g,a))[:,:LW]
            @pl.when(i==0)
            def _(): facc[0,a]=f
            @pl.when(i>0)
            def _(): facc[0,a]=facc[0,a]+f

def conv_back(at,ends,idx,ds,d4,w,part=None,deps=()):
    pairs=ds.shape[0]
    parts=() if part is None else (part,)
    facc=pl.BlockSpec((1,4,512,LW),lambda p,g:(p,0,0,0))
    scratch=[pltpu.VMEM((2,2048,128),F32)] if at else []
    return pl.pallas_call(skip(lambda *refs: back_kernel(at,*refs),5+len(parts),len(deps)),grid=(pairs,2),
        in_specs=[pl.BlockSpec(memory_space=pltpu.SMEM),pl.BlockSpec(memory_space=pltpu.SMEM),
                  pl.BlockSpec((1,1,XROWS,256),lambda p,g:(p,g+at,0,0)),
                  pl.BlockSpec((1,1,512,LW),lambda p,g:(p,g+at,0,0)),
                  pl.BlockSpec((1,WROWS,256),lambda p,g:(g+at,0,0))]+[facc]*len(parts)+[ANY]*len(deps),
        out_specs=pl.BlockSpec((4,256,PW),lambda p,g:(0,p,0)) if at else facc,
        out_shape=jax.ShapeDtypeStruct((4,pairs*256,PW),BF) if at else jax.ShapeDtypeStruct((pairs,4,512,LW),F32),
        scratch_shapes=scratch+[pltpu.VMEM((2,MROWS,128),F32),pltpu.VMEM((2,384,LW),F32),
            pltpu.VMEM((512,LW),BF),pltpu.VMEM((512,LW),jnp.int32)],
        cost_estimate=cost(100),
        compiler_params=pltpu.CompilerParams(vmem_limit_bytes=VM))(ends,idx,ds,d4,w,*parts,*deps)


def qkv_kernel(f0,f1,f2,f3,w_ref,bias_ref,gain_ref,shift_ref,q_ref,k_ref,v_ref,ml_ref,stat_ref):
    fs=[f[...].astype(F32) for f in (f0,f1,f2,f3)]
    fs=[jnp.concatenate([f[:,:LW],f[:,LW:]],axis=0) for f in fs]
    mean=sum(jnp.sum(f,axis=1,keepdims=True) for f in fs)*(1.0/768)
    cs=[f-mean for f in fs]
    var=sum(jnp.sum(c*c,axis=1,keepdims=True) for c in cs)*(1.0/768)
    rstd=lax.rsqrt(var+1e-5)
    n=mean.shape[0]
    pad=jnp.zeros((n,64),BF)
    out=None
    for m in range(4):
        ml=(cs[m]*rstd*gain_ref[m]+shift_ref[m]).astype(BF)
        ml_ref[m]=ml.reshape(2,256,LW)
        p=dot(jnp.concatenate([ml,pad],axis=1),w_ref[m])
        out=p if out is None else out+p
    out=(out+bias_ref[...]).astype(BF)
    out=out.reshape(2,256,768)
    q_ref[...]=out[:,:,0:192]; k_ref[...]=out[:,:,256:448]; v_ref[...]=out[:,:,512:704]
    lane=lax.broadcasted_iota(jnp.int32,(n,128),1)
    stat_ref[...]=jnp.where(lane==0,mean,jnp.where(lane==1,rstd,0.0)).reshape(2,256,128)

def qkv(fs,w,bias,gain,shift):
    pairs=fs[0].shape[0]//1024; R=2*pairs
    row=pl.BlockSpec((2,256,LW),lambda p,k:(p,k,0))
    full=lambda a: pl.BlockSpec(a.shape,lambda p,k:(0,)*a.ndim)
    return pl.pallas_call(qkv_kernel,grid=(pairs,4),
        in_specs=[pl.BlockSpec((256,PW),lambda p,k:(4*p+k,0))]*4+[full(w),full(bias),full(gain),full(shift)],
        out_specs=[row]*3+[pl.BlockSpec((4,2,256,LW),lambda p,k:(0,p,k,0)),pl.BlockSpec((2,256,128),lambda p,k:(p,k,0))],
        out_shape=[jax.ShapeDtypeStruct((R,1024,LW),BF)]*3+[jax.ShapeDtypeStruct((4,R,1024,LW),BF),jax.ShapeDtypeStruct((R,1024,128),F32)],
        cost_estimate=cost(10),
        compiler_params=pltpu.CompilerParams(vmem_limit_bytes=VM))(*fs,w,bias,gain,shift)

def seg_vec(seg_ref,r,shape,axis,start):
    t=lax.broadcasted_iota(jnp.int32,shape,axis)+start
    v=jnp.zeros(shape,jnp.int32)
    for i in range(8):
        v=v+(t>=seg_ref[r,i]).astype(jnp.int32)
    return v

def attn_kernel(idx_ref,seg_ref,q_ref,k_ref,v_ref,o_ref,of_ref,lse_ref):
    pair=pl.program_id(0); kb=pl.program_id(1)
    for r in range(2):
        sq=seg_vec(seg_ref,2*pair+r,(256,1),0,kb*256); sk=seg_vec(seg_ref,2*pair+r,(1,1024),1,0)
        same=sq==sk
        outs=[]; rows=[]
        for h in range(3):
            c=slice(64*h,64*h+64)
            s=jnp.where(same,dot_nt(q_ref[r,:,c],k_ref[r,:,c]),-1e30)
            mx=jnp.max(s,axis=1,keepdims=True)
            p=jnp.exp(s-mx)
            tot=jnp.sum(p,axis=1,keepdims=True)
            outs.append(dot(p.astype(BF),v_ref[r,:,c])/tot)
            rows.append(jnp.broadcast_to(mx+jnp.log(tot),(256,128)).T[0:1,:])
        o=jnp.concatenate(outs,axis=1)
        of_ref[r]=o
        o_ref[0,:,LW*r:LW*r+LW]=o.astype(BF)
        lse_ref[r,0]=jnp.concatenate(rows+[jnp.zeros((5,256),F32)],axis=0)

def attn(idx,ends,q,k,v):
    R=ends.shape[0]; pairs=R//2
    blk=pl.BlockSpec((2,256,LW),lambda p,b,i,s:(p,b,0)); full=pl.BlockSpec((2,1024,LW),lambda p,b,i,s:(p,0,0))
    return pl.pallas_call(attn_kernel,
        grid_spec=pltpu.PrefetchScalarGridSpec(num_scalar_prefetch=2,grid=(pairs,4),
        in_specs=[blk,full,full],
        out_specs=[pl.BlockSpec((1,256,PW),lambda p,b,i,s:(b^i[0],p,0)),blk,pl.BlockSpec((2,1,8,256),lambda p,b,i,s:(p,b,0,0))]),
        out_shape=[jax.ShapeDtypeStruct((4,pairs*256,PW),BF),jax.ShapeDtypeStruct((R,1024,LW),F32),jax.ShapeDtypeStruct((R,4,8,256),F32)],
        cost_estimate=cost(18),
        compiler_params=pltpu.CompilerParams(vmem_limit_bytes=VM))(idx,ends,q,k,v)

def attn_bwd_kernel(r,idx_ref,seg_ref,q_ref,k_ref,v_ref,o_ref,d0,d1,d2,d3,lse_ref,dq_ref,dk_ref,dv_ref,dks,dvs):
    pair=pl.program_id(0); kb=pl.program_id(1)
    m=kb^idx_ref[0]
    mine=slice(LW*r,LW*r+LW)
    dod=jnp.where(m<2,jnp.where(m==0,d0[...],d1[...]),jnp.where(m==2,d2[...],d3[...])).astype(F32)[:,mine].astype(BF)
    @pl.when(kb==0)
    def _():
        dks[...]=jnp.zeros_like(dks); dvs[...]=jnp.zeros_like(dvs)
    sq=seg_vec(seg_ref,2*pair+r,(1,256),1,kb*256); sk=seg_vec(seg_ref,2*pair+r,(1024,1),0,0)
    same=sk==sq
    dqs=[]; ks=[]; vs=[]
    for h in range(3):
        c=slice(64*h,64*h+64)
        q=q_ref[0,:,c]; k=k_ref[0,:,c]; do=dod[:,c]
        delta=jnp.sum(do.astype(F32)*o_ref[0,:,c],axis=1,keepdims=True)
        delta=jnp.broadcast_to(delta,(256,128)).T[0:1,:]
        st=jnp.where(same,dot_nt(k,q)-lse_ref[0,0,h:h+1,:],-1e30)
        p=jnp.exp(st)
        dp=dot_nt(v_ref[0,:,c],do)
        ds=(p*(dp-delta)).astype(BF)
        vs.append(dot(p.astype(BF),do)); ks.append(dot(ds,q)); dqs.append(dot_tn(ds,k))
    dks[...]+=jnp.concatenate(ks,axis=1); dvs[...]+=jnp.concatenate(vs,axis=1)
    dq_ref[0]=jnp.concatenate(dqs,axis=1).astype(BF)
    @pl.when(kb==3)
    def _():
        dk_ref[0]=dks[...].astype(BF); dv_ref[0]=dvs[...].astype(BF)

def attn_bwd(r,idx,ends,q,k,v,o,dos,lse,deps=()):
    pairs=ends.shape[0]//2
    blk=pl.BlockSpec((1,256,LW),lambda p,b,i,s:(2*p+r,b,0)); full=pl.BlockSpec((1,1024,LW),lambda p,b,i,s:(2*p+r,0,0))
    out=pl.BlockSpec((1,256,LW),lambda p,b,i,s:(p,b,0)); outs=pl.BlockSpec((1,1024,LW),lambda p,b,i,s:(p,0,0))
    return pl.pallas_call(skip(lambda *refs: attn_bwd_kernel(r,*refs),11,len(deps)),
        grid_spec=pltpu.PrefetchScalarGridSpec(num_scalar_prefetch=2,grid=(pairs,4),
        in_specs=[blk,full,full,blk]+[pl.BlockSpec((256,PW),lambda p,b,i,s:(p,0))]*4+[pl.BlockSpec((1,1,8,256),lambda p,b,i,s:(2*p+r,b,0,0))]+[ANY]*len(deps),
        out_specs=[out,outs,outs],scratch_shapes=[pltpu.VMEM((1024,LW),F32)]*2),
        out_shape=[jax.ShapeDtypeStruct((pairs,1024,LW),BF)]*3,
        cost_estimate=cost(60),
        compiler_params=pltpu.CompilerParams(vmem_limit_bytes=VM))(idx,ends,q,k,v,o,*dos,lse,*deps)

def pad3(a,b,c):
    z=jnp.zeros((a.shape[0],64),BF)
    return jnp.concatenate([a,z,b,z,c,z],axis=1)

def dmix_kernel(idx_ref,q0,k0,v0,q1,k1,v1,w_ref,sec_ref,f0,f1,f2,f3,stat_ref,gain_ref,keep_ref,send_ref,mom_ref):
    kb=pl.program_id(1)
    flat=lambda x: x[...].reshape(512,x.shape[-1])
    d=jnp.concatenate([pad3(q0[0],k0[0],v0[0]),pad3(q1[0],k1[0],v1[0])],axis=0)
    st=flat(stat_ref); mean=st[:,0:1]; rstd=st[:,1:2]
    mine=(kb==idx_ref[0]).astype(F32)
    m1=None
    for m,f in enumerate((f0,f1,f2,f3)):
        part=dot_nt(d,w_ref[m])[:,:LW]
        part=part+mine*sec_ref[m].reshape(512,LW)
        both=jnp.concatenate([part[:256],part[256:]],axis=1)
        if m%2: send_ref[m//2]=both.astype(BF)
        else: keep_ref[m//2]=both
        eg=part*gain_ref[m]
        f=f[...].astype(F32)
        xh=(jnp.concatenate([f[:,:LW],f[:,LW:]],axis=0)-mean)*rstd
        a=jnp.sum(eg,axis=1,keepdims=True); b=jnp.sum(eg*xh,axis=1,keepdims=True)
        m1=(a,b) if m1 is None else (m1[0]+a,m1[1]+b)
    lane=lax.broadcasted_iota(jnp.int32,(512,128),1)
    t=jnp.where(lane==0,m1[0],jnp.where(lane==1,m1[1],0.0)).T[0:8,:]
    mom_ref[0,0]=t[:,:256]; mom_ref[1,0]=t[:,256:]

def dmix(idx,heads,w,sec,fs,stat,gain,deps=()):
    pairs=heads[0].shape[0]; R=2*pairs
    blk=pl.BlockSpec((1,256,LW),lambda p,b,i:(p,b,0))
    full=lambda a: pl.BlockSpec(a.shape,lambda p,b,i:(0,)*a.ndim)
    pack=pl.BlockSpec((2,256,PW),lambda p,b,i:(0,4*p+b,0))
    return pl.pallas_call(skip(dmix_kernel,15,len(deps)),
        grid_spec=pltpu.PrefetchScalarGridSpec(num_scalar_prefetch=1,grid=(pairs,4),
        in_specs=[blk]*6+[full(w),pl.BlockSpec((4,2,256,LW),lambda p,b,i:(0,p,0,0))]+[pl.BlockSpec((256,PW),lambda p,b,i:(4*p+b,0))]*4
            +[pl.BlockSpec((2,256,128),lambda p,b,i:(p,b,0)),full(gain)]+[ANY]*len(deps),
        out_specs=[pack,pack,pl.BlockSpec((2,1,8,256),lambda p,b,i:(p,b,0,0))]),
        out_shape=[jax.ShapeDtypeStruct((2,pairs*1024,PW),F32),jax.ShapeDtypeStruct((2,pairs*1024,PW),BF),jax.ShapeDtypeStruct((R,4,8,256),F32)],
        cost_estimate=cost(0.1),
        compiler_params=pltpu.CompilerParams(vmem_limit_bytes=VM))(idx,*heads,w,sec,*fs,stat,gain,*deps)

def qkvw_kernel(q0,k0,v0,q1,k1,v1,ml_ref,out_ref,bias_ref,acc):
    i=pl.program_id(0)*2+pl.program_id(1)
    @pl.when(i==0)
    def _(): acc[...]=jnp.zeros_like(acc); bias_ref[...]=jnp.zeros_like(bias_ref)
    d=jnp.concatenate([pad3(q0[0],k0[0],v0[0]),pad3(q1[0],k1[0],v1[0])],axis=0)
    dt=d.T
    bias_ref[...]+=jnp.broadcast_to(jnp.sum(d.astype(F32),axis=0,keepdims=True),bias_ref.shape)
    pad=jnp.zeros((d.shape[0],64),BF)
    for m in range(4):
        acc[m]+=dot(dt,jnp.concatenate([ml_ref[m].reshape(d.shape[0],LW),pad],axis=1))
    @pl.when(i==2*pl.num_programs(0)-1)
    def _():
        for t in range(3):
            out_ref[t]=jnp.concatenate([acc[m,256*t:256*t+192,:LW] for m in range(4)],axis=1).astype(BF)

def qkvw(heads,ml,deps=()):
    pairs=heads[0].shape[0]
    row=pl.BlockSpec((1,512,LW),lambda p,i:(p,i,0))
    return pl.pallas_call(skip(qkvw_kernel,7,len(deps)),grid=(pairs,2),
        in_specs=[row]*6+[pl.BlockSpec((4,2,512,LW),lambda p,i:(0,p,i,0))]+[ANY]*len(deps),
        out_specs=[pl.BlockSpec((3,LW,768),lambda p,i:(0,0,0)),pl.BlockSpec((8,768),lambda p,i:(0,0))],
        out_shape=[jax.ShapeDtypeStruct((3,LW,768),BF),jax.ShapeDtypeStruct((8,768),F32)],
        scratch_shapes=[pltpu.VMEM((4,768,256),F32)],
        cost_estimate=cost(8),
        compiler_params=pltpu.CompilerParams(vmem_limit_bytes=VM))(*heads,ml,*deps)


def row_sum(x):
    return jnp.sum(x, axis=0, keepdims=True)


def norm_parts(x):
    c = x - jnp.mean(x, axis=1, keepdims=True)
    rstd = lax.rsqrt(jnp.mean(c * c, axis=1, keepdims=True) + 1e-5)
    return c * rstd, rstd


def norm_back(e, xhat, rstd, gain):
    eg = e * gain
    return rstd * (eg - jnp.mean(eg, axis=1, keepdims=True) - xhat * jnp.mean(eg * xhat, axis=1, keepdims=True))


def in_order(blocks, index):
    low = (index & 1) != 0
    high = (index & 2) != 0
    b = [jnp.where(low, blocks[m ^ 1], blocks[m]) for m in range(4)]
    return jnp.concatenate([jnp.where(high, b[m ^ 2], b[m]) for m in range(4)], axis=1)


def half(r):
    return slice(LW * (r % 2), LW * (r % 2) + LW)


def ff_kernel(
    idx_ref, f0, f1, f2, f3, a0, a1, a2, a3, og_ref, pw_ref, iw_ref, ow_ref, ib_ref, vec_ref,
    out_ref, act_ref, din_ref, ml_ref, do_ref, dp_ref, att_ref, datt_ref, sec_ref, sums_ref, ibg_ref,
    mid, xh2, rs2, acc, slopes,
):
    i = pl.program_id(0)
    index = idx_ref[0]
    R = 2 * f0.shape[0]
    M = R * 256
    pos_gain, pos_shift, proj_bias, gain2, shift2, outer_bias, gain3, shift3 = [vec_ref[j : j + 1, :] for j in range(8)]

    @pl.when(i == 0)
    def _():
        for r in range(R):
            rows = pl.ds(256 * r, 256)
            xhat, _ = norm_parts(in_order([f[r // 2, 0].astype(F32)[:, half(r)] for f in (f0, f1, f2, f3)], index))
            att_ref[rows] = in_order([a[pl.ds(256 * (r // 2), 256)].astype(F32)[:, half(r)] for a in (a0, a1, a2, a3)], index).astype(BF)
            second = xhat * pos_gain + pos_shift + dot(att_ref[rows], pw_ref[...]) + proj_bias
            xhat, rstd = norm_parts(second)
            xh2[rows] = xhat
            rs2[rows] = jnp.broadcast_to(rstd, (256, 128))
            middle = xhat * gain2 + shift2
            mid[rows] = middle
            ml_ref[rows] = middle.astype(BF)
        acc[...] = jnp.zeros_like(acc)

    @pl.when(i < 4)
    def _():
        for r in range(R):
            rows = pl.ds(256 * r, 256)
            inner = dot(ml_ref[rows], iw_ref[...]) + ib_ref[0]
            phi = erf_gelu_parts(inner)
            slopes[i, rows] = (phi + inner * (jnp.exp(-0.5 * inner * inner) * 0.3989422804014327)).astype(BF)
            act_ref[rows] = (inner * phi).astype(BF)
            acc[rows] += dot(act_ref[rows], ow_ref[...])

    @pl.when(i == 3)
    def _():
        g1 = g2 = g3 = jnp.zeros((1, 768), F32)
        for r in range(R):
            rows = pl.ds(256 * r, 256)
            xhat, rstd = norm_parts(mid[rows] + acc[rows] + outer_bias)
            out_ref[rows] = (xhat * gain3 + shift3).astype(BF)
            e = og_ref[rows].astype(F32)
            d = norm_back(e, xhat, rstd, gain3)
            low = d.astype(BF)
            do_ref[rows] = low
            mid[rows] = d
            g1, g2, g3 = g1 + row_sum(e * xhat), g2 + row_sum(e), g3 + row_sum(low.astype(F32))
        sums_ref[0:1] = g1
        sums_ref[1:2] = g2
        sums_ref[2:3] = g3
        sums_ref[3:8] = jnp.zeros((5, 768), F32)

    @pl.when(i >= 4)
    def _():
        g = jnp.zeros((1, 768), F32)
        for r in range(R):
            rows = pl.ds(256 * r, 256)
            d = dot_nt(do_ref[rows], ow_ref[...]) * slopes[7 - i, rows].astype(F32)
            low = d.astype(BF)
            din_ref[rows] = low
            g = g + row_sum(low.astype(F32))
            mid[rows] += dot_nt(low, iw_ref[...])
        ibg_ref[0] = g

    @pl.when(i == 7)
    def _():
        g1 = g2 = g3 = jnp.zeros((1, 768), F32)
        for r in range(R):
            rows = pl.ds(256 * r, 256)
            e = mid[rows]
            xhat = xh2[rows]
            d = norm_back(e, xhat, rs2[rows, 0:1], gain2)
            low = d.astype(BF)
            dp_ref[rows] = low
            datt = dot_nt(low, pw_ref[...]).astype(BF)
            for b in range(4):
                datt_ref[index ^ b, pl.ds(256 * (r // 2), 256), half(r)] = datt[:, LW * b : LW * b + LW]
                sec_ref[index ^ b, r] = d[:, LW * b : LW * b + LW]
            g1, g2, g3 = g1 + row_sum(e * xhat), g2 + row_sum(e), g3 + row_sum(low.astype(F32))
        sums_ref[3:4] = g1
        sums_ref[4:5] = g2
        sums_ref[5:6] = g3


def ff(idx, firsts, atts, out_grad, pw, iw, ow, ib, vec):
    pairs = atts[0].shape[0] // 256
    R = 2 * pairs
    M = R * 256
    chunk = lambda i: jnp.where(i < 4, i, 7 - i)
    whole = lambda *s: pl.BlockSpec(s, lambda i, x: (0,) * len(s))
    return pl.pallas_call(
        ff_kernel,
        grid_spec=pltpu.PrefetchScalarGridSpec(
            num_scalar_prefetch=1,
            grid=(8,),
            in_specs=[pl.BlockSpec((pairs, 1, 256, PW), lambda i, x: (0, x[0], 0, 0))] * 4
            + [whole(pairs * 256, PW)] * 4
            + [
                whole(M, 768),
                whole(768, 768),
                pl.BlockSpec((768, 768), lambda i, x: (0, chunk(i))),
                pl.BlockSpec((768, 768), lambda i, x: (chunk(i), 0)),
                pl.BlockSpec((1, 1, 768), lambda i, x: (chunk(i), 0, 0)),
                whole(8, 768),
            ],
            out_specs=[
                whole(M, 768),
                pl.BlockSpec((M, 768), lambda i, x: (0, jnp.minimum(i, 3))),
                pl.BlockSpec((M, 768), lambda i, x: (0, jnp.minimum(7 - i, 3))),
            ]
            + [whole(M, 768)] * 4
            + [
                whole(4, pairs * 256, PW),
                whole(4, R, 256, LW),
                whole(8, 768),
                pl.BlockSpec((1, 1, 768), lambda i, x: (jnp.minimum(7 - i, 3), 0, 0)),
            ],
            scratch_shapes=[
                pltpu.VMEM((M, 768), F32),
                pltpu.VMEM((M, 768), F32),
                pltpu.VMEM((M, 128), F32),
                pltpu.VMEM((M, 768), F32),
                pltpu.VMEM((4, M, 768), BF),
            ],
        ),
        out_shape=[
            jax.ShapeDtypeStruct((M, 768), BF),
            jax.ShapeDtypeStruct((M, 3072), BF),
            jax.ShapeDtypeStruct((M, 3072), BF),
        ]
        + [jax.ShapeDtypeStruct((M, 768), BF)] * 4
        + [
            jax.ShapeDtypeStruct((4, pairs * 256, PW), BF),
            jax.ShapeDtypeStruct((4, R, 256, LW), F32),
            jax.ShapeDtypeStruct((8, 768), F32),
            jax.ShapeDtypeStruct((4, 1, 768), F32),
        ],
        cost_estimate=cost(40),
        compiler_params=pltpu.CompilerParams(vmem_limit_bytes=VM),
    )(idx, *[f.reshape(pairs, 4, 256, PW) for f in firsts], *atts, out_grad, pw, iw, ow, ib, vec)


def put(index, keep, send, b, rows, value):
    m = index ^ b

    @pl.when((m & 1) == 0)
    def _():
        keep[m >> 1, rows] = value

    @pl.when((m & 1) == 1)
    def _():
        send[m >> 1, rows] = value


def outer_kernel(idx_ref, act_ref, do_ref, sums_ref, ibg_ref, keep_ref, send_ref):
    c = pl.program_id(0)
    index = idx_ref[0]
    outer = dot_tn(do_ref[...], act_ref[...]).astype(BF)
    for b in range(4):
        put(index, keep_ref, send_ref, b, pl.ds(pl.multiple_of(LW * c, LW), LW), outer[LW * b : LW * b + LW])

    @pl.when(c == 0)
    def _():
        for b in range(4):
            small = jnp.concatenate([sums_ref[:, LW * b : LW * b + LW], jnp.zeros((8, 576), F32)], axis=1)
            small = jnp.concatenate([small, ibg_ref[b], jnp.zeros((7, 768), F32)], axis=0)
            put(index, keep_ref, send_ref, b, pl.ds(768, 16), small.astype(BF))
            put(index, keep_ref, send_ref, b, pl.ds(784, 48), jnp.zeros((48, 768), BF))


def inner_kernel(idx_ref, din_ref, ml_ref, dp_ref, att_ref, keep_ref, send_ref):
    c = pl.program_id(0)
    index = idx_ref[0]
    put(index, keep_ref, send_ref, c, pl.ds(0, 768), dot_tn(ml_ref[...], din_ref[...]).astype(BF))

    @pl.when(c == 0)
    def _():
        proj = dot_tn(dp_ref[...], att_ref[...]).astype(BF)
        for b in range(4):
            put(index, keep_ref, send_ref, b, pl.ds(768, LW), proj[LW * b : LW * b + LW])


def weight_grads(kernel, rows, idx, wide, others, deps=()):
    M = wide.shape[0]
    whole = lambda a: pl.BlockSpec(a.shape, lambda i, x: (0,) * a.ndim)
    out = pl.BlockSpec((2, rows, 768), lambda i, x: (0, 0, 0))
    return pl.pallas_call(
        skip(kernel, 2 + len(others), len(deps)),
        grid_spec=pltpu.PrefetchScalarGridSpec(
            num_scalar_prefetch=1,
            grid=(4,),
            in_specs=[pl.BlockSpec((M, 768), lambda i, x: (0, i))] + [whole(a) for a in others] + [ANY] * len(deps),
            out_specs=[out, out],
        ),
        out_shape=[jax.ShapeDtypeStruct((2, rows, 768), BF)] * 2,
        cost_estimate=cost(8),
        compiler_params=pltpu.CompilerParams(vmem_limit_bytes=VM),
    )(idx, wide, *others, *deps)


def far_kernel(keep_ref, got_ref, out_ref):
    out_ref[...] = (keep_ref[0].astype(F32) + got_ref[0].astype(F32)).astype(BF)


def far_sum(keep, got, deps=()):
    n = keep.shape[1]
    block = pl.BlockSpec((1, n // 2, 768), lambda i: (1, i, 0))
    return pl.pallas_call(
        skip(far_kernel, 2, len(deps)),
        grid=(2,),
        in_specs=[block] * 2 + [ANY] * len(deps),
        out_specs=pl.BlockSpec((n // 2, 768), lambda i: (i, 0)),
        out_shape=jax.ShapeDtypeStruct((n, 768), BF),
        cost_estimate=cost(1),
        compiler_params=pltpu.CompilerParams(vmem_limit_bytes=VM),
    )(keep, got, *deps)


def own_kernel(keep_ref, got_ref, far_ref, out_ref):
    x = keep_ref[0].astype(F32) + got_ref[0].astype(F32) + far_ref[...].astype(F32)
    out_ref[...] = x.astype(BF).reshape(out_ref.shape)


def own_sum(keep, got, far, deps=()):
    n = keep.shape[1]
    block = pl.BlockSpec((1, n // 2, 768), lambda i: (0, i, 0))
    one = pl.BlockSpec((n // 2, 768), lambda i: (i, 0))
    return pl.pallas_call(
        skip(own_kernel, 3, len(deps)),
        grid=(2,),
        in_specs=[block] * 2 + [one] + [ANY] * len(deps),
        out_specs=one,
        out_shape=jax.ShapeDtypeStruct((n, 768), BF),
        cost_estimate=cost(1),
        compiler_params=pltpu.CompilerParams(vmem_limit_bytes=VM),
    )(keep, got, far, *deps)


def finish_kernel(in_ref, outer_ref, small_ref):
    for i in range(4):
        outer_ref[:, 768 * i : 768 * i + 768] = in_ref[LW * i : LW * i + LW].astype(F32)
    small_ref[...] = in_ref[768:784].astype(F32)


def finish(grads, deps=()):
    whole = lambda *s: pl.BlockSpec(s, lambda: (0, 0))
    shapes = (LW, 3072), (16, 768)
    return pl.pallas_call(
        skip(finish_kernel, 1, len(deps)),
        in_specs=[whole(832, 768)] + [ANY] * len(deps),
        out_specs=[whole(*s) for s in shapes],
        out_shape=[jax.ShapeDtypeStruct(s, F32) for s in shapes],
        cost_estimate=cost(6),
        compiler_params=pltpu.CompilerParams(vmem_limit_bytes=VM),
    )(grads, *deps)


def widen_kernel(in_ref, inner_ref, proj_ref):
    inner_ref[...] = in_ref[:768].astype(F32)
    proj_ref[...] = in_ref[768:].astype(F32)


def widen(x, deps=()):
    whole = lambda *s: pl.BlockSpec(s, lambda: (0, 0))
    shapes = (768, 768), (LW, 768)
    return pl.pallas_call(
        skip(widen_kernel, 1, len(deps)),
        in_specs=[whole(960, 768)] + [ANY] * len(deps),
        out_specs=[whole(*s) for s in shapes],
        out_shape=[jax.ShapeDtypeStruct(s, F32) for s in shapes],
        cost_estimate=cost(3),
        compiler_params=pltpu.CompilerParams(vmem_limit_bytes=VM),
    )(x, *deps)


def taps_kernel(own_ref, scale_ref, dir_ref, out_ref, square_ref, tmp):
    n = dir_ref.shape[0]
    at = pl.program_id(0) * n
    side = own_ref[0] // 2
    for k in range(n):
        x = dir_ref[k].astype(F32)
        total = jnp.sum(jnp.sum(x * x, axis=0, keepdims=True), axis=1, keepdims=True)
        square_ref[k : k + 1] = jnp.broadcast_to(total, (1, 128))
        x = jnp.where(side != 0, x[:, PW:], x[:, :PW])
        tmp[48 * k : 48 * k + 48] = (x * (scale_ref[at + k] * lax.rsqrt(total))).astype(BF)
    out_ref[...] = dot(tmp[...], own_pick(own_ref[0]))[:, :LW].astype(BF)


def own_pick(index):
    row = lax.broadcasted_iota(jnp.int32, (PW, 256), 0)
    lane = lax.broadcasted_iota(jnp.int32, (PW, 256), 1)
    return ((row == lane + LW * (index & 1)) & (lane < LW)).astype(F32).astype(BF)


def own_taps(idx, scale, tap_dir):
    return pl.pallas_call(
        taps_kernel,
        grid_spec=pltpu.PrefetchScalarGridSpec(
            num_scalar_prefetch=2,
            grid=(8,),
            in_specs=[pl.BlockSpec((16, 48, 768), lambda i, x, c: (i, 0, 0))],
            out_specs=[pl.BlockSpec((768, LW), lambda i, x, c: (i, 0)), pl.BlockSpec((16, 128), lambda i, x, c: (i, 0))],
            scratch_shapes=[pltpu.VMEM((768, PW), BF)],
        ),
        out_shape=[jax.ShapeDtypeStruct((6144, LW), BF), jax.ShapeDtypeStruct((128, 128), F32)],
        cost_estimate=cost(10),
        compiler_params=pltpu.CompilerParams(vmem_limit_bytes=VM),
    )(idx, scale, tap_dir)


def raw_kernel(own_ref, dir_ref, out_ref):
    out_ref[...] = dot(dir_ref[...], own_pick(own_ref[0]))[:, :LW].astype(BF)


def own_dirs(idx, tap_dir, deps=()):
    return pl.pallas_call(
        skip(raw_kernel, 2, len(deps)),
        grid_spec=pltpu.PrefetchScalarGridSpec(
            num_scalar_prefetch=1,
            grid=(4,),
            in_specs=[pl.BlockSpec((1536, PW), lambda i, x: (i, x[0] // 2))] + [ANY] * len(deps),
            out_specs=pl.BlockSpec((1536, LW), lambda i, x: (i, 0)),
        ),
        out_shape=jax.ShapeDtypeStruct((6144, LW), BF),
        cost_estimate=cost(5),
        compiler_params=pltpu.CompilerParams(vmem_limit_bytes=VM),
    )(idx, tap_dir.reshape(6144, 768), *deps)


def dots_kernel(tap_ref, dir_ref, out_ref):
    g = tap_ref[0].astype(F32).T
    p = g * dir_ref[...].astype(F32)
    rows = [jnp.sum(p[48 * t : 48 * t + 48], axis=0, keepdims=True) for t in range(16)]
    s = jnp.sum(jnp.concatenate(rows, axis=0), axis=1, keepdims=True)
    out_ref[0] = jnp.broadcast_to(s, (16, 128))


def tap_dots(tap, dirs, deps=()):
    return pl.pallas_call(
        skip(dots_kernel, 2, len(deps)),
        grid=(8,),
        in_specs=[pl.BlockSpec((1, LW, 768), lambda i: (i, 0, 0)), pl.BlockSpec((768, LW), lambda i: (i, 0))] + [ANY] * len(deps),
        out_specs=pl.BlockSpec((1, 16, 128), lambda i: (i, 0, 0)),
        out_shape=jax.ShapeDtypeStruct((8, 16, 128), F32),
        cost_estimate=cost(6),
        compiler_params=pltpu.CompilerParams(vmem_limit_bytes=VM),
    )(tap, dirs, *deps)


def last_kernel(left_ref, right_ref, dir_ref, coef_ref, beta_ref, out_ref, turned):
    i = pl.program_id(0)

    @pl.when(i == 0)
    def _():
        for J in range(8):
            for p, ref in enumerate((left_ref, right_ref)):
                t = ref[J].astype(F32).T
                at = 768 * J + 384 * p
                turned[0, at : at + 384] = t[:, :128]
                turned[1, at : at + 384, :64] = t[:, 128:]

    for c in range(8):
        at = pl.ds(8 * i + c, 128, stride=48)
        g = jnp.concatenate([turned[0, at].T, turned[1, at].T[:64]], axis=0)
        out_ref[c] = g * coef_ref[...] - dir_ref[c].astype(F32) * beta_ref[...]


def last_taps(coef, beta, left, right, dirs, deps=()):
    row = pl.BlockSpec((1, 128), lambda i: (0, 0))
    block = pl.BlockSpec((8, LW, 128), lambda i: (i, 0, 0))
    return pl.pallas_call(
        skip(last_kernel, 5, len(deps)),
        grid=(6,),
        in_specs=[pl.BlockSpec((8, LW, 384), lambda i: (0, 0, 0))] * 2 + [block, row, row] + [ANY] * len(deps),
        out_specs=block,
        out_shape=jax.ShapeDtypeStruct((48, LW, 128), F32),
        scratch_shapes=[pltpu.VMEM((2, 6144, 128), F32)],
        cost_estimate=cost(8),
        compiler_params=pltpu.CompilerParams(vmem_limit_bytes=VM),
    )(left, right, dirs, coef[None], beta[None], *deps)


def near_kernel(keep_ref, got_ref, mom_ref, mom_got, near_ref, far_ref, mom_out):
    N = keep_ref.shape[1]
    near_ref[...] = keep_ref[0] + got_ref[0].astype(F32)
    far_ref[:N] = (keep_ref[1] + got_ref[1].astype(F32)).astype(BF)
    mom = mom_ref[...] + mom_got[...]
    mom_out[...] = mom
    R = mom.shape[0]
    rows = jnp.concatenate([mom[r, k, 0:2] for r in range(R) for k in range(4)], axis=0)
    far_ref[N:] = jnp.concatenate([rows, jnp.zeros((8 * R, 128), F32)], axis=1).astype(BF)


def near_far(keep, got, moments, moments_got):
    N = keep.shape[1]
    R = moments.shape[0]
    whole = lambda a: pl.BlockSpec(a.shape, lambda: (0,) * a.ndim)
    shapes = [
        jax.ShapeDtypeStruct((N, PW), F32),
        jax.ShapeDtypeStruct((N + 8 * R, PW), BF),
        jax.ShapeDtypeStruct(moments.shape, F32),
    ]
    return pl.pallas_call(
        near_kernel,
        in_specs=[whole(a) for a in (keep, got, moments, moments_got)],
        out_specs=[whole(a) for a in shapes],
        out_shape=shapes,
        cost_estimate=cost(2),
        compiler_params=pltpu.CompilerParams(vmem_limit_bytes=VM),
    )(keep, got, moments, moments_got)


HALF = 384


def pick_kernel(bits_ref, a_ref, b_ref, sa_ref, sb_ref):
    sa_ref[...] = a_ref[...]
    sb_ref[...] = b_ref[...]


def first_sends(bits, x, deps=()):
    L, N, _ = x.shape
    n = N // 4
    out = pl.BlockSpec((L, n, HALF), lambda i, s: (0, i, 0))
    return pl.pallas_call(
        skip(pick_kernel, 3, len(deps)),
        grid_spec=pltpu.PrefetchScalarGridSpec(
            num_scalar_prefetch=1,
            grid=(2,),
            in_specs=[
                pl.BlockSpec((L, n, HALF), lambda i, s: (0, 2 - 2 * s[0] + i, 0)),
                pl.BlockSpec((L, n, HALF), lambda i, s: (0, 2 - 2 * s[1] + i, 1)),
            ]
            + [ANY] * len(deps),
            out_specs=[out, out],
        ),
        out_shape=[jax.ShapeDtypeStruct((L, N // 2, HALF), BF)] * 2,
        cost_estimate=cost(3),
        compiler_params=pltpu.CompilerParams(vmem_limit_bytes=VM),
    )(bits, x, x, *deps)


def stage_kernel(last, steps, bits_ref, ka, kb, ra, rb, *outs):
    i = pl.program_id(0)
    for p, (k, r) in enumerate(((ka, ra), (kb, rb))):
        y = k[...].reshape(r.shape).astype(F32) + r[...].astype(F32)
        if last:
            outs[p][...] = y.astype(BF)
            continue
        sum_ref, send_ref = outs[p], outs[2 + p]
        h = y.shape[1] * steps // 2
        halves = ((i, y),) if steps == 2 else ((0, y[:, :h]), (1, y[:, h:]))
        for at, half in halves:
            sum_ref[:, 0 if steps == 2 else at] = half.astype(BF)

            @pl.when(bits_ref[2 + p] != at)
            def _():
                send_ref[...] = half.astype(BF)


def stage(bits, a, b, ra, rb, last, deps=()):
    L, n, _ = ra.shape
    h = n // 2
    steps = 2 if not last and h % 16 == 0 else 1
    m = n // steps
    if a.ndim == 3:
        keep = lambda p: pl.BlockSpec((L, m, HALF), lambda i, s: (0, steps * s[p] + i, p))
    else:
        keep = lambda p: pl.BlockSpec((L, 1, m, HALF), lambda i, s: (0, s[p], i, 0))
    row = pl.BlockSpec((L, m, HALF), lambda i, s: (0, i, 0))
    if last:
        out_specs, out_shape = [row] * 2, [jax.ShapeDtypeStruct((L, n, HALF), BF)] * 2
    else:
        out_specs = [pl.BlockSpec((L, 2 // steps, h, HALF), lambda i, s: (0, i, 0, 0))] * 2
        out_specs += [pl.BlockSpec((L, h, HALF), lambda i, s: (0, 0, 0))] * 2
        out_shape = [jax.ShapeDtypeStruct((L, 2, h, HALF), BF)] * 2 + [jax.ShapeDtypeStruct((L, h, HALF), BF)] * 2
    return pl.pallas_call(
        skip(lambda *refs: stage_kernel(last, steps, *refs), 5, len(deps)),
        grid_spec=pltpu.PrefetchScalarGridSpec(
            num_scalar_prefetch=1,
            grid=(steps,),
            in_specs=[keep(0), keep(1), row, row] + [ANY] * len(deps),
            out_specs=out_specs,
        ),
        out_shape=out_shape,
        cost_estimate=cost(3),
        compiler_params=pltpu.CompilerParams(vmem_limit_bytes=VM),
    )(bits, a, b, ra, rb, *deps)


def join_kernel(bits_ref, a, b, ra, rb, oa, ob):
    for p, (k, r, o) in enumerate(((a, ra, oa), (b, rb, ob))):
        on = bits_ref[p]
        o[on] = k[...]
        o[1 - on] = r[...]


def join(bits, a, b, ra, rb, deps=()):
    shape = a.shape
    block = pl.BlockSpec(shape, lambda i, s: (0,) * len(shape))
    out = pl.BlockSpec((2,) + shape, lambda i, s: (0,) * (len(shape) + 1))
    oa, ob = pl.pallas_call(
        skip(join_kernel, 5, len(deps)),
        grid_spec=pltpu.PrefetchScalarGridSpec(
            num_scalar_prefetch=1,
            grid=(1,),
            in_specs=[block] * 4 + [ANY] * len(deps),
            out_specs=[out] * 2,
        ),
        out_shape=[jax.ShapeDtypeStruct((2,) + shape, BF)] * 2,
        cost_estimate=cost(2),
        compiler_params=pltpu.CompilerParams(vmem_limit_bytes=VM),
    )(bits, a, b, ra, rb, *deps)
    flat = (2 * shape[0],) + shape[1:]
    return oa.reshape(flat), ob.reshape(flat)


class RowSum:
    def __init__(self, x, deps=()):
        n = lax.axis_size("rows")
        bits = [1 << i for i in range(n.bit_length() - 1)]
        self.orders = (bits, bits[1::-1] + bits[2:])
        self.count = x.shape[1]
        full = -(-self.count // (16 * n)) * (16 * n) if n > 8 else self.count
        if full != self.count:
            x = jnp.pad(x, ((0, 0), (0, full - self.count), (0, 0)))
        self.parts = [x, x]
        self.at = 0
        self.got = None
        self.steps = len(bits)
        self.sends = first_sends(self.bits(0), x, deps)

    def bits(self, s):
        place = lax.axis_index("rows")
        pick = lambda o, i: (place // o[min(i, self.steps - 1)]) % 2
        return jnp.stack([pick(o, i) for i in (s, s + 1) for o in self.orders]).astype(jnp.int32)

    def go(self):
        self.got = [swap(s, "rows", o[self.at]) for s, o in zip(self.sends, self.orders)]

    def step(self, *deps):
        if self.got is None:
            self.go()
        got, self.got = self.got, None
        last = self.at == self.steps - 1
        outs = stage(self.bits(self.at), *self.parts, *got, last, deps)
        self.parts, self.sends = outs[:2], outs[2:]
        self.at += 1
        return self.parts[0]

    def back(self, *deps):
        self.at -= 1
        got = [swap(p, "rows", o[self.at]) for p, o in zip(self.parts, self.orders)]
        self.parts = join(self.bits(self.at), *self.parts, *got, deps)
        return self.parts[0]

    def result(self):
        return [p.reshape(-1, HALF)[: self.count] for p in self.parts]


def swap(x, axis, bit):
    return lax.ppermute(x, axis, [(i, i ^ bit) for i in range(lax.axis_size(axis))])


def gather_seq(x):
    far = swap(x, "seq", 2)
    near = swap(x, "seq", 1)
    return [x, near, far, swap(far, "seq", 1)]


def trade(blocks):
    return [blocks[0], swap(blocks[1], "seq", 1), swap(blocks[2], "seq", 2), swap(blocks[3], "seq", 3)]


def all_sum(x, axis):
    for i in range(lax.axis_size(axis).bit_length() - 1):
        x = x + swap(x, axis, 1 << i)
    return x


def assemble(blocks, index):
    low = (index & 1) != 0
    high = (index & 2) != 0
    b = [jnp.where(low, blocks[m ^ 1], blocks[m]) for m in range(4)]
    return [jnp.where(high, b[m ^ 2], b[m]) for m in range(4)]


def cut(x, start, size, axis):
    return lax.dynamic_slice_in_dim(x, start, size, axis)


def local(
    frames,
    utterance_lengths,
    tap_dir,
    tap_scale,
    conv_bias,
    pos_gain,
    pos_shift,
    query_weight,
    query_bias,
    key_weight,
    value_weight,
    value_bias,
    proj_weight,
    proj_bias,
    attend_gain,
    attend_shift,
    inner_weight,
    inner_bias,
    outer_weight,
    outer_bias,
    final_gain,
    final_shift,
    out_grad,
):
    R = frames.shape[0]
    index = lax.axis_index("seq")
    idx = jnp.full((1,), index, jnp.int32)
    ends = jnp.cumsum(utterance_lengths, axis=1, dtype=jnp.int32)
    order = [index ^ m for m in range(4)]
    own = index * LW

    def packed(x):
        return jnp.concatenate([x[0::2], x[1::2]], axis=2).reshape(R * 128, PW)

    sent = trade([packed(cut(frames, b * LW, LW, 2)) for b in order])
    taps, squares = own_taps(idx, tap_scale, tap_dir)
    w = build_w(taps)
    bias4 = jnp.tile(cut(conv_bias, own, LW, 0).reshape(4, 1, 48), (1, 4, 1)).reshape(4, 1, LW)
    first, pre, xs = conv_fwd(ends, idx, sent, w, bias4)
    firsts = gather_seq(first)

    def xor_rows(a):
        return jnp.stack([cut(a, b * LW, LW, 0) for b in order])

    def pad_to(a, axis, size):
        widths = [(0, 0)] * a.ndim
        widths[axis] = (0, size - a.shape[axis])
        return jnp.pad(a, widths)

    own_cols = [
        pad_to(cut(a, own, LW, 1), 1, 256)
        for a in (query_weight * jnp.asarray(0.125, BF), key_weight, value_weight)
    ]
    w_qkv = pad_to(xor_rows(jnp.concatenate(own_cols, axis=1)), 1, 256)
    b_qkv = jnp.concatenate(
        [
            pad_to(cut(query_bias, own, LW, 0) * 0.125, 0, 512),
            pad_to(cut(value_bias, own, LW, 0), 0, 256),
        ]
    )[None]
    gain_x = xor_rows(pos_gain)[:, None]
    shift_x = xor_rows(pos_shift)[:, None]
    q, k, v, mixed_low, stat = qkv(firsts, w_qkv, b_qkv, gain_x, shift_x)
    att, att_full, lse = attn(idx, ends, q, k, v)
    att_blocks = trade([att[m] for m in range(4)])

    vecs = jnp.stack([pos_gain, pos_shift, proj_bias, attend_gain, attend_shift, outer_bias, final_gain, final_shift])
    layer_out, act, d_inner, middle_low, d_outer, d_proj, attended, d_att, second_x, sums, inner_sums = ff(
        idx, firsts, att_blocks, out_grad.reshape(R * 256, 768), proj_weight, inner_weight, outer_weight,
        inner_bias.reshape(4, 1, 768), vecs,
    )
    dos = trade_out(d_att)
    keep_out, send_out = weight_grads(outer_kernel, 832, idx, act, (d_outer, sums, inner_sums))
    got_out = swap(send_out, "seq", 1)
    keep_in, send_in = weight_grads(inner_kernel, 960, idx, d_inner, (middle_low, d_proj, attended), (send_out,))
    far = far_sum(keep_out, got_out, (send_in,))
    got_in = swap(send_in, "seq", 1)

    heads = attn_bwd(0, idx, ends, q, k, v, att_full, dos, lse, (far,))
    heads += attn_bwd(1, idx, ends, q, k, v, att_full, dos, lse, (heads[0],))
    grads = own_sum(keep_out, got_out, swap(far, "seq", 2), (heads[3],))
    keep, send, moments = dmix(idx, heads, w_qkv, second_x, firsts, stat, gain_x, (grads,))
    grads_out = lax.psum(grads, "rows")
    e_near, e_far, moments = near_far(keep, swap(send, "seq", 1), moments, swap(moments, "seq", 1))
    g_qkv, b_grads = qkvw(heads, mixed_low, (e_far,))
    e_sent = e_far
    e_far = swap(e_far, "seq", 2)
    far = swap(far_sum(keep_in, got_in, (e_sent, g_qkv)), "seq", 2)
    dir_own = own_dirs(idx, tap_dir, (e_sent, g_qkv))
    dir_turned = jnp.transpose(dir_own.reshape(128, 48, LW), (1, 2, 0))
    moments = moments.reshape(R * 4, 8, 256)

    tap_part, ds, d4, conv_b, vec = tap_grads(
        ends, e_near, e_far, first, stat.reshape(R * 1024, 128), moments, cut(pos_gain, own, LW, 0)[None], pre, xs, g_qkv, (dir_own,),
    )
    if R > 2:
        tap_part = jnp.sum(tap_part.astype(F32), axis=0, keepdims=True).astype(BF)
    tap_part = tap_part[0]
    tap_sum = RowSum(tap_part.reshape(1, 11 * LW, 768))
    part = conv_back(0, ends, idx, ds, d4, w, None, tuple(tap_sum.sends))
    tap_sum.step(part)
    grads_in = lax.psum(own_sum(keep_in, got_in, far, (part, grads_out)), "rows")
    back = conv_back(2, ends, idx, ds, d4, w, part, tuple(tap_sum.sends))
    tap_sum.step(back)
    dots = tap_dots(tap_part, dir_own, tuple(tap_sum.sends))
    tap_sum.step(dots)
    dots = all_sum(dots[:, :, 0], "seq")
    back = trade_out(back)
    back = jnp.concatenate([b.reshape(R // 2, 1, 256, PW) for b in assemble(back, index)], axis=1)
    back = back.reshape(R // 2, 4, 256, 2, LW)
    frames_grad = jnp.transpose(back, (0, 3, 2, 1, 4)).reshape(R, 256, 768)
    while tap_sum.at:
        tap_sum.back()
    tap_left, tap_right = [p.reshape(11, LW, HALF) for p in tap_sum.result()]
    qkv_std = assemble([x[8:11, :, LW * m : LW * m + LW] for x in (tap_left, tap_right) for m in range(2)], index)
    t_qkv = jnp.concatenate(qkv_std, axis=2).astype(F32)
    t_outer, small = finish(grads_out, (tap_sum.parts[0],))
    lates = jnp.concatenate(
        [
            jnp.sum(conv_b, axis=(0, 2)).reshape(4, 4, 48).sum(1).reshape(LW),
            jnp.sum(vec[:, 0], axis=0),
            jnp.sum(vec[:, 1], axis=0),
            b_grads[0, 0:LW] * 0.125,
            b_grads[0, 512 : 512 + LW],
            dots.reshape(128),
            jnp.zeros((2048 - 1088,), F32),
        ]
    )
    lates = all_sum(lates.reshape(16, 128), "rows").reshape(2048)
    dots = lates[5 * LW : 5 * LW + 128]
    inverse = lax.rsqrt(squares[:, 0])
    coef = tap_scale * inverse
    turned = last_taps(coef, coef * dots * inverse * inverse, tap_left, tap_right, dir_turned, (frames_grad, t_outer))
    g_tap_dir = jnp.transpose(turned, (2, 0, 1))
    t_inner, t_proj = widen(grads_in, (turned,))
    g_tap_scale = cut(dots * inverse, index * 32, 32, 0)

    return (
        layer_out.reshape(R, 256, 768),
        frames_grad,
        g_tap_dir,
        g_tap_scale,
        lates[0:LW],
        lates[LW : 2 * LW],
        lates[2 * LW : 3 * LW],
        t_qkv[0].T * 0.125,
        lates[3 * LW : 4 * LW],
        t_qkv[1].T,
        t_qkv[2].T,
        lates[4 * LW : 5 * LW],
        t_proj.T,
        small[5, :LW],
        small[3, :LW],
        small[4, :LW],
        t_inner,
        small[8],
        t_outer.T,
        small[2, :LW],
        small[0, :LW],
        small[1, :LW],
    )


def trade_out(x):
    return trade([x[m] for m in range(4)])


def solution(mesh):
    split = P("rows", "seq", None)
    col = P(None, "seq")
    one = P("seq")
    return jax.shard_map(
        local,
        mesh=mesh,
        in_specs=(split, P("rows", None)) + (P(),) * 20 + (split,),
        out_specs=(split, split, P(None, None, "seq"), one, one, one, one)
        + (col, one, col, col, one, col, one, one, one, col, one, col, one, one, one),
        check_vma=False,
    )
```

```python
import jax, jax.numpy as jnp
from jax import lax
from jax.sharding import PartitionSpec as P
from jax.experimental import pallas as pl
from jax.experimental.pallas import tpu as pltpu
F32=jnp.float32; BF=jnp.bfloat16
CH=48; PH=4; LW=PH*CH
NJ=33; SEGL=48; XROWS=(SEGL+NJ-1)*16; MROWS=SEGL*16
VM=60*1024*1024

def cost(us):
    return pl.CostEstimate(flops=int(us*1.0e9),bytes_accessed=int(us*3.0e6),transcendentals=0)

ANY=pl.BlockSpec(memory_space=pl.ANY)
PW=2*LW

def skip(kernel,at,count):
    if not count:
        return kernel
    return lambda *refs: kernel(*refs[:at],*refs[at+count:])

def dot(a,b): return jnp.dot(a,b,preferred_element_type=F32)
def dot_nt(a,b): return lax.dot_general(a,b,(((1,),(1,)),((),())),preferred_element_type=F32)
def dot_tn(a,b): return lax.dot_general(a,b,(((0,),(0,)),((),())),preferred_element_type=F32)

def erf_gelu_parts(v):
    phi=0.5*(1.0+lax.erf(v*0.7071067811865476))
    return phi

WROWS=6400
def build_w_kernel(t_ref, w_ref, tp, rs):
    g=pl.program_id(0)
    rows=t_ref.shape[0]
    @pl.when(g==0)
    def _():
        tp[0:144,:]=jnp.zeros((144,LW),BF)
        tp[144:144+rows,:]=t_ref[...]
        tp[144+rows:,:]=jnp.zeros((256,LW),BF)
    src=lax.broadcasted_iota(jnp.int32,(LW,256),0); l=lax.broadcasted_iota(jnp.int32,(LW,256),1)
    pick=((src==48*g+lax.rem(l,48))&(l<LW)).astype(F32).astype(BF)
    n=1600
    lane=lax.broadcasted_iota(jnp.int32,(n,256),1)
    for i in range(WROWS//n):
        r0=i*n
        R=dot(tp[r0:r0+n+144,:],pick).astype(BF)
        lo=jnp.where(lane[:,:128]<96,jnp.where(lane[:,:128]<48,R[144:144+n,:128],R[96:96+n,:128]),R[48:48+n,:128])
        hi=jnp.where(lane[:,128:]<144,R[48:48+n,128:],R[0:n,128:])
        w_ref[0,r0:r0+n,:128]=lo
        w_ref[0,r0:r0+n,128:]=hi

def build_w(taps2):
    rows=taps2.shape[0]
    return pl.pallas_call(build_w_kernel,grid=(4,),
        in_specs=[pl.BlockSpec((rows,LW),lambda g:(0,0))],
        out_specs=pl.BlockSpec((1,WROWS,256),lambda g:(g,0,0)),
        out_shape=jax.ShapeDtypeStruct((4,WROWS,256),BF),
        scratch_shapes=[pltpu.VMEM((rows+144+256,LW),BF),pltpu.VMEM((16,256),BF)],
        cost_estimate=cost(10),
        compiler_params=pltpu.CompilerParams(vmem_limit_bytes=VM))(taps2)

def sload(ref,start,n,stride):
    return jnp.concatenate([ref[0,pl.ds(start,n,stride=stride),:],ref[1,pl.ds(start,n,stride=stride),:]],axis=1)[:,:LW]
def sstore(ref,start,n,stride,v):
    ref[0,pl.ds(start,n,stride=stride),:]=v[:,:128]
    ref[1,pl.ds(start,n,stride=stride),:]=jnp.concatenate([v[:,128:],jnp.zeros((n,64),v.dtype)],axis=1)
def fload(ref,start,n):
    return jnp.concatenate([ref[0,pl.ds(start,n),:],ref[1,pl.ds(start,n),:]],axis=1)[:,:LW]
def fstore(ref,start,n,v):
    ref[0,pl.ds(start,n),:]=v[:,:128]
    ref[1,pl.ds(start,n),:]=jnp.concatenate([v[:,128:],jnp.zeros((n,64),v.dtype)],axis=1)

def pick_matrix(g,a):
    ch=lax.broadcasted_iota(jnp.int32,(LW,256),0); l=lax.broadcasted_iota(jnp.int32,(LW,256),1)
    return ((ch==48*g+(l-48*a))&(l>=48*a)&(l<48*a+48)).astype(F32).astype(BF)

def pick_back(g,a):
    l=lax.broadcasted_iota(jnp.int32,(LW,256),0); ch=lax.broadcasted_iota(jnp.int32,(LW,256),1)
    return ((ch==48*g+(l-48*a))&(l>=48*a)&(l<48*a+48)).astype(F32).astype(BF)

def fill_ids(seg_ref,pair,sid):
    sub=lax.broadcasted_iota(jnp.int32,(256,LW),0); l=lax.broadcasted_iota(jnp.int32,(256,LW),1)
    t=4*sub+(l>=48).astype(jnp.int32)+(l>=96).astype(jnp.int32)+(l>=144).astype(jnp.int32)
    for r in range(2):
        v=jnp.zeros((256,LW),jnp.int32)
        end=0
        for q in range(7):
            end=end+seg_ref[pair*2+r,q]
            v=v+(t>=end).astype(jnp.int32)
        sid[pl.ds(256*r,256),:]=v

TAIL=48
def respace(sid,src,xr,xsf):
    xsf[0,1280:1280+TAIL,:]=jnp.zeros((TAIL,128),F32); xsf[1,1280:1280+TAIL,:]=jnp.zeros((TAIL,128),F32)
    for r in range(2):
        for B in range(26):
            v=jnp.zeros((16,LW),F32)
            for q in range(8):
                bb=B-1-q
                if 0<=bb<16:
                    rows=pl.ds(r*256+16*bb,16)
                    v=jnp.where(sid[rows,:]==q,src[rows,:],v)
            xr[r,pl.ds(16*B,16),:]=v
        for sp in range(8):
            sstore(xsf,r*8+sp,80,16,xr[r,pl.ds(48*sp,80),:])

def unspace(sid,acc,yr,emit):
    for r in range(2):
        for sp in range(8):
            yr[r,pl.ds(48*sp,48),:]=sload(acc,r*8+sp,48,16)
        for bb in range(16):
            v=jnp.zeros((16,LW),F32)
            ids=sid[pl.ds(r*256+16*bb,16),:]
            for q in range(8):
                v=jnp.where(ids==q,yr[r,pl.ds(16*(bb+q),16),:],v)
            emit(r*256+16*bb,v)

def conv_fwd_kernel(seg_ref,idx_ref,x0_ref,x1_ref,x2_ref,x3_ref,w_ref,bias_ref,first_ref,pre_ref,xs_ref,xt,xa,x4,xr,xsf,acc,yr,facc,sid):
    pair=pl.program_id(0); g=pl.program_id(1)
    @pl.when(g==0)
    def _():
        fill_ids(seg_ref,pair,sid)
        for m,x_ref in enumerate((x0_ref,x1_ref,x2_ref,x3_ref)):
            k=pl.multiple_of((idx_ref[0]^m)*256,256)
            for r in range(2):
                fstore(xt,r*1024+k,256,x_ref[...].astype(F32)[:,LW*r:LW*r+LW])
        for a in range(4):
            xa[a]=sload(xt,a,512,4).astype(BF)
    v=dot(xa[0],pick_matrix(g,0))
    for a in range(1,4):
        v=v+dot(xa[a],pick_matrix(g,a))
    x4[...]=v[:,:LW]
    respace(sid,x4,xr,xsf)
    n=XROWS+32
    zt=jnp.zeros((n+16,64),F32)
    va=xsf[0,0:n+16,:]; vb=xsf[1,0:n+16,:]
    z0=jnp.concatenate([zt,va[:,:64]],axis=1); z1=jnp.concatenate([va[:,64:],vb[:,:64]],axis=1)
    for at,piece in enumerate((va[0:n].astype(BF),(vb[0:n]+z0[16:]).astype(BF),z1[16:].astype(BF))):
        xs_ref[0,0,:,128*at:128*at+128]=piece[:XROWS]
        xs_ref[0,0,:,384+128*at:512+128*at]=piece[32:]
    s=dot(xs_ref[0,0,512:512+MROWS,0:256],w_ref[0,6144:6400,:])
    for J in range(8):
        s=s+dot(xs_ref[0,0,64*J:64*J+MROWS,:],w_ref[0,768*J:768*J+768,:])
    acc[0]=s[:,:128]; acc[1]=s[:,128:]
    bias=bias_ref[0]
    def emit(row,v):
        pre_ref[0,0,pl.ds(row,16),:]=v+bias
    unspace(sid,acc,yr,emit)
    pre=pre_ref[0,0]
    fs=(x4[...]+pre*erf_gelu_parts(pre)).astype(BF)
    for a in range(4):
        f=dot(fs,pick_back(g,a))[:,:LW]
        @pl.when(g==0)
        def _(): facc[a]=f
        @pl.when(g>0)
        def _(): facc[a]=facc[a]+f
    @pl.when(g==3)
    def _():
        for a in range(4):
            sstore(xt,a,512,4,facc[a])
        first_ref[...]=jnp.concatenate([fload(xt,0,1024),fload(xt,1024,1024)],axis=1).astype(BF)

def conv_fwd(ends,idx,xs4,w,bias4):
    pairs=xs4[0].shape[0]//256
    return pl.pallas_call(conv_fwd_kernel,grid=(pairs,4),
        in_specs=[pl.BlockSpec(memory_space=pltpu.SMEM)]*2+[pl.BlockSpec((256,PW),lambda p,g:(p,0))]*4+[
                  pl.BlockSpec((1,WROWS,256),lambda p,g:(g,0,0)),
                  pl.BlockSpec((1,1,LW),lambda p,g:(g,0,0))],
        out_specs=[pl.BlockSpec((1024,PW),lambda p,g:(p,0)),
                   pl.BlockSpec((1,1,512,LW),lambda p,g:(p,g,0,0)),
                   pl.BlockSpec((1,1,XROWS,768),lambda p,g:(p,g,0,0))],
        out_shape=[jax.ShapeDtypeStruct((pairs*1024,PW),BF),
                   jax.ShapeDtypeStruct((pairs,4,512,LW),F32),
                   jax.ShapeDtypeStruct((pairs,4,XROWS,768),BF)],
        scratch_shapes=[pltpu.VMEM((2,2048,128),F32),pltpu.VMEM((4,512,LW),BF),pltpu.VMEM((512,LW),F32),
            pltpu.VMEM((2,416,LW),F32),pltpu.VMEM((2,XROWS+TAIL,128),F32),pltpu.VMEM((2,MROWS,128),F32),pltpu.VMEM((2,384,LW),F32),
            pltpu.VMEM((4,512,LW),F32),pltpu.VMEM((512,LW),jnp.int32)],
        cost_estimate=cost(35),
        compiler_params=pltpu.CompilerParams(vmem_limit_bytes=VM))(ends,idx,*xs4,w,bias4)

def tap_kernel(seg_ref,e0_ref,e1_ref,first_ref,stat_ref,mom_ref,mox_ref,gain_ref,pre_ref,xs_ref,qkv_ref,tap_ref,ds_ref,d4_ref,bias_ref,vec_ref,xt,xa,dc,xr,xsf,A,sid):
    pair=pl.program_id(0); g=pl.program_id(1)
    @pl.when(g==0)
    def _():
        fill_ids(seg_ref,pair,sid)
        gain=gain_ref[...]
        sg=jnp.zeros((1,LW),F32); sh=jnp.zeros((1,LW),F32)
        for t in range(8):
            r,k=t//4,t%4
            rows=slice(256*k,256*k+256); cols=slice(LW*r,LW*r+LW)
            e=(e0_ref[rows]+e1_ref[rows].astype(F32))[:,cols]
            st=stat_ref[256*t:256*t+256]
            mean=st[:,0:1]; rstd=st[:,1:2]
            mom=jnp.concatenate([mom_ref[t,0:2]+mox_ref[2*t:2*t+2].astype(F32)[:,:256],jnp.zeros((126,256),F32)],axis=0).T*(1.0/768)
            xhat=(first_ref[rows].astype(F32)[:,cols]-mean)*rstd
            sg=sg+jnp.sum(e*xhat,axis=0,keepdims=True); sh=sh+jnp.sum(e,axis=0,keepdims=True)
            fstore(xt,256*t,256,rstd*(e*gain-mom[:,0:1]-xhat*mom[:,1:2]))
        vec_ref[0,0:1]=sg; vec_ref[0,1:2]=sh; vec_ref[0,2:8]=jnp.zeros((6,LW),F32)
        for a in range(4):
            xa[a]=sload(xt,a,512,4).astype(BF)
    v=dot(xa[0],pick_matrix(g,0))
    for a in range(1,4):
        v=v+dot(xa[a],pick_matrix(g,a))
    v=v[:,:LW]
    d4_ref[0,0]=v.astype(BF)
    pre=pre_ref[0,0]
    cdf=erf_gelu_parts(pre)
    slope=cdf+pre*(jnp.exp(-0.5*pre*pre)*0.3989422804014327)
    d=v*slope
    dc[...]=d
    bias_ref[0,0]=jnp.sum(d,axis=0,keepdims=True)
    respace(sid,dc,xr,xsf)
    ds_ref[0,0,:,0:128]=xsf[0,0:XROWS].astype(BF); ds_ref[0,0,:,128:256]=xsf[1,0:XROWS].astype(BF)
    DT=fload(xsf,256,MROWS).astype(BF).T
    for J in range(8):
        A[:,768*J:768*J+768]=dot(DT,xs_ref[0,0,64*J:64*J+MROWS,:])
    A[:,6144:6400]=dot(DT,xs_ref[0,0,512:512+MROWS,0:256])
    n=6144
    o=A[0:48,0:n]
    for b in range(1,4):
        o=o+A[48*b:48*b+48,48*b:48*b+n]
    for J in range(8):
        tap_ref[0,J]=o[:,768*J:768*J+768].astype(BF)
    tap_ref[0,8:11]=jnp.where(pair==0,qkv_ref[...],jnp.zeros((3,48,768),BF))

def tap_grads(ends,e0,e1,first,stat,mom,gain,pre,xs,g_qkv,deps=()):
    pairs=e0.shape[0]//1024
    return pl.pallas_call(skip(tap_kernel,11,len(deps)),grid=(pairs,4),
        in_specs=[pl.BlockSpec(memory_space=pltpu.SMEM),
                  pl.BlockSpec((1024,PW),lambda p,g:(p,0)),
                  pl.BlockSpec((1024,PW),lambda p,g:(p,0)),
                  pl.BlockSpec((1024,PW),lambda p,g:(p,0)),
                  pl.BlockSpec((2048,128),lambda p,g:(p,0)),
                  pl.BlockSpec((8,8,256),lambda p,g:(p,0,0)),
                  pl.BlockSpec((16,PW),lambda p,g:(64*pairs+p,0)),
                  pl.BlockSpec((1,LW),lambda p,g:(0,0)),
                  pl.BlockSpec((1,1,512,LW),lambda p,g:(p,g,0,0)),
                  pl.BlockSpec((1,1,XROWS,768),lambda p,g:(p,g,0,0)),
                  pl.BlockSpec((3,48,768),lambda p,g:(0,g,0))]+[ANY]*len(deps),
        out_specs=[pl.BlockSpec((1,11,48,768),lambda p,g:(p,0,g,0)),
                   pl.BlockSpec((1,1,XROWS,256),lambda p,g:(p,g,0,0)),
                   pl.BlockSpec((1,1,512,LW),lambda p,g:(p,g,0,0)),
                   pl.BlockSpec((1,1,1,LW),lambda p,g:(p,g,0,0)),
                   pl.BlockSpec((1,8,LW),lambda p,g:(p,0,0))],
        out_shape=[jax.ShapeDtypeStruct((pairs,11,LW,768),BF),
                   jax.ShapeDtypeStruct((pairs,4,XROWS,256),BF),
                   jax.ShapeDtypeStruct((pairs,4,512,LW),BF),
                   jax.ShapeDtypeStruct((pairs,4,1,LW),F32),jax.ShapeDtypeStruct((pairs,8,LW),F32)],
        scratch_shapes=[pltpu.VMEM((2,2048,128),F32),pltpu.VMEM((4,512,LW),BF),pltpu.VMEM((512,LW),F32),
            pltpu.VMEM((2,416,LW),F32),pltpu.VMEM((2,XROWS+TAIL,128),F32),pltpu.VMEM((LW,6400),F32),pltpu.VMEM((512,LW),jnp.int32)],
        cost_estimate=cost(24),
        compiler_params=pltpu.CompilerParams(vmem_limit_bytes=VM))(ends,e0,e1,first,stat,mom,e1,gain,pre,xs,g_qkv,*deps)

def back_kernel(at,seg_ref,idx_ref,ds_ref,d4_ref,w_ref,*rest):
    if at:
        part_ref,out_ref,xt,acc,yr,fs,sid=rest
    else:
        facc,acc,yr,fs,sid=rest
    pair=pl.program_id(0); i=pl.program_id(1); g=i+at
    @pl.when(i==0)
    def _(): fill_ids(seg_ref,pair,sid)
    s=None
    for j in range(NJ):
        p=dot_nt(ds_ref[0,0,16*(NJ-1-j):16*(NJ-1-j)+MROWS,:],w_ref[0,LW*j:LW*j+256,:])
        s=p if s is None else s+p
    def emit(row,v):
        fs[pl.ds(row,16),:]=(v+d4_ref[0,0,pl.ds(row,16),:].astype(F32)).astype(BF)
    acc[0]=s[:,:128]; acc[1]=s[:,128:]
    unspace(sid,acc,yr,emit)
    if at:
        for a in range(4):
            f=dot(fs[...],pick_back(g,a))[:,:LW]
            @pl.when(i==0)
            def _(): sstore(xt,a,512,4,f+part_ref[0,a])
            @pl.when(i>0)
            def _(): sstore(xt,a,512,4,f+sload(xt,a,512,4))
        @pl.when(i==1)
        def _():
            for k in range(4):
                out_ref[idx_ref[0]^k]=jnp.concatenate([fload(xt,k*256,256),fload(xt,1024+k*256,256)],axis=1).astype(BF)
    else:
        for a in range(4):
            f=dot(fs[...],pick_back(g,a))[:,:LW]
            @pl.when(i==0)
            def _(): facc[0,a]=f
            @pl.when(i>0)
            def _(): facc[0,a]=facc[0,a]+f

def conv_back(at,ends,idx,ds,d4,w,part=None,deps=()):
    pairs=ds.shape[0]
    parts=() if part is None else (part,)
    facc=pl.BlockSpec((1,4,512,LW),lambda p,g:(p,0,0,0))
    scratch=[pltpu.VMEM((2,2048,128),F32)] if at else []
    return pl.pallas_call(skip(lambda *refs: back_kernel(at,*refs),5+len(parts),len(deps)),grid=(pairs,2),
        in_specs=[pl.BlockSpec(memory_space=pltpu.SMEM),pl.BlockSpec(memory_space=pltpu.SMEM),
                  pl.BlockSpec((1,1,XROWS,256),lambda p,g:(p,g+at,0,0)),
                  pl.BlockSpec((1,1,512,LW),lambda p,g:(p,g+at,0,0)),
                  pl.BlockSpec((1,WROWS,256),lambda p,g:(g+at,0,0))]+[facc]*len(parts)+[ANY]*len(deps),
        out_specs=pl.BlockSpec((4,256,PW),lambda p,g:(0,p,0)) if at else facc,
        out_shape=jax.ShapeDtypeStruct((4,pairs*256,PW),BF) if at else jax.ShapeDtypeStruct((pairs,4,512,LW),F32),
        scratch_shapes=scratch+[pltpu.VMEM((2,MROWS,128),F32),pltpu.VMEM((2,384,LW),F32),
            pltpu.VMEM((512,LW),BF),pltpu.VMEM((512,LW),jnp.int32)],
        cost_estimate=cost(100),
        compiler_params=pltpu.CompilerParams(vmem_limit_bytes=VM))(ends,idx,ds,d4,w,*parts,*deps)


def qkv_kernel(f0,f1,f2,f3,w_ref,bias_ref,gain_ref,shift_ref,q_ref,k_ref,v_ref,ml_ref,stat_ref):
    fs=[f[...].astype(F32) for f in (f0,f1,f2,f3)]
    fs=[jnp.concatenate([f[:,:LW],f[:,LW:]],axis=0) for f in fs]
    mean=sum(jnp.sum(f,axis=1,keepdims=True) for f in fs)*(1.0/768)
    cs=[f-mean for f in fs]
    var=sum(jnp.sum(c*c,axis=1,keepdims=True) for c in cs)*(1.0/768)
    rstd=lax.rsqrt(var+1e-5)
    n=mean.shape[0]
    pad=jnp.zeros((n,64),BF)
    out=None
    for m in range(4):
        ml=(cs[m]*rstd*gain_ref[m]+shift_ref[m]).astype(BF)
        ml_ref[m]=ml.reshape(2,256,LW)
        p=dot(jnp.concatenate([ml,pad],axis=1),w_ref[m])
        out=p if out is None else out+p
    out=(out+bias_ref[...]).astype(BF)
    out=out.reshape(2,256,768)
    q_ref[...]=out[:,:,0:192]; k_ref[...]=out[:,:,256:448]; v_ref[...]=out[:,:,512:704]
    lane=lax.broadcasted_iota(jnp.int32,(n,128),1)
    stat_ref[...]=jnp.where(lane==0,mean,jnp.where(lane==1,rstd,0.0)).reshape(2,256,128)

def qkv(fs,w,bias,gain,shift):
    pairs=fs[0].shape[0]//1024; R=2*pairs
    row=pl.BlockSpec((2,256,LW),lambda p,k:(p,k,0))
    full=lambda a: pl.BlockSpec(a.shape,lambda p,k:(0,)*a.ndim)
    return pl.pallas_call(qkv_kernel,grid=(pairs,4),
        in_specs=[pl.BlockSpec((256,PW),lambda p,k:(4*p+k,0))]*4+[full(w),full(bias),full(gain),full(shift)],
        out_specs=[row]*3+[pl.BlockSpec((4,2,256,LW),lambda p,k:(0,p,k,0)),pl.BlockSpec((2,256,128),lambda p,k:(p,k,0))],
        out_shape=[jax.ShapeDtypeStruct((R,1024,LW),BF)]*3+[jax.ShapeDtypeStruct((4,R,1024,LW),BF),jax.ShapeDtypeStruct((R,1024,128),F32)],
        cost_estimate=cost(10),
        compiler_params=pltpu.CompilerParams(vmem_limit_bytes=VM))(*fs,w,bias,gain,shift)

def seg_vec(seg_ref,r,shape,axis,start):
    t=lax.broadcasted_iota(jnp.int32,shape,axis)+start
    v=jnp.zeros(shape,jnp.int32)
    end=0
    for i in range(8):
        end=end+seg_ref[r,i]
        v=v+(t>=end).astype(jnp.int32)
    return v

def attn_kernel(idx_ref,seg_ref,q_ref,k_ref,v_ref,o_ref,of_ref,lse_ref):
    pair=pl.program_id(0); kb=pl.program_id(1)
    for r in range(2):
        sq=seg_vec(seg_ref,2*pair+r,(256,1),0,kb*256); sk=seg_vec(seg_ref,2*pair+r,(1,1024),1,0)
        same=sq==sk
        outs=[]; rows=[]
        for h in range(3):
            c=slice(64*h,64*h+64)
            s=jnp.where(same,dot_nt(q_ref[r,:,c],k_ref[r,:,c]),-1e30)
            mx=jnp.max(s,axis=1,keepdims=True)
            p=jnp.exp(s-mx)
            tot=jnp.sum(p,axis=1,keepdims=True)
            outs.append(dot(p.astype(BF),v_ref[r,:,c])/tot)
            rows.append(jnp.broadcast_to(mx+jnp.log(tot),(256,128)).T[0:1,:])
        o=jnp.concatenate(outs,axis=1)
        of_ref[r]=o
        o_ref[0,:,LW*r:LW*r+LW]=o.astype(BF)
        lse_ref[r,0]=jnp.concatenate(rows+[jnp.zeros((5,256),F32)],axis=0)

def attn(idx,ends,q,k,v):
    R=ends.shape[0]; pairs=R//2
    blk=pl.BlockSpec((2,256,LW),lambda p,b,i,s:(p,b,0)); full=pl.BlockSpec((2,1024,LW),lambda p,b,i,s:(p,0,0))
    return pl.pallas_call(attn_kernel,
        grid_spec=pltpu.PrefetchScalarGridSpec(num_scalar_prefetch=2,grid=(pairs,4),
        in_specs=[blk,full,full],
        out_specs=[pl.BlockSpec((1,256,PW),lambda p,b,i,s:(b^i[0],p,0)),blk,pl.BlockSpec((2,1,8,256),lambda p,b,i,s:(p,b,0,0))]),
        out_shape=[jax.ShapeDtypeStruct((4,pairs*256,PW),BF),jax.ShapeDtypeStruct((R,1024,LW),F32),jax.ShapeDtypeStruct((R,4,8,256),F32)],
        cost_estimate=cost(18),
        compiler_params=pltpu.CompilerParams(vmem_limit_bytes=VM))(idx,ends,q,k,v)

def attn_bwd_kernel(r,idx_ref,seg_ref,q_ref,k_ref,v_ref,o_ref,d0,d1,d2,d3,lse_ref,dq_ref,dk_ref,dv_ref,dks,dvs):
    pair=pl.program_id(0); kb=pl.program_id(1)
    m=kb^idx_ref[0]
    mine=slice(LW*r,LW*r+LW)
    dod=jnp.where(m<2,jnp.where(m==0,d0[...],d1[...]),jnp.where(m==2,d2[...],d3[...])).astype(F32)[:,mine].astype(BF)
    @pl.when(kb==0)
    def _():
        dks[...]=jnp.zeros_like(dks); dvs[...]=jnp.zeros_like(dvs)
    sq=seg_vec(seg_ref,2*pair+r,(1,256),1,kb*256); sk=seg_vec(seg_ref,2*pair+r,(1024,1),0,0)
    same=sk==sq
    dqs=[]; ks=[]; vs=[]
    for h in range(3):
        c=slice(64*h,64*h+64)
        q=q_ref[0,:,c]; k=k_ref[0,:,c]; do=dod[:,c]
        delta=jnp.sum(do.astype(F32)*o_ref[0,:,c],axis=1,keepdims=True)
        delta=jnp.broadcast_to(delta,(256,128)).T[0:1,:]
        st=jnp.where(same,dot_nt(k,q)-lse_ref[0,0,h:h+1,:],-1e30)
        p=jnp.exp(st)
        dp=dot_nt(v_ref[0,:,c],do)
        ds=(p*(dp-delta)).astype(BF)
        vs.append(dot(p.astype(BF),do)); ks.append(dot(ds,q)); dqs.append(dot_tn(ds,k))
    dks[...]+=jnp.concatenate(ks,axis=1); dvs[...]+=jnp.concatenate(vs,axis=1)
    dq_ref[0]=jnp.concatenate(dqs,axis=1).astype(BF)
    @pl.when(kb==3)
    def _():
        dk_ref[0]=dks[...].astype(BF); dv_ref[0]=dvs[...].astype(BF)

def attn_bwd(r,idx,ends,q,k,v,o,dos,lse,deps=()):
    pairs=ends.shape[0]//2
    blk=pl.BlockSpec((1,256,LW),lambda p,b,i,s:(2*p+r,b,0)); full=pl.BlockSpec((1,1024,LW),lambda p,b,i,s:(2*p+r,0,0))
    out=pl.BlockSpec((1,256,LW),lambda p,b,i,s:(p,b,0)); outs=pl.BlockSpec((1,1024,LW),lambda p,b,i,s:(p,0,0))
    return pl.pallas_call(skip(lambda *refs: attn_bwd_kernel(r,*refs),11,len(deps)),
        grid_spec=pltpu.PrefetchScalarGridSpec(num_scalar_prefetch=2,grid=(pairs,4),
        in_specs=[blk,full,full,blk]+[pl.BlockSpec((256,PW),lambda p,b,i,s:(p,0))]*4+[pl.BlockSpec((1,1,8,256),lambda p,b,i,s:(2*p+r,b,0,0))]+[ANY]*len(deps),
        out_specs=[out,outs,outs],scratch_shapes=[pltpu.VMEM((1024,LW),F32)]*2),
        out_shape=[jax.ShapeDtypeStruct((pairs,1024,LW),BF)]*3,
        cost_estimate=cost(60),
        compiler_params=pltpu.CompilerParams(vmem_limit_bytes=VM))(idx,ends,q,k,v,o,*dos,lse,*deps)

def pad3(a,b,c):
    z=jnp.zeros((a.shape[0],64),BF)
    return jnp.concatenate([a,z,b,z,c,z],axis=1)

def dmix_kernel(idx_ref,q0,k0,v0,q1,k1,v1,w_ref,sec_ref,f0,f1,f2,f3,stat_ref,gain_ref,keep_ref,send_ref,mom_ref):
    kb=pl.program_id(1)
    flat=lambda x: x[...].reshape(512,x.shape[-1])
    d=jnp.concatenate([pad3(q0[0],k0[0],v0[0]),pad3(q1[0],k1[0],v1[0])],axis=0)
    st=flat(stat_ref); mean=st[:,0:1]; rstd=st[:,1:2]
    mine=(kb==idx_ref[0]).astype(F32)
    m1=None
    for m,f in enumerate((f0,f1,f2,f3)):
        part=dot_nt(d,w_ref[m])[:,:LW]
        part=part+mine*sec_ref[m].reshape(512,LW)
        both=jnp.concatenate([part[:256],part[256:]],axis=1)
        if m%2: send_ref[m//2]=both.astype(BF)
        else: keep_ref[m//2]=both
        eg=part*gain_ref[m]
        f=f[...].astype(F32)
        xh=(jnp.concatenate([f[:,:LW],f[:,LW:]],axis=0)-mean)*rstd
        a=jnp.sum(eg,axis=1,keepdims=True); b=jnp.sum(eg*xh,axis=1,keepdims=True)
        m1=(a,b) if m1 is None else (m1[0]+a,m1[1]+b)
    lane=lax.broadcasted_iota(jnp.int32,(512,128),1)
    t=jnp.where(lane==0,m1[0],jnp.where(lane==1,m1[1],0.0)).T[0:8,:]
    mom_ref[0,0]=t[:,:256]; mom_ref[1,0]=t[:,256:]

def dmix(idx,heads,w,sec,fs,stat,gain,deps=()):
    pairs=heads[0].shape[0]; R=2*pairs
    blk=pl.BlockSpec((1,256,LW),lambda p,b,i:(p,b,0))
    full=lambda a: pl.BlockSpec(a.shape,lambda p,b,i:(0,)*a.ndim)
    pack=pl.BlockSpec((2,256,PW),lambda p,b,i:(0,4*p+b,0))
    return pl.pallas_call(skip(dmix_kernel,15,len(deps)),
        grid_spec=pltpu.PrefetchScalarGridSpec(num_scalar_prefetch=1,grid=(pairs,4),
        in_specs=[blk]*6+[full(w),pl.BlockSpec((4,2,256,LW),lambda p,b,i:(0,p,0,0))]+[pl.BlockSpec((256,PW),lambda p,b,i:(4*p+b,0))]*4
            +[pl.BlockSpec((2,256,128),lambda p,b,i:(p,b,0)),full(gain)]+[ANY]*len(deps),
        out_specs=[pack,pack,pl.BlockSpec((2,1,8,256),lambda p,b,i:(p,b,0,0))]),
        out_shape=[jax.ShapeDtypeStruct((2,pairs*1024,PW),F32),jax.ShapeDtypeStruct((2,pairs*1024,PW),BF),jax.ShapeDtypeStruct((R,4,8,256),F32)],
        cost_estimate=cost(0.1),
        compiler_params=pltpu.CompilerParams(vmem_limit_bytes=VM))(idx,*heads,w,sec,*fs,stat,gain,*deps)

def qkvw_kernel(q0,k0,v0,q1,k1,v1,ml_ref,out_ref,bias_ref,acc):
    i=pl.program_id(0)*2+pl.program_id(1)
    @pl.when(i==0)
    def _(): acc[...]=jnp.zeros_like(acc); bias_ref[...]=jnp.zeros_like(bias_ref)
    d=jnp.concatenate([pad3(q0[0],k0[0],v0[0]),pad3(q1[0],k1[0],v1[0])],axis=0)
    dt=d.T
    bias_ref[...]+=jnp.broadcast_to(jnp.sum(d.astype(F32),axis=0,keepdims=True),bias_ref.shape)
    pad=jnp.zeros((d.shape[0],64),BF)
    for m in range(4):
        acc[m]+=dot(dt,jnp.concatenate([ml_ref[m].reshape(d.shape[0],LW),pad],axis=1))
    @pl.when(i==2*pl.num_programs(0)-1)
    def _():
        for t in range(3):
            out_ref[t]=jnp.concatenate([acc[m,256*t:256*t+192,:LW] for m in range(4)],axis=1).astype(BF)

def qkvw(heads,ml,deps=()):
    pairs=heads[0].shape[0]
    row=pl.BlockSpec((1,512,LW),lambda p,i:(p,i,0))
    return pl.pallas_call(skip(qkvw_kernel,7,len(deps)),grid=(pairs,2),
        in_specs=[row]*6+[pl.BlockSpec((4,2,512,LW),lambda p,i:(0,p,i,0))]+[ANY]*len(deps),
        out_specs=[pl.BlockSpec((3,LW,768),lambda p,i:(0,0,0)),pl.BlockSpec((8,768),lambda p,i:(0,0))],
        out_shape=[jax.ShapeDtypeStruct((3,LW,768),BF),jax.ShapeDtypeStruct((8,768),F32)],
        scratch_shapes=[pltpu.VMEM((4,768,256),F32)],
        cost_estimate=cost(8),
        compiler_params=pltpu.CompilerParams(vmem_limit_bytes=VM))(*heads,ml,*deps)


def row_sum(x):
    return jnp.sum(x, axis=0, keepdims=True)


def norm_parts(x):
    c = x - jnp.mean(x, axis=1, keepdims=True)
    rstd = lax.rsqrt(jnp.mean(c * c, axis=1, keepdims=True) + 1e-5)
    return c * rstd, rstd


def norm_back(e, xhat, rstd, gain):
    eg = e * gain
    return rstd * (eg - jnp.mean(eg, axis=1, keepdims=True) - xhat * jnp.mean(eg * xhat, axis=1, keepdims=True))


def in_order(blocks, index):
    low = (index & 1) != 0
    high = (index & 2) != 0
    b = [jnp.where(low, blocks[m ^ 1], blocks[m]) for m in range(4)]
    return jnp.concatenate([jnp.where(high, b[m ^ 2], b[m]) for m in range(4)], axis=1)


def half(r):
    return slice(LW * (r % 2), LW * (r % 2) + LW)


def ff_kernel(
    idx_ref, f0, f1, f2, f3, a0, a1, a2, a3, og_ref, pw_ref, iw_ref, ow_ref, ib_ref, vec_ref,
    out_ref, act_ref, din_ref, ml_ref, do_ref, dp_ref, att_ref, datt_ref, sec_ref, sums_ref, ibg_ref,
    mid, xh2, rs2, acc, slopes,
):
    i = pl.program_id(0)
    index = idx_ref[0]
    R = 2 * f0.shape[0]
    M = R * 256
    pos_gain, pos_shift, proj_bias, gain2, shift2, outer_bias, gain3, shift3 = [vec_ref[j : j + 1, :] for j in range(8)]

    @pl.when(i == 0)
    def _():
        for r in range(R):
            rows = pl.ds(256 * r, 256)
            xhat, _ = norm_parts(in_order([f[r // 2, 0].astype(F32)[:, half(r)] for f in (f0, f1, f2, f3)], index))
            att_ref[rows] = in_order([a[pl.ds(256 * (r // 2), 256)].astype(F32)[:, half(r)] for a in (a0, a1, a2, a3)], index).astype(BF)
            second = xhat * pos_gain + pos_shift + dot(att_ref[rows], pw_ref[...]) + proj_bias
            xhat, rstd = norm_parts(second)
            xh2[rows] = xhat
            rs2[rows] = jnp.broadcast_to(rstd, (256, 128))
            middle = xhat * gain2 + shift2
            mid[rows] = middle
            ml_ref[rows] = middle.astype(BF)
        acc[...] = jnp.zeros_like(acc)

    @pl.when(i < 4)
    def _():
        for r in range(R):
            rows = pl.ds(256 * r, 256)
            inner = dot(ml_ref[rows], iw_ref[...]) + ib_ref[0]
            phi = erf_gelu_parts(inner)
            slopes[i, rows] = (phi + inner * (jnp.exp(-0.5 * inner * inner) * 0.3989422804014327)).astype(BF)
            act_ref[rows] = (inner * phi).astype(BF)
            acc[rows] += dot(act_ref[rows], ow_ref[...])

    @pl.when(i == 3)
    def _():
        g1 = g2 = g3 = jnp.zeros((1, 768), F32)
        for r in range(R):
            rows = pl.ds(256 * r, 256)
            xhat, rstd = norm_parts(mid[rows] + acc[rows] + outer_bias)
            out_ref[rows] = (xhat * gain3 + shift3).astype(BF)
            e = og_ref[rows].astype(F32)
            d = norm_back(e, xhat, rstd, gain3)
            low = d.astype(BF)
            do_ref[rows] = low
            mid[rows] = d
            g1, g2, g3 = g1 + row_sum(e * xhat), g2 + row_sum(e), g3 + row_sum(low.astype(F32))
        sums_ref[0:1] = g1
        sums_ref[1:2] = g2
        sums_ref[2:3] = g3
        sums_ref[3:8] = jnp.zeros((5, 768), F32)

    @pl.when(i >= 4)
    def _():
        g = jnp.zeros((1, 768), F32)
        for r in range(R):
            rows = pl.ds(256 * r, 256)
            d = dot_nt(do_ref[rows], ow_ref[...]) * slopes[7 - i, rows].astype(F32)
            low = d.astype(BF)
            din_ref[rows] = low
            g = g + row_sum(low.astype(F32))
            mid[rows] += dot_nt(low, iw_ref[...])
        ibg_ref[0] = g

    @pl.when(i == 7)
    def _():
        g1 = g2 = g3 = jnp.zeros((1, 768), F32)
        for r in range(R):
            rows = pl.ds(256 * r, 256)
            e = mid[rows]
            xhat = xh2[rows]
            d = norm_back(e, xhat, rs2[rows, 0:1], gain2)
            low = d.astype(BF)
            dp_ref[rows] = low
            datt = dot_nt(low, pw_ref[...]).astype(BF)
            for b in range(4):
                datt_ref[index ^ b, pl.ds(256 * (r // 2), 256), half(r)] = datt[:, LW * b : LW * b + LW]
                sec_ref[index ^ b, r] = d[:, LW * b : LW * b + LW]
            g1, g2, g3 = g1 + row_sum(e * xhat), g2 + row_sum(e), g3 + row_sum(low.astype(F32))
        sums_ref[3:4] = g1
        sums_ref[4:5] = g2
        sums_ref[5:6] = g3


def ff(idx, firsts, atts, out_grad, pw, iw, ow, ib, vec):
    pairs = atts[0].shape[0] // 256
    R = 2 * pairs
    M = R * 256
    chunk = lambda i: jnp.where(i < 4, i, 7 - i)
    whole = lambda *s: pl.BlockSpec(s, lambda i, x: (0,) * len(s))
    return pl.pallas_call(
        ff_kernel,
        grid_spec=pltpu.PrefetchScalarGridSpec(
            num_scalar_prefetch=1,
            grid=(8,),
            in_specs=[pl.BlockSpec((pairs, 1, 256, PW), lambda i, x: (0, x[0], 0, 0))] * 4
            + [whole(pairs * 256, PW)] * 4
            + [
                whole(M, 768),
                whole(768, 768),
                pl.BlockSpec((768, 768), lambda i, x: (0, chunk(i))),
                pl.BlockSpec((768, 768), lambda i, x: (chunk(i), 0)),
                pl.BlockSpec((1, 1, 768), lambda i, x: (chunk(i), 0, 0)),
                whole(8, 768),
            ],
            out_specs=[
                whole(M, 768),
                pl.BlockSpec((M, 768), lambda i, x: (0, jnp.minimum(i, 3))),
                pl.BlockSpec((M, 768), lambda i, x: (0, jnp.minimum(7 - i, 3))),
            ]
            + [whole(M, 768)] * 4
            + [
                whole(4, pairs * 256, PW),
                whole(4, R, 256, LW),
                whole(8, 768),
                pl.BlockSpec((1, 1, 768), lambda i, x: (jnp.minimum(7 - i, 3), 0, 0)),
            ],
            scratch_shapes=[
                pltpu.VMEM((M, 768), F32),
                pltpu.VMEM((M, 768), F32),
                pltpu.VMEM((M, 128), F32),
                pltpu.VMEM((M, 768), F32),
                pltpu.VMEM((4, M, 768), BF),
            ],
        ),
        out_shape=[
            jax.ShapeDtypeStruct((M, 768), BF),
            jax.ShapeDtypeStruct((M, 3072), BF),
            jax.ShapeDtypeStruct((M, 3072), BF),
        ]
        + [jax.ShapeDtypeStruct((M, 768), BF)] * 4
        + [
            jax.ShapeDtypeStruct((4, pairs * 256, PW), BF),
            jax.ShapeDtypeStruct((4, R, 256, LW), F32),
            jax.ShapeDtypeStruct((8, 768), F32),
            jax.ShapeDtypeStruct((4, 1, 768), F32),
        ],
        cost_estimate=cost(40),
        compiler_params=pltpu.CompilerParams(vmem_limit_bytes=VM),
    )(idx, *[f.reshape(pairs, 4, 256, PW) for f in firsts], *atts, out_grad, pw, iw, ow, ib, vec)


def put(index, keep, send, b, rows, value):
    m = index ^ b

    @pl.when((m & 1) == 0)
    def _():
        keep[m >> 1, rows] = value

    @pl.when((m & 1) == 1)
    def _():
        send[m >> 1, rows] = value


def outer_kernel(idx_ref, act_ref, do_ref, sums_ref, ibg_ref, keep_ref, send_ref):
    c = pl.program_id(0)
    index = idx_ref[0]
    outer = dot_tn(do_ref[...], act_ref[...]).astype(BF)
    for b in range(4):
        put(index, keep_ref, send_ref, b, pl.ds(pl.multiple_of(LW * c, LW), LW), outer[LW * b : LW * b + LW])

    @pl.when(c == 0)
    def _():
        for b in range(4):
            small = jnp.concatenate([sums_ref[:, LW * b : LW * b + LW], jnp.zeros((8, 576), F32)], axis=1)
            small = jnp.concatenate([small, ibg_ref[b], jnp.zeros((7, 768), F32)], axis=0)
            put(index, keep_ref, send_ref, b, pl.ds(768, 16), small.astype(BF))
            put(index, keep_ref, send_ref, b, pl.ds(784, 48), jnp.zeros((48, 768), BF))


def inner_kernel(idx_ref, din_ref, ml_ref, dp_ref, att_ref, keep_ref, send_ref):
    c = pl.program_id(0)
    index = idx_ref[0]
    put(index, keep_ref, send_ref, c, pl.ds(0, 768), dot_tn(ml_ref[...], din_ref[...]).astype(BF))

    @pl.when(c == 0)
    def _():
        proj = dot_tn(dp_ref[...], att_ref[...]).astype(BF)
        for b in range(4):
            put(index, keep_ref, send_ref, b, pl.ds(768, LW), proj[LW * b : LW * b + LW])


def weight_grads(kernel, rows, idx, wide, others, deps=()):
    M = wide.shape[0]
    whole = lambda a: pl.BlockSpec(a.shape, lambda i, x: (0,) * a.ndim)
    out = pl.BlockSpec((2, rows, 768), lambda i, x: (0, 0, 0))
    return pl.pallas_call(
        skip(kernel, 2 + len(others), len(deps)),
        grid_spec=pltpu.PrefetchScalarGridSpec(
            num_scalar_prefetch=1,
            grid=(4,),
            in_specs=[pl.BlockSpec((M, 768), lambda i, x: (0, i))] + [whole(a) for a in others] + [ANY] * len(deps),
            out_specs=[out, out],
        ),
        out_shape=[jax.ShapeDtypeStruct((2, rows, 768), BF)] * 2,
        cost_estimate=cost(8),
        compiler_params=pltpu.CompilerParams(vmem_limit_bytes=VM),
    )(idx, wide, *others, *deps)


def far_kernel(keep_ref, got_ref, out_ref):
    out_ref[...] = (keep_ref[0].astype(F32) + got_ref[0].astype(F32)).astype(BF)


def far_sum(keep, got, deps=()):
    n = keep.shape[1]
    block = pl.BlockSpec((1, n // 2, 768), lambda i: (1, i, 0))
    return pl.pallas_call(
        skip(far_kernel, 2, len(deps)),
        grid=(2,),
        in_specs=[block] * 2 + [ANY] * len(deps),
        out_specs=pl.BlockSpec((n // 2, 768), lambda i: (i, 0)),
        out_shape=jax.ShapeDtypeStruct((n, 768), BF),
        cost_estimate=cost(1),
        compiler_params=pltpu.CompilerParams(vmem_limit_bytes=VM),
    )(keep, got, *deps)


def own_kernel(keep_ref, got_ref, far_ref, out_ref):
    x = keep_ref[0].astype(F32) + got_ref[0].astype(F32) + far_ref[...].astype(F32)
    out_ref[...] = x.astype(BF).reshape(out_ref.shape)


def own_sum(keep, got, far, deps=()):
    n = keep.shape[1]
    block = pl.BlockSpec((1, n // 2, 768), lambda i: (0, i, 0))
    one = pl.BlockSpec((n // 2, 768), lambda i: (i, 0))
    return pl.pallas_call(
        skip(own_kernel, 3, len(deps)),
        grid=(2,),
        in_specs=[block] * 2 + [one] + [ANY] * len(deps),
        out_specs=one,
        out_shape=jax.ShapeDtypeStruct((n, 768), BF),
        cost_estimate=cost(1),
        compiler_params=pltpu.CompilerParams(vmem_limit_bytes=VM),
    )(keep, got, far, *deps)


def finish_kernel(in_ref, outer_ref, small_ref):
    for i in range(4):
        outer_ref[:, 768 * i : 768 * i + 768] = in_ref[LW * i : LW * i + LW].astype(F32)
    small_ref[...] = in_ref[768:784].astype(F32)


def finish(grads, deps=()):
    whole = lambda *s: pl.BlockSpec(s, lambda: (0, 0))
    shapes = (LW, 3072), (16, 768)
    return pl.pallas_call(
        skip(finish_kernel, 1, len(deps)),
        in_specs=[whole(832, 768)] + [ANY] * len(deps),
        out_specs=[whole(*s) for s in shapes],
        out_shape=[jax.ShapeDtypeStruct(s, F32) for s in shapes],
        cost_estimate=cost(6),
        compiler_params=pltpu.CompilerParams(vmem_limit_bytes=VM),
    )(grads, *deps)


def widen_kernel(in_ref, inner_ref, proj_ref):
    inner_ref[...] = in_ref[:768].astype(F32)
    proj_ref[...] = in_ref[768:].astype(F32)


def widen(x, deps=()):
    whole = lambda *s: pl.BlockSpec(s, lambda: (0, 0))
    shapes = (768, 768), (LW, 768)
    return pl.pallas_call(
        skip(widen_kernel, 1, len(deps)),
        in_specs=[whole(960, 768)] + [ANY] * len(deps),
        out_specs=[whole(*s) for s in shapes],
        out_shape=[jax.ShapeDtypeStruct(s, F32) for s in shapes],
        cost_estimate=cost(3),
        compiler_params=pltpu.CompilerParams(vmem_limit_bytes=VM),
    )(x, *deps)


def taps_kernel(own_ref, scale_ref, dir_ref, out_ref, square_ref, tmp):
    n = dir_ref.shape[0]
    at = pl.program_id(0) * n
    side = own_ref[0] // 2
    for k in range(n):
        x = dir_ref[k].astype(F32)
        total = jnp.sum(jnp.sum(x * x, axis=0, keepdims=True), axis=1, keepdims=True)
        square_ref[k : k + 1] = jnp.broadcast_to(total, (1, 128))
        x = jnp.where(side != 0, x[:, PW:], x[:, :PW])
        tmp[48 * k : 48 * k + 48] = (x * (scale_ref[at + k] * lax.rsqrt(total))).astype(BF)
    out_ref[...] = dot(tmp[...], own_pick(own_ref[0]))[:, :LW].astype(BF)


def own_pick(index):
    row = lax.broadcasted_iota(jnp.int32, (PW, 256), 0)
    lane = lax.broadcasted_iota(jnp.int32, (PW, 256), 1)
    return ((row == lane + LW * (index & 1)) & (lane < LW)).astype(F32).astype(BF)


def own_taps(idx, scale, tap_dir):
    return pl.pallas_call(
        taps_kernel,
        grid_spec=pltpu.PrefetchScalarGridSpec(
            num_scalar_prefetch=2,
            grid=(8,),
            in_specs=[pl.BlockSpec((16, 48, 768), lambda i, x, c: (i, 0, 0))],
            out_specs=[pl.BlockSpec((768, LW), lambda i, x, c: (i, 0)), pl.BlockSpec((16, 128), lambda i, x, c: (i, 0))],
            scratch_shapes=[pltpu.VMEM((768, PW), BF)],
        ),
        out_shape=[jax.ShapeDtypeStruct((6144, LW), BF), jax.ShapeDtypeStruct((128, 128), F32)],
        cost_estimate=cost(10),
        compiler_params=pltpu.CompilerParams(vmem_limit_bytes=VM),
    )(idx, scale, tap_dir)


def raw_kernel(own_ref, dir_ref, out_ref):
    out_ref[...] = dot(dir_ref[...], own_pick(own_ref[0]))[:, :LW].astype(BF)


def own_dirs(idx, tap_dir, deps=()):
    return pl.pallas_call(
        skip(raw_kernel, 2, len(deps)),
        grid_spec=pltpu.PrefetchScalarGridSpec(
            num_scalar_prefetch=1,
            grid=(4,),
            in_specs=[pl.BlockSpec((1536, PW), lambda i, x: (i, x[0] // 2))] + [ANY] * len(deps),
            out_specs=pl.BlockSpec((1536, LW), lambda i, x: (i, 0)),
        ),
        out_shape=jax.ShapeDtypeStruct((6144, LW), BF),
        cost_estimate=cost(5),
        compiler_params=pltpu.CompilerParams(vmem_limit_bytes=VM),
    )(idx, tap_dir.reshape(6144, 768), *deps)


def dots_kernel(tap_ref, dir_ref, out_ref):
    g = tap_ref[0].astype(F32).T
    p = g * dir_ref[...].astype(F32)
    rows = [jnp.sum(p[48 * t : 48 * t + 48], axis=0, keepdims=True) for t in range(16)]
    s = jnp.sum(jnp.concatenate(rows, axis=0), axis=1, keepdims=True)
    out_ref[0] = jnp.broadcast_to(s, (16, 128))


def tap_dots(tap, dirs, deps=()):
    return pl.pallas_call(
        skip(dots_kernel, 2, len(deps)),
        grid=(8,),
        in_specs=[pl.BlockSpec((1, LW, 768), lambda i: (i, 0, 0)), pl.BlockSpec((768, LW), lambda i: (i, 0))] + [ANY] * len(deps),
        out_specs=pl.BlockSpec((1, 16, 128), lambda i: (i, 0, 0)),
        out_shape=jax.ShapeDtypeStruct((8, 16, 128), F32),
        cost_estimate=cost(6),
        compiler_params=pltpu.CompilerParams(vmem_limit_bytes=VM),
    )(tap, dirs, *deps)


def last_kernel(left_ref, right_ref, dir_ref, coef_ref, beta_ref, out_ref, turned):
    i = pl.program_id(0)

    @pl.when(i == 0)
    def _():
        for J in range(8):
            for p, ref in enumerate((left_ref, right_ref)):
                t = ref[J].astype(F32).T
                at = 768 * J + 384 * p
                turned[0, at : at + 384] = t[:, :128]
                turned[1, at : at + 384, :64] = t[:, 128:]

    for c in range(8):
        at = pl.ds(8 * i + c, 128, stride=48)
        g = jnp.concatenate([turned[0, at].T, turned[1, at].T[:64]], axis=0)
        out_ref[c] = g * coef_ref[...] - dir_ref[c].astype(F32) * beta_ref[...]


def last_taps(coef, beta, left, right, dirs, deps=()):
    row = pl.BlockSpec((1, 128), lambda i: (0, 0))
    block = pl.BlockSpec((8, LW, 128), lambda i: (i, 0, 0))
    return pl.pallas_call(
        skip(last_kernel, 5, len(deps)),
        grid=(6,),
        in_specs=[pl.BlockSpec((8, LW, 384), lambda i: (0, 0, 0))] * 2 + [block, row, row] + [ANY] * len(deps),
        out_specs=block,
        out_shape=jax.ShapeDtypeStruct((48, LW, 128), F32),
        scratch_shapes=[pltpu.VMEM((2, 6144, 128), F32)],
        cost_estimate=cost(8),
        compiler_params=pltpu.CompilerParams(vmem_limit_bytes=VM),
    )(left, right, dirs, coef[None], beta[None], *deps)


def near_kernel(keep_ref, got_ref, mom_ref, mom_got, near_ref, far_ref, mom_out):
    N = keep_ref.shape[1]
    near_ref[...] = keep_ref[0] + got_ref[0].astype(F32)
    far_ref[:N] = (keep_ref[1] + got_ref[1].astype(F32)).astype(BF)
    mom = mom_ref[...] + mom_got[...]
    mom_out[...] = mom
    R = mom.shape[0]
    rows = jnp.concatenate([mom[r, k, 0:2] for r in range(R) for k in range(4)], axis=0)
    far_ref[N:] = jnp.concatenate([rows, jnp.zeros((8 * R, 128), F32)], axis=1).astype(BF)


def near_far(keep, got, moments, moments_got):
    N = keep.shape[1]
    R = moments.shape[0]
    whole = lambda a: pl.BlockSpec(a.shape, lambda: (0,) * a.ndim)
    shapes = [
        jax.ShapeDtypeStruct((N, PW), F32),
        jax.ShapeDtypeStruct((N + 8 * R, PW), BF),
        jax.ShapeDtypeStruct(moments.shape, F32),
    ]
    return pl.pallas_call(
        near_kernel,
        in_specs=[whole(a) for a in (keep, got, moments, moments_got)],
        out_specs=[whole(a) for a in shapes],
        out_shape=shapes,
        cost_estimate=cost(2),
        compiler_params=pltpu.CompilerParams(vmem_limit_bytes=VM),
    )(keep, got, moments, moments_got)


HALF = 384


def pick_kernel(bits_ref, a_ref, b_ref, sa_ref, sb_ref):
    sa_ref[...] = a_ref[...]
    sb_ref[...] = b_ref[...]


def first_sends(bits, x, deps=()):
    L, N, _ = x.shape
    n = N // 4
    out = pl.BlockSpec((L, n, HALF), lambda i, s: (0, i, 0))
    return pl.pallas_call(
        skip(pick_kernel, 3, len(deps)),
        grid_spec=pltpu.PrefetchScalarGridSpec(
            num_scalar_prefetch=1,
            grid=(2,),
            in_specs=[
                pl.BlockSpec((L, n, HALF), lambda i, s: (0, 2 - 2 * s[0] + i, 0)),
                pl.BlockSpec((L, n, HALF), lambda i, s: (0, 2 - 2 * s[1] + i, 1)),
            ]
            + [ANY] * len(deps),
            out_specs=[out, out],
        ),
        out_shape=[jax.ShapeDtypeStruct((L, N // 2, HALF), BF)] * 2,
        cost_estimate=cost(3),
        compiler_params=pltpu.CompilerParams(vmem_limit_bytes=VM),
    )(bits, x, x, *deps)


def stage_kernel(last, steps, bits_ref, ka, kb, ra, rb, *outs):
    i = pl.program_id(0)
    for p, (k, r) in enumerate(((ka, ra), (kb, rb))):
        y = k[...].reshape(r.shape).astype(F32) + r[...].astype(F32)
        if last:
            outs[p][...] = y.astype(BF)
            continue
        sum_ref, send_ref = outs[p], outs[2 + p]
        h = y.shape[1] * steps // 2
        halves = ((i, y),) if steps == 2 else ((0, y[:, :h]), (1, y[:, h:]))
        for at, half in halves:
            sum_ref[:, 0 if steps == 2 else at] = half.astype(BF)

            @pl.when(bits_ref[2 + p] != at)
            def _():
                send_ref[...] = half.astype(BF)


def stage(bits, a, b, ra, rb, last, deps=()):
    L, n, _ = ra.shape
    h = n // 2
    steps = 2 if not last and h % 16 == 0 else 1
    m = n // steps
    if a.ndim == 3:
        keep = lambda p: pl.BlockSpec((L, m, HALF), lambda i, s: (0, steps * s[p] + i, p))
    else:
        keep = lambda p: pl.BlockSpec((L, 1, m, HALF), lambda i, s: (0, s[p], i, 0))
    row = pl.BlockSpec((L, m, HALF), lambda i, s: (0, i, 0))
    if last:
        out_specs, out_shape = [row] * 2, [jax.ShapeDtypeStruct((L, n, HALF), BF)] * 2
    else:
        out_specs = [pl.BlockSpec((L, 2 // steps, h, HALF), lambda i, s: (0, i, 0, 0))] * 2
        out_specs += [pl.BlockSpec((L, h, HALF), lambda i, s: (0, 0, 0))] * 2
        out_shape = [jax.ShapeDtypeStruct((L, 2, h, HALF), BF)] * 2 + [jax.ShapeDtypeStruct((L, h, HALF), BF)] * 2
    return pl.pallas_call(
        skip(lambda *refs: stage_kernel(last, steps, *refs), 5, len(deps)),
        grid_spec=pltpu.PrefetchScalarGridSpec(
            num_scalar_prefetch=1,
            grid=(steps,),
            in_specs=[keep(0), keep(1), row, row] + [ANY] * len(deps),
            out_specs=out_specs,
        ),
        out_shape=out_shape,
        cost_estimate=cost(3),
        compiler_params=pltpu.CompilerParams(vmem_limit_bytes=VM),
    )(bits, a, b, ra, rb, *deps)


def join_kernel(bits_ref, a, b, ra, rb, oa, ob):
    for p, (k, r, o) in enumerate(((a, ra, oa), (b, rb, ob))):
        on = bits_ref[p]
        o[on] = k[...]
        o[1 - on] = r[...]


def join(bits, a, b, ra, rb, deps=()):
    shape = a.shape
    block = pl.BlockSpec(shape, lambda i, s: (0,) * len(shape))
    out = pl.BlockSpec((2,) + shape, lambda i, s: (0,) * (len(shape) + 1))
    oa, ob = pl.pallas_call(
        skip(join_kernel, 5, len(deps)),
        grid_spec=pltpu.PrefetchScalarGridSpec(
            num_scalar_prefetch=1,
            grid=(1,),
            in_specs=[block] * 4 + [ANY] * len(deps),
            out_specs=[out] * 2,
        ),
        out_shape=[jax.ShapeDtypeStruct((2,) + shape, BF)] * 2,
        cost_estimate=cost(2),
        compiler_params=pltpu.CompilerParams(vmem_limit_bytes=VM),
    )(bits, a, b, ra, rb, *deps)
    flat = (2 * shape[0],) + shape[1:]
    return oa.reshape(flat), ob.reshape(flat)


class RowSum:
    def __init__(self, x, deps=()):
        n = lax.axis_size("rows")
        bits = [1 << i for i in range(n.bit_length() - 1)]
        self.orders = (bits, bits[1::-1] + bits[2:])
        self.count = x.shape[1]
        full = -(-self.count // (16 * n)) * (16 * n) if n > 8 else self.count
        if full != self.count:
            x = jnp.pad(x, ((0, 0), (0, full - self.count), (0, 0)))
        self.parts = [x, x]
        self.at = 0
        self.got = None
        self.steps = len(bits)
        self.sends = first_sends(self.bits(0), x, deps)

    def bits(self, s):
        place = lax.axis_index("rows")
        pick = lambda o, i: (place // o[min(i, self.steps - 1)]) % 2
        return jnp.stack([pick(o, i) for i in (s, s + 1) for o in self.orders]).astype(jnp.int32)

    def go(self):
        self.got = [swap(s, "rows", o[self.at]) for s, o in zip(self.sends, self.orders)]

    def step(self, *deps):
        if self.got is None:
            self.go()
        got, self.got = self.got, None
        last = self.at == self.steps - 1
        outs = stage(self.bits(self.at), *self.parts, *got, last, deps)
        self.parts, self.sends = outs[:2], outs[2:]
        self.at += 1
        return self.parts[0]

    def back(self, *deps):
        self.at -= 1
        got = [swap(p, "rows", o[self.at]) for p, o in zip(self.parts, self.orders)]
        self.parts = join(self.bits(self.at), *self.parts, *got, deps)
        return self.parts[0]

    def result(self):
        return [p.reshape(-1, HALF)[: self.count] for p in self.parts]


def swap(x, axis, bit):
    return lax.ppermute(x, axis, [(i, i ^ bit) for i in range(lax.axis_size(axis))])


def gather_seq(x):
    far = swap(x, "seq", 2)
    near = swap(x, "seq", 1)
    return [x, near, far, swap(far, "seq", 1)]


def trade(blocks):
    return [blocks[0], swap(blocks[1], "seq", 1), swap(blocks[2], "seq", 2), swap(blocks[3], "seq", 3)]


def all_sum(x, axis):
    for i in range(lax.axis_size(axis).bit_length() - 1):
        x = x + swap(x, axis, 1 << i)
    return x


def assemble(blocks, index):
    low = (index & 1) != 0
    high = (index & 2) != 0
    b = [jnp.where(low, blocks[m ^ 1], blocks[m]) for m in range(4)]
    return [jnp.where(high, b[m ^ 2], b[m]) for m in range(4)]


def cut(x, start, size, axis):
    return lax.dynamic_slice_in_dim(x, start, size, axis)


def local(
    frames,
    utterance_lengths,
    tap_dir,
    tap_scale,
    conv_bias,
    pos_gain,
    pos_shift,
    query_weight,
    query_bias,
    key_weight,
    value_weight,
    value_bias,
    proj_weight,
    proj_bias,
    attend_gain,
    attend_shift,
    inner_weight,
    inner_bias,
    outer_weight,
    outer_bias,
    final_gain,
    final_shift,
    out_grad,
):
    R = frames.shape[0]
    index = lax.axis_index("seq")
    idx = jnp.full((1,), index, jnp.int32)
    ends = utterance_lengths
    order = [index ^ m for m in range(4)]
    own = index * LW

    def packed(x):
        return jnp.concatenate([x[0::2], x[1::2]], axis=2).reshape(R * 128, PW)

    sent = trade([packed(cut(frames, b * LW, LW, 2)) for b in order])
    taps, squares = own_taps(idx, tap_scale, tap_dir)
    w = build_w(taps)
    bias4 = jnp.tile(cut(conv_bias, own, LW, 0).reshape(4, 1, 48), (1, 4, 1)).reshape(4, 1, LW)
    first, pre, xs = conv_fwd(ends, idx, sent, w, bias4)
    firsts = gather_seq(first)

    def xor_rows(a):
        return jnp.stack([cut(a, b * LW, LW, 0) for b in order])

    def pad_to(a, axis, size):
        widths = [(0, 0)] * a.ndim
        widths[axis] = (0, size - a.shape[axis])
        return jnp.pad(a, widths)

    own_cols = [
        pad_to(cut(a, own, LW, 1), 1, 256)
        for a in (query_weight * jnp.asarray(0.125, BF), key_weight, value_weight)
    ]
    w_qkv = pad_to(xor_rows(jnp.concatenate(own_cols, axis=1)), 1, 256)
    b_qkv = jnp.concatenate(
        [
            pad_to(cut(query_bias, own, LW, 0) * 0.125, 0, 512),
            pad_to(cut(value_bias, own, LW, 0), 0, 256),
        ]
    )[None]
    gain_x = xor_rows(pos_gain)[:, None]
    shift_x = xor_rows(pos_shift)[:, None]
    q, k, v, mixed_low, stat = qkv(firsts, w_qkv, b_qkv, gain_x, shift_x)
    att, att_full, lse = attn(idx, ends, q, k, v)
    att_blocks = trade([att[m] for m in range(4)])

    vecs = jnp.stack([pos_gain, pos_shift, proj_bias, attend_gain, attend_shift, outer_bias, final_gain, final_shift])
    layer_out, act, d_inner, middle_low, d_outer, d_proj, attended, d_att, second_x, sums, inner_sums = ff(
        idx, firsts, att_blocks, out_grad.reshape(R * 256, 768), proj_weight, inner_weight, outer_weight,
        inner_bias.reshape(4, 1, 768), vecs,
    )
    dos = trade_out(d_att)
    keep_out, send_out = weight_grads(outer_kernel, 832, idx, act, (d_outer, sums, inner_sums))
    got_out = swap(send_out, "seq", 1)
    keep_in, send_in = weight_grads(inner_kernel, 960, idx, d_inner, (middle_low, d_proj, attended), (send_out,))
    far = far_sum(keep_out, got_out, (send_in,))
    got_in = swap(send_in, "seq", 1)

    heads = attn_bwd(0, idx, ends, q, k, v, att_full, dos, lse, (far,))
    heads += attn_bwd(1, idx, ends, q, k, v, att_full, dos, lse, (heads[0],))
    grads = own_sum(keep_out, got_out, swap(far, "seq", 2), (heads[3],))
    keep, send, moments = dmix(idx, heads, w_qkv, second_x, firsts, stat, gain_x, (grads,))
    grads_out = lax.psum(grads, "rows")
    e_near, e_far, moments = near_far(keep, swap(send, "seq", 1), moments, swap(moments, "seq", 1))
    g_qkv, b_grads = qkvw(heads, mixed_low, (e_far,))
    e_sent = e_far
    e_far = swap(e_far, "seq", 2)
    far = swap(far_sum(keep_in, got_in, (e_sent, g_qkv)), "seq", 2)
    moments = moments.reshape(R * 4, 8, 256)

    tap_part, ds, d4, conv_b, vec = tap_grads(
        ends, e_near, e_far, first, stat.reshape(R * 1024, 128), moments, cut(pos_gain, own, LW, 0)[None], pre, xs, g_qkv,
    )
    if R > 2:
        tap_part = jnp.sum(tap_part.astype(F32), axis=0, keepdims=True).astype(BF)
    tap_part = tap_part[0]
    tap_sum = RowSum(tap_part.reshape(1, 11 * LW, 768))
    part = conv_back(0, ends, idx, ds, d4, w, None, tuple(tap_sum.sends))
    dir_own = own_dirs(idx, tap_dir, (part,))
    dir_turned = jnp.transpose(dir_own.reshape(128, 48, LW), (1, 2, 0))
    tap_sum.step(part)
    grads_in = lax.psum(own_sum(keep_in, got_in, far, (part, grads_out)), "rows")
    back = conv_back(2, ends, idx, ds, d4, w, part, tuple(tap_sum.sends))
    tap_sum.step(back)
    dots = tap_dots(tap_part, dir_own, tuple(tap_sum.sends))
    tap_sum.step(dots)
    dots = all_sum(dots[:, :, 0], "seq")
    back = trade_out(back)
    back = jnp.concatenate([b.reshape(R // 2, 1, 256, PW) for b in assemble(back, index)], axis=1)
    back = back.reshape(R // 2, 4, 256, 2, LW)
    frames_grad = jnp.transpose(back, (0, 3, 2, 1, 4)).reshape(R, 256, 768)
    while tap_sum.at:
        tap_sum.back()
    tap_left, tap_right = [p.reshape(11, LW, HALF) for p in tap_sum.result()]
    qkv_std = assemble([x[8:11, :, LW * m : LW * m + LW] for x in (tap_left, tap_right) for m in range(2)], index)
    t_qkv = jnp.concatenate(qkv_std, axis=2).astype(F32)
    t_outer, small = finish(grads_out, (tap_sum.parts[0],))
    lates = jnp.concatenate(
        [
            jnp.sum(conv_b, axis=(0, 2)).reshape(4, 4, 48).sum(1).reshape(LW),
            jnp.sum(vec[:, 0], axis=0),
            jnp.sum(vec[:, 1], axis=0),
            b_grads[0, 0:LW] * 0.125,
            b_grads[0, 512 : 512 + LW],
            dots.reshape(128),
            jnp.zeros((2048 - 1088,), F32),
        ]
    )
    lates = all_sum(lates.reshape(16, 128), "rows").reshape(2048)
    dots = lates[5 * LW : 5 * LW + 128]
    inverse = lax.rsqrt(squares[:, 0])
    coef = tap_scale * inverse
    turned = last_taps(coef, coef * dots * inverse * inverse, tap_left, tap_right, dir_turned, (frames_grad, t_outer))
    g_tap_dir = jnp.transpose(turned, (2, 0, 1))
    t_inner, t_proj = widen(grads_in, (turned,))
    g_tap_scale = cut(dots * inverse, index * 32, 32, 0)

    return (
        layer_out.reshape(R, 256, 768),
        frames_grad,
        g_tap_dir,
        g_tap_scale,
        lates[0:LW],
        lates[LW : 2 * LW],
        lates[2 * LW : 3 * LW],
        t_qkv[0].T * 0.125,
        lates[3 * LW : 4 * LW],
        t_qkv[1].T,
        t_qkv[2].T,
        lates[4 * LW : 5 * LW],
        t_proj.T,
        small[5, :LW],
        small[3, :LW],
        small[4, :LW],
        t_inner,
        small[8],
        t_outer.T,
        small[2, :LW],
        small[0, :LW],
        small[1, :LW],
    )


def trade_out(x):
    return trade([x[m] for m in range(4)])


def solution(mesh):
    split = P("rows", "seq", None)
    col = P(None, "seq")
    one = P("seq")
    return jax.shard_map(
        local,
        mesh=mesh,
        in_specs=(split, P("rows", None)) + (P(),) * 20 + (split,),
        out_specs=(split, split, P(None, None, "seq"), one, one, one, one)
        + (col, one, col, col, one, col, one, one, one, col, one, col, one, one, one),
        check_vma=False,
    )
```

```python
import jax, jax.numpy as jnp
from jax import lax
from jax.sharding import PartitionSpec as P
from jax.experimental import pallas as pl
from jax.experimental.pallas import tpu as pltpu
F32=jnp.float32; BF=jnp.bfloat16
CH=48; PH=4; LW=PH*CH
NJ=33; SEGL=48; XROWS=(SEGL+NJ-1)*16; MROWS=SEGL*16
VM=60*1024*1024

def cost(us):
    return pl.CostEstimate(flops=int(us*1.0e9),bytes_accessed=int(us*3.0e6),transcendentals=0)

ANY=pl.BlockSpec(memory_space=pl.ANY)
PW=2*LW

def skip(kernel,at,count):
    if not count:
        return kernel
    return lambda *refs: kernel(*refs[:at],*refs[at+count:])

def dot(a,b): return jnp.dot(a,b,preferred_element_type=F32)
def dot_nt(a,b): return lax.dot_general(a,b,(((1,),(1,)),((),())),preferred_element_type=F32)
def dot_tn(a,b): return lax.dot_general(a,b,(((0,),(0,)),((),())),preferred_element_type=F32)

def erf_gelu_parts(v):
    phi=0.5*(1.0+lax.erf(v*0.7071067811865476))
    return phi

WROWS=6400
def build_w_kernel(t_ref, w_ref, tp, rs):
    g=pl.program_id(0)
    rows=t_ref.shape[0]
    @pl.when(g==0)
    def _():
        tp[0:144,:]=jnp.zeros((144,LW),BF)
        tp[144:144+rows,:]=t_ref[...]
        tp[144+rows:,:]=jnp.zeros((256,LW),BF)
    src=lax.broadcasted_iota(jnp.int32,(LW,256),0); l=lax.broadcasted_iota(jnp.int32,(LW,256),1)
    pick=((src==48*g+lax.rem(l,48))&(l<LW)).astype(F32).astype(BF)
    n=1600
    lane=lax.broadcasted_iota(jnp.int32,(n,256),1)
    for i in range(WROWS//n):
        r0=i*n
        R=dot(tp[r0:r0+n+144,:],pick).astype(BF)
        lo=jnp.where(lane[:,:128]<96,jnp.where(lane[:,:128]<48,R[144:144+n,:128],R[96:96+n,:128]),R[48:48+n,:128])
        hi=jnp.where(lane[:,128:]<144,R[48:48+n,128:],R[0:n,128:])
        w_ref[0,r0:r0+n,:128]=lo
        w_ref[0,r0:r0+n,128:]=hi

def build_w(taps2):
    rows=taps2.shape[0]
    return pl.pallas_call(build_w_kernel,grid=(4,),
        in_specs=[pl.BlockSpec((rows,LW),lambda g:(0,0))],
        out_specs=pl.BlockSpec((1,WROWS,256),lambda g:(g,0,0)),
        out_shape=jax.ShapeDtypeStruct((4,WROWS,256),BF),
        scratch_shapes=[pltpu.VMEM((rows+144+256,LW),BF),pltpu.VMEM((16,256),BF)],
        cost_estimate=cost(10),
        compiler_params=pltpu.CompilerParams(vmem_limit_bytes=VM))(taps2)

def sload(ref,start,n,stride):
    return jnp.concatenate([ref[0,pl.ds(start,n,stride=stride),:],ref[1,pl.ds(start,n,stride=stride),:]],axis=1)[:,:LW]
def sstore(ref,start,n,stride,v):
    ref[0,pl.ds(start,n,stride=stride),:]=v[:,:128]
    ref[1,pl.ds(start,n,stride=stride),:]=jnp.concatenate([v[:,128:],jnp.zeros((n,64),v.dtype)],axis=1)
def fload(ref,start,n):
    return jnp.concatenate([ref[0,pl.ds(start,n),:],ref[1,pl.ds(start,n),:]],axis=1)[:,:LW]
def fstore(ref,start,n,v):
    ref[0,pl.ds(start,n),:]=v[:,:128]
    ref[1,pl.ds(start,n),:]=jnp.concatenate([v[:,128:],jnp.zeros((n,64),v.dtype)],axis=1)

def pick_matrix(g,a):
    ch=lax.broadcasted_iota(jnp.int32,(LW,256),0); l=lax.broadcasted_iota(jnp.int32,(LW,256),1)
    return ((ch==48*g+(l-48*a))&(l>=48*a)&(l<48*a+48)).astype(F32).astype(BF)

def pick_back(g,a):
    l=lax.broadcasted_iota(jnp.int32,(LW,256),0); ch=lax.broadcasted_iota(jnp.int32,(LW,256),1)
    return ((ch==48*g+(l-48*a))&(l>=48*a)&(l<48*a+48)).astype(F32).astype(BF)

def fill_ids(seg_ref,pair,sid):
    sub=lax.broadcasted_iota(jnp.int32,(256,LW),0); l=lax.broadcasted_iota(jnp.int32,(256,LW),1)
    t=4*sub+(l>=48).astype(jnp.int32)+(l>=96).astype(jnp.int32)+(l>=144).astype(jnp.int32)
    for r in range(2):
        v=jnp.zeros((256,LW),jnp.int32)
        end=0
        for q in range(7):
            end=end+seg_ref[pair*2+r,q]
            v=v+(t>=end).astype(jnp.int32)
        sid[pl.ds(256*r,256),:]=v

TAIL=48
def respace(sid,src,xr,xsf):
    xsf[0,1280:1280+TAIL,:]=jnp.zeros((TAIL,128),F32); xsf[1,1280:1280+TAIL,:]=jnp.zeros((TAIL,128),F32)
    for r in range(2):
        for B in range(26):
            v=jnp.zeros((16,LW),F32)
            for q in range(8):
                bb=B-1-q
                if 0<=bb<16:
                    rows=pl.ds(r*256+16*bb,16)
                    v=jnp.where(sid[rows,:]==q,src[rows,:],v)
            xr[r,pl.ds(16*B,16),:]=v
        for sp in range(8):
            sstore(xsf,r*8+sp,80,16,xr[r,pl.ds(48*sp,80),:])

def unspace(sid,acc,yr,emit):
    for r in range(2):
        for sp in range(8):
            yr[r,pl.ds(48*sp,48),:]=sload(acc,r*8+sp,48,16)
        for bb in range(16):
            v=jnp.zeros((16,LW),F32)
            ids=sid[pl.ds(r*256+16*bb,16),:]
            for q in range(8):
                v=jnp.where(ids==q,yr[r,pl.ds(16*(bb+q),16),:],v)
            emit(r*256+16*bb,v)

def conv_fwd_kernel(seg_ref,idx_ref,x0_ref,x1_ref,x2_ref,x3_ref,w_ref,bias_ref,first_ref,pre_ref,xs_ref,xt,xa,x4,xr,xsf,acc,yr,facc,sid):
    pair=pl.program_id(0); g=pl.program_id(1)
    @pl.when(g==0)
    def _():
        fill_ids(seg_ref,pair,sid)
        for m,x_ref in enumerate((x0_ref,x1_ref,x2_ref,x3_ref)):
            k=pl.multiple_of((idx_ref[0]^m)*256,256)
            for r in range(2):
                fstore(xt,r*1024+k,256,x_ref[...].astype(F32)[:,LW*r:LW*r+LW])
        for a in range(4):
            xa[a]=sload(xt,a,512,4).astype(BF)
    v=dot(xa[0],pick_matrix(g,0))
    for a in range(1,4):
        v=v+dot(xa[a],pick_matrix(g,a))
    x4[...]=v[:,:LW]
    respace(sid,x4,xr,xsf)
    n=XROWS+32
    zt=jnp.zeros((n+16,64),F32)
    va=xsf[0,0:n+16,:]; vb=xsf[1,0:n+16,:]
    z0=jnp.concatenate([zt,va[:,:64]],axis=1); z1=jnp.concatenate([va[:,64:],vb[:,:64]],axis=1)
    for at,piece in enumerate((va[0:n].astype(BF),(vb[0:n]+z0[16:]).astype(BF),z1[16:].astype(BF))):
        xs_ref[0,0,:,128*at:128*at+128]=piece[:XROWS]
        xs_ref[0,0,:,384+128*at:512+128*at]=piece[32:]
    s=dot(xs_ref[0,0,512:512+MROWS,0:256],w_ref[0,6144:6400,:])
    for J in range(8):
        s=s+dot(xs_ref[0,0,64*J:64*J+MROWS,:],w_ref[0,768*J:768*J+768,:])
    acc[0]=s[:,:128]; acc[1]=s[:,128:]
    bias=bias_ref[0]
    def emit(row,v):
        pre_ref[0,0,pl.ds(row,16),:]=v+bias
    unspace(sid,acc,yr,emit)
    pre=pre_ref[0,0]
    fs=(x4[...]+pre*erf_gelu_parts(pre)).astype(BF)
    for a in range(4):
        f=dot(fs,pick_back(g,a))[:,:LW]
        @pl.when(g==0)
        def _(): facc[a]=f
        @pl.when(g>0)
        def _(): facc[a]=facc[a]+f
    @pl.when(g==3)
    def _():
        for a in range(4):
            sstore(xt,a,512,4,facc[a])
        first_ref[...]=jnp.concatenate([fload(xt,0,1024),fload(xt,1024,1024)],axis=1).astype(BF)

def conv_fwd(ends,idx,xs4,w,bias4):
    pairs=xs4[0].shape[0]//256
    return pl.pallas_call(conv_fwd_kernel,grid=(pairs,4),
        in_specs=[pl.BlockSpec(memory_space=pltpu.SMEM)]*2+[pl.BlockSpec((256,PW),lambda p,g:(p,0))]*4+[
                  pl.BlockSpec((1,WROWS,256),lambda p,g:(g,0,0)),
                  pl.BlockSpec((1,1,LW),lambda p,g:(g,0,0))],
        out_specs=[pl.BlockSpec((1024,PW),lambda p,g:(p,0)),
                   pl.BlockSpec((1,1,512,LW),lambda p,g:(p,g,0,0)),
                   pl.BlockSpec((1,1,XROWS,768),lambda p,g:(p,g,0,0))],
        out_shape=[jax.ShapeDtypeStruct((pairs*1024,PW),BF),
                   jax.ShapeDtypeStruct((pairs,4,512,LW),F32),
                   jax.ShapeDtypeStruct((pairs,4,XROWS,768),BF)],
        scratch_shapes=[pltpu.VMEM((2,2048,128),F32),pltpu.VMEM((4,512,LW),BF),pltpu.VMEM((512,LW),F32),
            pltpu.VMEM((2,416,LW),F32),pltpu.VMEM((2,XROWS+TAIL,128),F32),pltpu.VMEM((2,MROWS,128),F32),pltpu.VMEM((2,384,LW),F32),
            pltpu.VMEM((4,512,LW),F32),pltpu.VMEM((512,LW),jnp.int32)],
        cost_estimate=cost(35),
        compiler_params=pltpu.CompilerParams(vmem_limit_bytes=VM))(ends,idx,*xs4,w,bias4)

def tap_kernel(seg_ref,e0_ref,e1_ref,first_ref,stat_ref,mom_ref,mox_ref,gain_ref,pre_ref,xs_ref,qkv_ref,tap_ref,ds_ref,d4_ref,bias_ref,vec_ref,xt,xa,dc,xr,xsf,A,sid):
    pair=pl.program_id(0); g=pl.program_id(1)
    @pl.when(g==0)
    def _():
        fill_ids(seg_ref,pair,sid)
        gain=gain_ref[...]
        sg=jnp.zeros((1,LW),F32); sh=jnp.zeros((1,LW),F32)
        for t in range(8):
            r,k=t//4,t%4
            rows=slice(256*k,256*k+256); cols=slice(LW*r,LW*r+LW)
            e=(e0_ref[rows]+e1_ref[rows].astype(F32))[:,cols]
            st=stat_ref[256*t:256*t+256]
            mean=st[:,0:1]; rstd=st[:,1:2]
            mom=jnp.concatenate([mom_ref[t,0:2]+mox_ref[2*t:2*t+2].astype(F32)[:,:256],jnp.zeros((126,256),F32)],axis=0).T*(1.0/768)
            xhat=(first_ref[rows].astype(F32)[:,cols]-mean)*rstd
            sg=sg+jnp.sum(e*xhat,axis=0,keepdims=True); sh=sh+jnp.sum(e,axis=0,keepdims=True)
            fstore(xt,256*t,256,rstd*(e*gain-mom[:,0:1]-xhat*mom[:,1:2]))
        vec_ref[0,0:1]=sg; vec_ref[0,1:2]=sh; vec_ref[0,2:8]=jnp.zeros((6,LW),F32)
        for a in range(4):
            xa[a]=sload(xt,a,512,4).astype(BF)
    v=dot(xa[0],pick_matrix(g,0))
    for a in range(1,4):
        v=v+dot(xa[a],pick_matrix(g,a))
    v=v[:,:LW]
    d4_ref[0,0]=v.astype(BF)
    pre=pre_ref[0,0]
    cdf=erf_gelu_parts(pre)
    slope=cdf+pre*(jnp.exp(-0.5*pre*pre)*0.3989422804014327)
    d=v*slope
    dc[...]=d
    bias_ref[0,0]=jnp.sum(d,axis=0,keepdims=True)
    respace(sid,dc,xr,xsf)
    ds_ref[0,0,:,0:128]=xsf[0,0:XROWS].astype(BF); ds_ref[0,0,:,128:256]=xsf[1,0:XROWS].astype(BF)
    DT=fload(xsf,256,MROWS).astype(BF).T
    for J in range(8):
        A[:,768*J:768*J+768]=dot(DT,xs_ref[0,0,64*J:64*J+MROWS,:])
    A[:,6144:6400]=dot(DT,xs_ref[0,0,512:512+MROWS,0:256])
    n=6144
    o=A[0:48,0:n]
    for b in range(1,4):
        o=o+A[48*b:48*b+48,48*b:48*b+n]
    for J in range(8):
        tap_ref[0,J]=o[:,768*J:768*J+768].astype(BF)
    tap_ref[0,8:11]=jnp.where(pair==0,qkv_ref[...],jnp.zeros((3,48,768),BF))

def tap_grads(ends,e0,e1,first,stat,mom,gain,pre,xs,g_qkv,deps=()):
    pairs=e0.shape[0]//1024
    return pl.pallas_call(skip(tap_kernel,11,len(deps)),grid=(pairs,4),
        in_specs=[pl.BlockSpec(memory_space=pltpu.SMEM),
                  pl.BlockSpec((1024,PW),lambda p,g:(p,0)),
                  pl.BlockSpec((1024,PW),lambda p,g:(p,0)),
                  pl.BlockSpec((1024,PW),lambda p,g:(p,0)),
                  pl.BlockSpec((2048,128),lambda p,g:(p,0)),
                  pl.BlockSpec((8,8,256),lambda p,g:(p,0,0)),
                  pl.BlockSpec((16,PW),lambda p,g:(64*pairs+p,0)),
                  pl.BlockSpec((1,LW),lambda p,g:(0,0)),
                  pl.BlockSpec((1,1,512,LW),lambda p,g:(p,g,0,0)),
                  pl.BlockSpec((1,1,XROWS,768),lambda p,g:(p,g,0,0)),
                  pl.BlockSpec((3,48,768),lambda p,g:(0,g,0))]+[ANY]*len(deps),
        out_specs=[pl.BlockSpec((1,11,48,768),lambda p,g:(p,0,g,0)),
                   pl.BlockSpec((1,1,XROWS,256),lambda p,g:(p,g,0,0)),
                   pl.BlockSpec((1,1,512,LW),lambda p,g:(p,g,0,0)),
                   pl.BlockSpec((1,1,1,LW),lambda p,g:(p,g,0,0)),
                   pl.BlockSpec((1,8,LW),lambda p,g:(p,0,0))],
        out_shape=[jax.ShapeDtypeStruct((pairs,11,LW,768),BF),
                   jax.ShapeDtypeStruct((pairs,4,XROWS,256),BF),
                   jax.ShapeDtypeStruct((pairs,4,512,LW),BF),
                   jax.ShapeDtypeStruct((pairs,4,1,LW),F32),jax.ShapeDtypeStruct((pairs,8,LW),F32)],
        scratch_shapes=[pltpu.VMEM((2,2048,128),F32),pltpu.VMEM((4,512,LW),BF),pltpu.VMEM((512,LW),F32),
            pltpu.VMEM((2,416,LW),F32),pltpu.VMEM((2,XROWS+TAIL,128),F32),pltpu.VMEM((LW,6400),F32),pltpu.VMEM((512,LW),jnp.int32)],
        cost_estimate=cost(24),
        compiler_params=pltpu.CompilerParams(vmem_limit_bytes=VM))(ends,e0,e1,first,stat,mom,e1,gain,pre,xs,g_qkv,*deps)

def back_kernel(at,seg_ref,idx_ref,ds_ref,d4_ref,w_ref,*rest):
    if at:
        part_ref,out_ref,xt,acc,yr,fs,sid=rest
    else:
        facc,acc,yr,fs,sid=rest
    pair=pl.program_id(0); i=pl.program_id(1); g=i+at
    @pl.when(i==0)
    def _(): fill_ids(seg_ref,pair,sid)
    s=None
    for j in range(NJ):
        p=dot_nt(ds_ref[0,0,16*(NJ-1-j):16*(NJ-1-j)+MROWS,:],w_ref[0,LW*j:LW*j+256,:])
        s=p if s is None else s+p
    def emit(row,v):
        fs[pl.ds(row,16),:]=(v+d4_ref[0,0,pl.ds(row,16),:].astype(F32)).astype(BF)
    acc[0]=s[:,:128]; acc[1]=s[:,128:]
    unspace(sid,acc,yr,emit)
    if at:
        for a in range(4):
            f=dot(fs[...],pick_back(g,a))[:,:LW]
            @pl.when(i==0)
            def _(): sstore(xt,a,512,4,f+part_ref[0,a])
            @pl.when(i>0)
            def _(): sstore(xt,a,512,4,f+sload(xt,a,512,4))
        @pl.when(i==1)
        def _():
            for k in range(4):
                out_ref[idx_ref[0]^k]=jnp.concatenate([fload(xt,k*256,256),fload(xt,1024+k*256,256)],axis=1).astype(BF)
    else:
        for a in range(4):
            f=dot(fs[...],pick_back(g,a))[:,:LW]
            @pl.when(i==0)
            def _(): facc[0,a]=f
            @pl.when(i>0)
            def _(): facc[0,a]=facc[0,a]+f

def conv_back(at,ends,idx,ds,d4,w,part=None,deps=()):
    pairs=ds.shape[0]
    parts=() if part is None else (part,)
    facc=pl.BlockSpec((1,4,512,LW),lambda p,g:(p,0,0,0))
    scratch=[pltpu.VMEM((2,2048,128),F32)] if at else []
    return pl.pallas_call(skip(lambda *refs: back_kernel(at,*refs),5+len(parts),len(deps)),grid=(pairs,2),
        in_specs=[pl.BlockSpec(memory_space=pltpu.SMEM),pl.BlockSpec(memory_space=pltpu.SMEM),
                  pl.BlockSpec((1,1,XROWS,256),lambda p,g:(p,g+at,0,0)),
                  pl.BlockSpec((1,1,512,LW),lambda p,g:(p,g+at,0,0)),
                  pl.BlockSpec((1,WROWS,256),lambda p,g:(g+at,0,0))]+[facc]*len(parts)+[ANY]*len(deps),
        out_specs=pl.BlockSpec((4,256,PW),lambda p,g:(0,p,0)) if at else facc,
        out_shape=jax.ShapeDtypeStruct((4,pairs*256,PW),BF) if at else jax.ShapeDtypeStruct((pairs,4,512,LW),F32),
        scratch_shapes=scratch+[pltpu.VMEM((2,MROWS,128),F32),pltpu.VMEM((2,384,LW),F32),
            pltpu.VMEM((512,LW),BF),pltpu.VMEM((512,LW),jnp.int32)],
        cost_estimate=cost(100),
        compiler_params=pltpu.CompilerParams(vmem_limit_bytes=VM))(ends,idx,ds,d4,w,*parts,*deps)


def qkv_kernel(f0,f1,f2,f3,w_ref,bias_ref,gain_ref,shift_ref,q_ref,k_ref,v_ref,ml_ref,stat_ref):
    fs=[f[...].astype(F32) for f in (f0,f1,f2,f3)]
    fs=[jnp.concatenate([f[:,:LW],f[:,LW:]],axis=0) for f in fs]
    mean=sum(jnp.sum(f,axis=1,keepdims=True) for f in fs)*(1.0/768)
    cs=[f-mean for f in fs]
    var=sum(jnp.sum(c*c,axis=1,keepdims=True) for c in cs)*(1.0/768)
    rstd=lax.rsqrt(var+1e-5)
    n=mean.shape[0]
    pad=jnp.zeros((n,64),BF)
    out=None
    for m in range(4):
        ml=(cs[m]*rstd*gain_ref[m]+shift_ref[m]).astype(BF)
        ml_ref[m]=ml.reshape(2,256,LW)
        p=dot(jnp.concatenate([ml,pad],axis=1),w_ref[m])
        out=p if out is None else out+p
    out=(out+bias_ref[...]).astype(BF)
    out=out.reshape(2,256,768)
    q_ref[...]=out[:,:,0:192]; k_ref[...]=out[:,:,256:448]; v_ref[...]=out[:,:,512:704]
    lane=lax.broadcasted_iota(jnp.int32,(n,128),1)
    stat_ref[...]=jnp.where(lane==0,mean,jnp.where(lane==1,rstd,0.0)).reshape(2,256,128)

def qkv(fs,w,bias,gain,shift):
    pairs=fs[0].shape[0]//1024; R=2*pairs
    row=pl.BlockSpec((2,256,LW),lambda p,k:(p,k,0))
    full=lambda a: pl.BlockSpec(a.shape,lambda p,k:(0,)*a.ndim)
    return pl.pallas_call(qkv_kernel,grid=(pairs,4),
        in_specs=[pl.BlockSpec((256,PW),lambda p,k:(4*p+k,0))]*4+[full(w),full(bias),full(gain),full(shift)],
        out_specs=[row]*3+[pl.BlockSpec((4,2,256,LW),lambda p,k:(0,p,k,0)),pl.BlockSpec((2,256,128),lambda p,k:(p,k,0))],
        out_shape=[jax.ShapeDtypeStruct((R,1024,LW),BF)]*3+[jax.ShapeDtypeStruct((4,R,1024,LW),BF),jax.ShapeDtypeStruct((R,1024,128),F32)],
        cost_estimate=cost(10),
        compiler_params=pltpu.CompilerParams(vmem_limit_bytes=VM))(*fs,w,bias,gain,shift)

def seg_vec(seg_ref,r,shape,axis,start):
    t=lax.broadcasted_iota(jnp.int32,shape,axis)+start
    v=jnp.zeros(shape,jnp.int32)
    end=0
    for i in range(8):
        end=end+seg_ref[r,i]
        v=v+(t>=end).astype(jnp.int32)
    return v

def attn_kernel(idx_ref,seg_ref,q_ref,k_ref,v_ref,o_ref,of_ref,lse_ref):
    pair=pl.program_id(0); kb=pl.program_id(1)
    for r in range(2):
        sq=seg_vec(seg_ref,2*pair+r,(256,1),0,kb*256); sk=seg_vec(seg_ref,2*pair+r,(1,1024),1,0)
        same=sq==sk
        outs=[]; rows=[]
        for h in range(3):
            c=slice(64*h,64*h+64)
            s=jnp.where(same,dot_nt(q_ref[r,:,c],k_ref[r,:,c]),-1e30)
            mx=jnp.max(s,axis=1,keepdims=True)
            p=jnp.exp(s-mx)
            tot=jnp.sum(p,axis=1,keepdims=True)
            outs.append(dot(p.astype(BF),v_ref[r,:,c])/tot)
            rows.append(jnp.broadcast_to(mx+jnp.log(tot),(256,128)).T[0:1,:])
        o=jnp.concatenate(outs,axis=1)
        of_ref[r]=o
        o_ref[0,:,LW*r:LW*r+LW]=o.astype(BF)
        lse_ref[r,0]=jnp.concatenate(rows+[jnp.zeros((5,256),F32)],axis=0)

def attn(idx,ends,q,k,v):
    R=ends.shape[0]; pairs=R//2
    blk=pl.BlockSpec((2,256,LW),lambda p,b,i,s:(p,b,0)); full=pl.BlockSpec((2,1024,LW),lambda p,b,i,s:(p,0,0))
    return pl.pallas_call(attn_kernel,
        grid_spec=pltpu.PrefetchScalarGridSpec(num_scalar_prefetch=2,grid=(pairs,4),
        in_specs=[blk,full,full],
        out_specs=[pl.BlockSpec((1,256,PW),lambda p,b,i,s:(b^i[0],p,0)),blk,pl.BlockSpec((2,1,8,256),lambda p,b,i,s:(p,b,0,0))]),
        out_shape=[jax.ShapeDtypeStruct((4,pairs*256,PW),BF),jax.ShapeDtypeStruct((R,1024,LW),F32),jax.ShapeDtypeStruct((R,4,8,256),F32)],
        cost_estimate=cost(18),
        compiler_params=pltpu.CompilerParams(vmem_limit_bytes=VM))(idx,ends,q,k,v)

def attn_bwd_kernel(r,idx_ref,seg_ref,q_ref,k_ref,v_ref,o_ref,d0,d1,d2,d3,lse_ref,dq_ref,dk_ref,dv_ref,dks,dvs):
    pair=pl.program_id(0); kb=pl.program_id(1)
    m=kb^idx_ref[0]
    mine=slice(LW*r,LW*r+LW)
    dod=jnp.where(m<2,jnp.where(m==0,d0[...],d1[...]),jnp.where(m==2,d2[...],d3[...])).astype(F32)[:,mine].astype(BF)
    @pl.when(kb==0)
    def _():
        dks[...]=jnp.zeros_like(dks); dvs[...]=jnp.zeros_like(dvs)
    sq=seg_vec(seg_ref,2*pair+r,(1,256),1,kb*256); sk=seg_vec(seg_ref,2*pair+r,(1024,1),0,0)
    same=sk==sq
    dqs=[]; ks=[]; vs=[]
    for h in range(3):
        c=slice(64*h,64*h+64)
        q=q_ref[0,:,c]; k=k_ref[0,:,c]; do=dod[:,c]
        delta=jnp.sum(do.astype(F32)*o_ref[0,:,c],axis=1,keepdims=True)
        delta=jnp.broadcast_to(delta,(256,128)).T[0:1,:]
        st=jnp.where(same,dot_nt(k,q)-lse_ref[0,0,h:h+1,:],-1e30)
        p=jnp.exp(st)
        dp=dot_nt(v_ref[0,:,c],do)
        ds=(p*(dp-delta)).astype(BF)
        vs.append(dot(p.astype(BF),do)); ks.append(dot(ds,q)); dqs.append(dot_tn(ds,k))
    dks[...]+=jnp.concatenate(ks,axis=1); dvs[...]+=jnp.concatenate(vs,axis=1)
    dq_ref[0]=jnp.concatenate(dqs,axis=1).astype(BF)
    @pl.when(kb==3)
    def _():
        dk_ref[0]=dks[...].astype(BF); dv_ref[0]=dvs[...].astype(BF)

def attn_bwd(r,idx,ends,q,k,v,o,dos,lse,deps=()):
    pairs=ends.shape[0]//2
    blk=pl.BlockSpec((1,256,LW),lambda p,b,i,s:(2*p+r,b,0)); full=pl.BlockSpec((1,1024,LW),lambda p,b,i,s:(2*p+r,0,0))
    out=pl.BlockSpec((1,256,LW),lambda p,b,i,s:(p,b,0)); outs=pl.BlockSpec((1,1024,LW),lambda p,b,i,s:(p,0,0))
    return pl.pallas_call(skip(lambda *refs: attn_bwd_kernel(r,*refs),11,len(deps)),
        grid_spec=pltpu.PrefetchScalarGridSpec(num_scalar_prefetch=2,grid=(pairs,4),
        in_specs=[blk,full,full,blk]+[pl.BlockSpec((256,PW),lambda p,b,i,s:(p,0))]*4+[pl.BlockSpec((1,1,8,256),lambda p,b,i,s:(2*p+r,b,0,0))]+[ANY]*len(deps),
        out_specs=[out,outs,outs],scratch_shapes=[pltpu.VMEM((1024,LW),F32)]*2),
        out_shape=[jax.ShapeDtypeStruct((pairs,1024,LW),BF)]*3,
        cost_estimate=cost(60),
        compiler_params=pltpu.CompilerParams(vmem_limit_bytes=VM))(idx,ends,q,k,v,o,*dos,lse,*deps)

def pad3(a,b,c):
    z=jnp.zeros((a.shape[0],64),BF)
    return jnp.concatenate([a,z,b,z,c,z],axis=1)

def dmix_kernel(idx_ref,q0,k0,v0,q1,k1,v1,w_ref,sec_ref,f0,f1,f2,f3,stat_ref,gain_ref,keep_ref,send_ref,mom_ref):
    kb=pl.program_id(1)
    flat=lambda x: x[...].reshape(512,x.shape[-1])
    d=jnp.concatenate([pad3(q0[0],k0[0],v0[0]),pad3(q1[0],k1[0],v1[0])],axis=0)
    st=flat(stat_ref); mean=st[:,0:1]; rstd=st[:,1:2]
    mine=(kb==idx_ref[0]).astype(F32)
    m1=None
    for m,f in enumerate((f0,f1,f2,f3)):
        part=dot_nt(d,w_ref[m])[:,:LW]
        part=part+mine*sec_ref[m].reshape(512,LW)
        both=jnp.concatenate([part[:256],part[256:]],axis=1)
        if m%2: send_ref[m//2]=both.astype(BF)
        else: keep_ref[m//2]=both
        eg=part*gain_ref[m]
        f=f[...].astype(F32)
        xh=(jnp.concatenate([f[:,:LW],f[:,LW:]],axis=0)-mean)*rstd
        a=jnp.sum(eg,axis=1,keepdims=True); b=jnp.sum(eg*xh,axis=1,keepdims=True)
        m1=(a,b) if m1 is None else (m1[0]+a,m1[1]+b)
    lane=lax.broadcasted_iota(jnp.int32,(512,128),1)
    t=jnp.where(lane==0,m1[0],jnp.where(lane==1,m1[1],0.0)).T[0:8,:]
    mom_ref[0,0]=t[:,:256]; mom_ref[1,0]=t[:,256:]

def dmix(idx,heads,w,sec,fs,stat,gain,deps=()):
    pairs=heads[0].shape[0]; R=2*pairs
    blk=pl.BlockSpec((1,256,LW),lambda p,b,i:(p,b,0))
    full=lambda a: pl.BlockSpec(a.shape,lambda p,b,i:(0,)*a.ndim)
    pack=pl.BlockSpec((2,256,PW),lambda p,b,i:(0,4*p+b,0))
    return pl.pallas_call(skip(dmix_kernel,15,len(deps)),
        grid_spec=pltpu.PrefetchScalarGridSpec(num_scalar_prefetch=1,grid=(pairs,4),
        in_specs=[blk]*6+[full(w),pl.BlockSpec((4,2,256,LW),lambda p,b,i:(0,p,0,0))]+[pl.BlockSpec((256,PW),lambda p,b,i:(4*p+b,0))]*4
            +[pl.BlockSpec((2,256,128),lambda p,b,i:(p,b,0)),full(gain)]+[ANY]*len(deps),
        out_specs=[pack,pack,pl.BlockSpec((2,1,8,256),lambda p,b,i:(p,b,0,0))]),
        out_shape=[jax.ShapeDtypeStruct((2,pairs*1024,PW),F32),jax.ShapeDtypeStruct((2,pairs*1024,PW),BF),jax.ShapeDtypeStruct((R,4,8,256),F32)],
        cost_estimate=cost(0.1),
        compiler_params=pltpu.CompilerParams(vmem_limit_bytes=VM))(idx,*heads,w,sec,*fs,stat,gain,*deps)

def qkvw_kernel(q0,k0,v0,q1,k1,v1,ml_ref,out_ref,bias_ref,acc):
    i=pl.program_id(0)*2+pl.program_id(1)
    @pl.when(i==0)
    def _(): acc[...]=jnp.zeros_like(acc); bias_ref[...]=jnp.zeros_like(bias_ref)
    d=jnp.concatenate([pad3(q0[0],k0[0],v0[0]),pad3(q1[0],k1[0],v1[0])],axis=0)
    dt=d.T
    bias_ref[...]+=jnp.broadcast_to(jnp.sum(d.astype(F32),axis=0,keepdims=True),bias_ref.shape)
    pad=jnp.zeros((d.shape[0],64),BF)
    for m in range(4):
        acc[m]+=dot(dt,jnp.concatenate([ml_ref[m].reshape(d.shape[0],LW),pad],axis=1))
    @pl.when(i==2*pl.num_programs(0)-1)
    def _():
        for t in range(3):
            out_ref[t]=jnp.concatenate([acc[m,256*t:256*t+192,:LW] for m in range(4)],axis=1).astype(BF)

def qkvw(heads,ml,deps=()):
    pairs=heads[0].shape[0]
    row=pl.BlockSpec((1,512,LW),lambda p,i:(p,i,0))
    return pl.pallas_call(skip(qkvw_kernel,7,len(deps)),grid=(pairs,2),
        in_specs=[row]*6+[pl.BlockSpec((4,2,512,LW),lambda p,i:(0,p,i,0))]+[ANY]*len(deps),
        out_specs=[pl.BlockSpec((3,LW,768),lambda p,i:(0,0,0)),pl.BlockSpec((8,768),lambda p,i:(0,0))],
        out_shape=[jax.ShapeDtypeStruct((3,LW,768),BF),jax.ShapeDtypeStruct((8,768),F32)],
        scratch_shapes=[pltpu.VMEM((4,768,256),F32)],
        cost_estimate=cost(8),
        compiler_params=pltpu.CompilerParams(vmem_limit_bytes=VM))(*heads,ml,*deps)


def row_sum(x):
    return jnp.sum(x, axis=0, keepdims=True)


def norm_parts(x):
    c = x - jnp.mean(x, axis=1, keepdims=True)
    rstd = lax.rsqrt(jnp.mean(c * c, axis=1, keepdims=True) + 1e-5)
    return c * rstd, rstd


def norm_back(e, xhat, rstd, gain):
    eg = e * gain
    return rstd * (eg - jnp.mean(eg, axis=1, keepdims=True) - xhat * jnp.mean(eg * xhat, axis=1, keepdims=True))


def in_order(blocks, index):
    low = (index & 1) != 0
    high = (index & 2) != 0
    b = [jnp.where(low, blocks[m ^ 1], blocks[m]) for m in range(4)]
    return jnp.concatenate([jnp.where(high, b[m ^ 2], b[m]) for m in range(4)], axis=1)


def half(r):
    return slice(LW * (r % 2), LW * (r % 2) + LW)


def ff_kernel(
    idx_ref, f0, f1, f2, f3, a0, a1, a2, a3, og_ref, pw_ref, iw_ref, ow_ref, ib_ref, vec_ref,
    out_ref, act_ref, din_ref, ml_ref, do_ref, dp_ref, att_ref, datt_ref, sec_ref, sums_ref, ibg_ref,
    mid, xh2, rs2, acc, slopes,
):
    i = pl.program_id(0)
    index = idx_ref[0]
    R = 2 * f0.shape[0]
    M = R * 256
    pos_gain, pos_shift, proj_bias, gain2, shift2, outer_bias, gain3, shift3 = [vec_ref[j : j + 1, :] for j in range(8)]

    @pl.when(i == 0)
    def _():
        for r in range(R):
            rows = pl.ds(256 * r, 256)
            xhat, _ = norm_parts(in_order([f[r // 2, 0].astype(F32)[:, half(r)] for f in (f0, f1, f2, f3)], index))
            att_ref[rows] = in_order([a[pl.ds(256 * (r // 2), 256)].astype(F32)[:, half(r)] for a in (a0, a1, a2, a3)], index).astype(BF)
            second = xhat * pos_gain + pos_shift + dot(att_ref[rows], pw_ref[...]) + proj_bias
            xhat, rstd = norm_parts(second)
            xh2[rows] = xhat
            rs2[rows] = jnp.broadcast_to(rstd, (256, 128))
            middle = xhat * gain2 + shift2
            mid[rows] = middle
            ml_ref[rows] = middle.astype(BF)
        acc[...] = jnp.zeros_like(acc)

    @pl.when(i < 4)
    def _():
        for r in range(R):
            rows = pl.ds(256 * r, 256)
            inner = dot(ml_ref[rows], iw_ref[...]) + ib_ref[0]
            phi = erf_gelu_parts(inner)
            slopes[i, rows] = (phi + inner * (jnp.exp(-0.5 * inner * inner) * 0.3989422804014327)).astype(BF)
            act_ref[rows] = (inner * phi).astype(BF)
            acc[rows] += dot(act_ref[rows], ow_ref[...])

    @pl.when(i == 3)
    def _():
        g1 = g2 = g3 = jnp.zeros((1, 768), F32)
        for r in range(R):
            rows = pl.ds(256 * r, 256)
            xhat, rstd = norm_parts(mid[rows] + acc[rows] + outer_bias)
            out_ref[rows] = (xhat * gain3 + shift3).astype(BF)
            e = og_ref[rows].astype(F32)
            d = norm_back(e, xhat, rstd, gain3)
            low = d.astype(BF)
            do_ref[rows] = low
            mid[rows] = d
            g1, g2, g3 = g1 + row_sum(e * xhat), g2 + row_sum(e), g3 + row_sum(low.astype(F32))
        sums_ref[0:1] = g1
        sums_ref[1:2] = g2
        sums_ref[2:3] = g3
        sums_ref[3:8] = jnp.zeros((5, 768), F32)

    @pl.when(i >= 4)
    def _():
        g = jnp.zeros((1, 768), F32)
        for r in range(R):
            rows = pl.ds(256 * r, 256)
            d = dot_nt(do_ref[rows], ow_ref[...]) * slopes[7 - i, rows].astype(F32)
            low = d.astype(BF)
            din_ref[rows] = low
            g = g + row_sum(low.astype(F32))
            mid[rows] += dot_nt(low, iw_ref[...])
        ibg_ref[0] = g

    @pl.when(i == 7)
    def _():
        g1 = g2 = g3 = jnp.zeros((1, 768), F32)
        for r in range(R):
            rows = pl.ds(256 * r, 256)
            e = mid[rows]
            xhat = xh2[rows]
            d = norm_back(e, xhat, rs2[rows, 0:1], gain2)
            low = d.astype(BF)
            dp_ref[rows] = low
            datt = dot_nt(low, pw_ref[...]).astype(BF)
            for b in range(4):
                datt_ref[index ^ b, pl.ds(256 * (r // 2), 256), half(r)] = datt[:, LW * b : LW * b + LW]
                sec_ref[index ^ b, r] = d[:, LW * b : LW * b + LW]
            g1, g2, g3 = g1 + row_sum(e * xhat), g2 + row_sum(e), g3 + row_sum(low.astype(F32))
        sums_ref[3:4] = g1
        sums_ref[4:5] = g2
        sums_ref[5:6] = g3


def ff(idx, firsts, atts, out_grad, pw, iw, ow, ib, vec):
    pairs = atts[0].shape[0] // 256
    R = 2 * pairs
    M = R * 256
    chunk = lambda i: jnp.where(i < 4, i, 7 - i)
    whole = lambda *s: pl.BlockSpec(s, lambda i, x: (0,) * len(s))
    return pl.pallas_call(
        ff_kernel,
        grid_spec=pltpu.PrefetchScalarGridSpec(
            num_scalar_prefetch=1,
            grid=(8,),
            in_specs=[pl.BlockSpec((pairs, 1, 256, PW), lambda i, x: (0, x[0], 0, 0))] * 4
            + [whole(pairs * 256, PW)] * 4
            + [
                whole(M, 768),
                whole(768, 768),
                pl.BlockSpec((768, 768), lambda i, x: (0, chunk(i))),
                pl.BlockSpec((768, 768), lambda i, x: (chunk(i), 0)),
                pl.BlockSpec((1, 1, 768), lambda i, x: (chunk(i), 0, 0)),
                whole(8, 768),
            ],
            out_specs=[
                whole(M, 768),
                pl.BlockSpec((M, 768), lambda i, x: (0, jnp.minimum(i, 3))),
                pl.BlockSpec((M, 768), lambda i, x: (0, jnp.minimum(7 - i, 3))),
            ]
            + [whole(M, 768)] * 4
            + [
                whole(4, pairs * 256, PW),
                whole(4, R, 256, LW),
                whole(8, 768),
                pl.BlockSpec((1, 1, 768), lambda i, x: (jnp.minimum(7 - i, 3), 0, 0)),
            ],
            scratch_shapes=[
                pltpu.VMEM((M, 768), F32),
                pltpu.VMEM((M, 768), F32),
                pltpu.VMEM((M, 128), F32),
                pltpu.VMEM((M, 768), F32),
                pltpu.VMEM((4, M, 768), BF),
            ],
        ),
        out_shape=[
            jax.ShapeDtypeStruct((M, 768), BF),
            jax.ShapeDtypeStruct((M, 3072), BF),
            jax.ShapeDtypeStruct((M, 3072), BF),
        ]
        + [jax.ShapeDtypeStruct((M, 768), BF)] * 4
        + [
            jax.ShapeDtypeStruct((4, pairs * 256, PW), BF),
            jax.ShapeDtypeStruct((4, R, 256, LW), F32),
            jax.ShapeDtypeStruct((8, 768), F32),
            jax.ShapeDtypeStruct((4, 1, 768), F32),
        ],
        cost_estimate=cost(40),
        compiler_params=pltpu.CompilerParams(vmem_limit_bytes=VM),
    )(idx, *[f.reshape(pairs, 4, 256, PW) for f in firsts], *atts, out_grad, pw, iw, ow, ib, vec)


def put(index, keep, send, b, rows, value):
    m = index ^ b

    @pl.when((m & 1) == 0)
    def _():
        keep[m >> 1, rows] = value

    @pl.when((m & 1) == 1)
    def _():
        send[m >> 1, rows] = value


def outer_kernel(idx_ref, act_ref, do_ref, sums_ref, ibg_ref, keep_ref, send_ref):
    c = pl.program_id(0)
    index = idx_ref[0]
    outer = dot_tn(do_ref[...], act_ref[...]).astype(BF)
    for b in range(4):
        put(index, keep_ref, send_ref, b, pl.ds(pl.multiple_of(LW * c, LW), LW), outer[LW * b : LW * b + LW])

    @pl.when(c == 0)
    def _():
        for b in range(4):
            small = jnp.concatenate([sums_ref[:, LW * b : LW * b + LW], jnp.zeros((8, 576), F32)], axis=1)
            small = jnp.concatenate([small, ibg_ref[b], jnp.zeros((7, 768), F32)], axis=0)
            put(index, keep_ref, send_ref, b, pl.ds(768, 16), small.astype(BF))
            put(index, keep_ref, send_ref, b, pl.ds(784, 16), jnp.zeros((16, 768), BF))


def inner_kernel(idx_ref, din_ref, ml_ref, dp_ref, att_ref, keep_ref, send_ref):
    c = pl.program_id(0)
    index = idx_ref[0]
    put(index, keep_ref, send_ref, c, pl.ds(0, 768), dot_tn(ml_ref[...], din_ref[...]).astype(BF))

    @pl.when(c == 0)
    def _():
        proj = dot_tn(dp_ref[...], att_ref[...]).astype(BF)
        for b in range(4):
            put(index, keep_ref, send_ref, b, pl.ds(768, LW), proj[LW * b : LW * b + LW])


def weight_grads(kernel, rows, idx, wide, others, deps=()):
    M = wide.shape[0]
    whole = lambda a: pl.BlockSpec(a.shape, lambda i, x: (0,) * a.ndim)
    out = pl.BlockSpec((2, rows, 768), lambda i, x: (0, 0, 0))
    return pl.pallas_call(
        skip(kernel, 2 + len(others), len(deps)),
        grid_spec=pltpu.PrefetchScalarGridSpec(
            num_scalar_prefetch=1,
            grid=(4,),
            in_specs=[pl.BlockSpec((M, 768), lambda i, x: (0, i))] + [whole(a) for a in others] + [ANY] * len(deps),
            out_specs=[out, out],
        ),
        out_shape=[jax.ShapeDtypeStruct((2, rows, 768), BF)] * 2,
        cost_estimate=cost(8),
        compiler_params=pltpu.CompilerParams(vmem_limit_bytes=VM),
    )(idx, wide, *others, *deps)


def far_kernel(keep_ref, got_ref, out_ref):
    out_ref[...] = (keep_ref[0].astype(F32) + got_ref[0].astype(F32)).astype(BF)


def far_sum(keep, got, deps=()):
    n = keep.shape[1]
    block = pl.BlockSpec((1, n // 2, 768), lambda i: (1, i, 0))
    return pl.pallas_call(
        skip(far_kernel, 2, len(deps)),
        grid=(2,),
        in_specs=[block] * 2 + [ANY] * len(deps),
        out_specs=pl.BlockSpec((n // 2, 768), lambda i: (i, 0)),
        out_shape=jax.ShapeDtypeStruct((n, 768), BF),
        cost_estimate=cost(1),
        compiler_params=pltpu.CompilerParams(vmem_limit_bytes=VM),
    )(keep, got, *deps)


def own_kernel(keep_ref, got_ref, far_ref, out_ref):
    x = keep_ref[0].astype(F32) + got_ref[0].astype(F32) + far_ref[...].astype(F32)
    out_ref[...] = x.astype(BF).reshape(out_ref.shape)


def own_sum(keep, got, far, deps=()):
    n = keep.shape[1]
    block = pl.BlockSpec((1, n // 2, 768), lambda i: (0, i, 0))
    one = pl.BlockSpec((n // 2, 768), lambda i: (i, 0))
    return pl.pallas_call(
        skip(own_kernel, 3, len(deps)),
        grid=(2,),
        in_specs=[block] * 2 + [one] + [ANY] * len(deps),
        out_specs=one,
        out_shape=jax.ShapeDtypeStruct((n, 768), BF),
        cost_estimate=cost(1),
        compiler_params=pltpu.CompilerParams(vmem_limit_bytes=VM),
    )(keep, got, far, *deps)


def finish_kernel(in_ref, outer_ref, small_ref):
    for i in range(4):
        outer_ref[:, 768 * i : 768 * i + 768] = in_ref[LW * i : LW * i + LW].astype(F32)
    small_ref[...] = in_ref[768:784].astype(F32)


def finish(grads, deps=()):
    whole = lambda *s: pl.BlockSpec(s, lambda: (0, 0))
    shapes = (LW, 3072), (16, 768)
    return pl.pallas_call(
        skip(finish_kernel, 1, len(deps)),
        in_specs=[whole(800, 768)] + [ANY] * len(deps),
        out_specs=[whole(*s) for s in shapes],
        out_shape=[jax.ShapeDtypeStruct(s, F32) for s in shapes],
        cost_estimate=cost(6),
        compiler_params=pltpu.CompilerParams(vmem_limit_bytes=VM),
    )(grads, *deps)


def widen_kernel(in_ref, inner_ref, proj_ref):
    inner_ref[...] = in_ref[:768].astype(F32)
    proj_ref[...] = in_ref[768:].astype(F32)


def widen(x, deps=()):
    whole = lambda *s: pl.BlockSpec(s, lambda: (0, 0))
    shapes = (768, 768), (LW, 768)
    return pl.pallas_call(
        skip(widen_kernel, 1, len(deps)),
        in_specs=[whole(960, 768)] + [ANY] * len(deps),
        out_specs=[whole(*s) for s in shapes],
        out_shape=[jax.ShapeDtypeStruct(s, F32) for s in shapes],
        cost_estimate=cost(3),
        compiler_params=pltpu.CompilerParams(vmem_limit_bytes=VM),
    )(x, *deps)


def taps_kernel(own_ref, scale_ref, dir_ref, out_ref, square_ref, tmp):
    n = dir_ref.shape[0]
    at = pl.program_id(0) * n
    side = own_ref[0] // 2
    for k in range(n):
        x = dir_ref[k].astype(F32)
        x = x * x
        x = sum(x[:, 128 * i : 128 * i + 128] for i in range(6))
        total = jnp.sum(jnp.sum(x, axis=0, keepdims=True), axis=1, keepdims=True)
        square_ref[k : k + 1] = jnp.broadcast_to(total, (1, 128))
        x = dir_ref[k, :, pl.ds(pl.multiple_of(side * PW, 128), PW)].astype(F32)
        tmp[48 * k : 48 * k + 48] = (x * (scale_ref[at + k] * lax.rsqrt(total))).astype(BF)
    out_ref[...] = dot(tmp[...], own_pick(own_ref[0]))[:, :LW].astype(BF)


def own_pick(index):
    row = lax.broadcasted_iota(jnp.int32, (PW, 256), 0)
    lane = lax.broadcasted_iota(jnp.int32, (PW, 256), 1)
    return ((row == lane + LW * (index & 1)) & (lane < LW)).astype(F32).astype(BF)


def own_taps(idx, scale, tap_dir):
    return pl.pallas_call(
        taps_kernel,
        grid_spec=pltpu.PrefetchScalarGridSpec(
            num_scalar_prefetch=2,
            grid=(8,),
            in_specs=[pl.BlockSpec((16, 48, 768), lambda i, x, c: (i, 0, 0))],
            out_specs=[pl.BlockSpec((768, LW), lambda i, x, c: (i, 0)), pl.BlockSpec((16, 128), lambda i, x, c: (i, 0))],
            scratch_shapes=[pltpu.VMEM((768, PW), BF)],
        ),
        out_shape=[jax.ShapeDtypeStruct((6144, LW), BF), jax.ShapeDtypeStruct((128, 128), F32)],
        cost_estimate=cost(10),
        compiler_params=pltpu.CompilerParams(vmem_limit_bytes=VM),
    )(idx, scale, tap_dir)


def raw_kernel(own_ref, dir_ref, out_ref):
    out_ref[...] = dot(dir_ref[...], own_pick(own_ref[0]))[:, :LW].astype(BF)


def own_dirs(idx, tap_dir, deps=()):
    return pl.pallas_call(
        skip(raw_kernel, 2, len(deps)),
        grid_spec=pltpu.PrefetchScalarGridSpec(
            num_scalar_prefetch=1,
            grid=(4,),
            in_specs=[pl.BlockSpec((1536, PW), lambda i, x: (i, x[0] // 2))] + [ANY] * len(deps),
            out_specs=pl.BlockSpec((1536, LW), lambda i, x: (i, 0)),
        ),
        out_shape=jax.ShapeDtypeStruct((6144, LW), BF),
        cost_estimate=cost(5),
        compiler_params=pltpu.CompilerParams(vmem_limit_bytes=VM),
    )(idx, tap_dir.reshape(6144, 768), *deps)


def dots_kernel(tap_ref, dir_ref, out_ref):
    g = tap_ref[0].astype(F32).T
    p = g * dir_ref[...].astype(F32)
    rows = [jnp.sum(p[48 * t : 48 * t + 48], axis=0, keepdims=True) for t in range(16)]
    s = jnp.sum(jnp.concatenate(rows, axis=0), axis=1, keepdims=True)
    out_ref[0] = jnp.broadcast_to(s, (16, 128))


def tap_dots(tap, dirs, deps=()):
    return pl.pallas_call(
        skip(dots_kernel, 2, len(deps)),
        grid=(8,),
        in_specs=[pl.BlockSpec((1, LW, 768), lambda i: (i, 0, 0)), pl.BlockSpec((768, LW), lambda i: (i, 0))] + [ANY] * len(deps),
        out_specs=pl.BlockSpec((1, 16, 128), lambda i: (i, 0, 0)),
        out_shape=jax.ShapeDtypeStruct((8, 16, 128), F32),
        cost_estimate=cost(6),
        compiler_params=pltpu.CompilerParams(vmem_limit_bytes=VM),
    )(tap, dirs, *deps)


def last_kernel(left_ref, right_ref, dir_ref, coef_ref, beta_ref, out_ref, turned):
    i = pl.program_id(0)

    @pl.when(i == 0)
    def _():
        for J in range(8):
            for p, ref in enumerate((left_ref, right_ref)):
                t = ref[J].astype(F32).T
                at = 768 * J + 384 * p
                turned[0, at : at + 384] = t[:, :128]
                turned[1, at : at + 384, :64] = t[:, 128:]

    for c in range(8):
        at = pl.ds(8 * i + c, 128, stride=48)
        g = jnp.concatenate([turned[0, at].T, turned[1, at].T[:64]], axis=0)
        out_ref[c] = g * coef_ref[...] - dir_ref[c].astype(F32) * beta_ref[...]


def last_taps(coef, beta, left, right, dirs, deps=()):
    row = pl.BlockSpec((1, 128), lambda i: (0, 0))
    block = pl.BlockSpec((8, LW, 128), lambda i: (i, 0, 0))
    return pl.pallas_call(
        skip(last_kernel, 5, len(deps)),
        grid=(6,),
        in_specs=[pl.BlockSpec((8, LW, 384), lambda i: (0, 0, 0))] * 2 + [block, row, row] + [ANY] * len(deps),
        out_specs=block,
        out_shape=jax.ShapeDtypeStruct((48, LW, 128), F32),
        scratch_shapes=[pltpu.VMEM((2, 6144, 128), F32)],
        cost_estimate=cost(8),
        compiler_params=pltpu.CompilerParams(vmem_limit_bytes=VM),
    )(left, right, dirs, coef[None], beta[None], *deps)


def near_kernel(keep_ref, got_ref, mom_ref, mom_got, near_ref, far_ref, mom_out):
    N = keep_ref.shape[1]
    near_ref[...] = keep_ref[0] + got_ref[0].astype(F32)
    far_ref[:N] = (keep_ref[1] + got_ref[1].astype(F32)).astype(BF)
    mom = mom_ref[...] + mom_got[...]
    mom_out[...] = mom
    R = mom.shape[0]
    rows = jnp.concatenate([mom[r, k, 0:2] for r in range(R) for k in range(4)], axis=0)
    far_ref[N:] = jnp.concatenate([rows, jnp.zeros((8 * R, 128), F32)], axis=1).astype(BF)


def near_far(keep, got, moments, moments_got):
    N = keep.shape[1]
    R = moments.shape[0]
    whole = lambda a: pl.BlockSpec(a.shape, lambda: (0,) * a.ndim)
    shapes = [
        jax.ShapeDtypeStruct((N, PW), F32),
        jax.ShapeDtypeStruct((N + 8 * R, PW), BF),
        jax.ShapeDtypeStruct(moments.shape, F32),
    ]
    return pl.pallas_call(
        near_kernel,
        in_specs=[whole(a) for a in (keep, got, moments, moments_got)],
        out_specs=[whole(a) for a in shapes],
        out_shape=shapes,
        cost_estimate=cost(2),
        compiler_params=pltpu.CompilerParams(vmem_limit_bytes=VM),
    )(keep, got, moments, moments_got)


HALF = 384


def pick_kernel(bits_ref, a_ref, b_ref, sa_ref, sb_ref):
    sa_ref[...] = a_ref[...]
    sb_ref[...] = b_ref[...]


def first_sends(bits, x, deps=()):
    L, N, _ = x.shape
    n = N // 4
    out = pl.BlockSpec((L, n, HALF), lambda i, s: (0, i, 0))
    return pl.pallas_call(
        skip(pick_kernel, 3, len(deps)),
        grid_spec=pltpu.PrefetchScalarGridSpec(
            num_scalar_prefetch=1,
            grid=(2,),
            in_specs=[
                pl.BlockSpec((L, n, HALF), lambda i, s: (0, 2 - 2 * s[0] + i, 0)),
                pl.BlockSpec((L, n, HALF), lambda i, s: (0, 2 - 2 * s[1] + i, 1)),
            ]
            + [ANY] * len(deps),
            out_specs=[out, out],
        ),
        out_shape=[jax.ShapeDtypeStruct((L, N // 2, HALF), BF)] * 2,
        cost_estimate=cost(3),
        compiler_params=pltpu.CompilerParams(vmem_limit_bytes=VM),
    )(bits, x, x, *deps)


def stage_kernel(last, steps, bits_ref, ka, kb, ra, rb, *outs):
    i = pl.program_id(0)
    for p, (k, r) in enumerate(((ka, ra), (kb, rb))):
        y = k[...].reshape(r.shape).astype(F32) + r[...].astype(F32)
        if last:
            outs[p][...] = y.astype(BF)
            continue
        sum_ref, send_ref = outs[p], outs[2 + p]
        h = y.shape[1] * steps // 2
        halves = ((i, y),) if steps == 2 else ((0, y[:, :h]), (1, y[:, h:]))
        for at, half in halves:
            sum_ref[:, 0 if steps == 2 else at] = half.astype(BF)

            @pl.when(bits_ref[2 + p] != at)
            def _():
                send_ref[...] = half.astype(BF)


def stage(bits, a, b, ra, rb, last, deps=()):
    L, n, _ = ra.shape
    h = n // 2
    steps = 2 if not last and h % 16 == 0 else 1
    m = n // steps
    if a.ndim == 3:
        keep = lambda p: pl.BlockSpec((L, m, HALF), lambda i, s: (0, steps * s[p] + i, p))
    else:
        keep = lambda p: pl.BlockSpec((L, 1, m, HALF), lambda i, s: (0, s[p], i, 0))
    row = pl.BlockSpec((L, m, HALF), lambda i, s: (0, i, 0))
    if last:
        out_specs, out_shape = [row] * 2, [jax.ShapeDtypeStruct((L, n, HALF), BF)] * 2
    else:
        out_specs = [pl.BlockSpec((L, 2 // steps, h, HALF), lambda i, s: (0, i, 0, 0))] * 2
        out_specs += [pl.BlockSpec((L, h, HALF), lambda i, s: (0, 0, 0))] * 2
        out_shape = [jax.ShapeDtypeStruct((L, 2, h, HALF), BF)] * 2 + [jax.ShapeDtypeStruct((L, h, HALF), BF)] * 2
    return pl.pallas_call(
        skip(lambda *refs: stage_kernel(last, steps, *refs), 5, len(deps)),
        grid_spec=pltpu.PrefetchScalarGridSpec(
            num_scalar_prefetch=1,
            grid=(steps,),
            in_specs=[keep(0), keep(1), row, row] + [ANY] * len(deps),
            out_specs=out_specs,
        ),
        out_shape=out_shape,
        cost_estimate=cost(3),
        compiler_params=pltpu.CompilerParams(vmem_limit_bytes=VM),
    )(bits, a, b, ra, rb, *deps)


def join_kernel(bits_ref, a, b, ra, rb, oa, ob):
    for p, (k, r, o) in enumerate(((a, ra, oa), (b, rb, ob))):
        on = bits_ref[p]
        o[on] = k[...]
        o[1 - on] = r[...]


def join(bits, a, b, ra, rb, deps=()):
    shape = a.shape
    block = pl.BlockSpec(shape, lambda i, s: (0,) * len(shape))
    out = pl.BlockSpec((2,) + shape, lambda i, s: (0,) * (len(shape) + 1))
    oa, ob = pl.pallas_call(
        skip(join_kernel, 5, len(deps)),
        grid_spec=pltpu.PrefetchScalarGridSpec(
            num_scalar_prefetch=1,
            grid=(1,),
            in_specs=[block] * 4 + [ANY] * len(deps),
            out_specs=[out] * 2,
        ),
        out_shape=[jax.ShapeDtypeStruct((2,) + shape, BF)] * 2,
        cost_estimate=cost(2),
        compiler_params=pltpu.CompilerParams(vmem_limit_bytes=VM),
    )(bits, a, b, ra, rb, *deps)
    flat = (2 * shape[0],) + shape[1:]
    return oa.reshape(flat), ob.reshape(flat)


class RowSum:
    def __init__(self, x, deps=()):
        n = lax.axis_size("rows")
        bits = [1 << i for i in range(n.bit_length() - 1)]
        self.orders = (bits, bits[1::-1] + bits[2:])
        self.count = x.shape[1]
        full = -(-self.count // (16 * n)) * (16 * n) if n > 8 else self.count
        if full != self.count:
            x = jnp.pad(x, ((0, 0), (0, full - self.count), (0, 0)))
        self.parts = [x, x]
        self.at = 0
        self.got = None
        self.steps = len(bits)
        self.sends = first_sends(self.bits(0), x, deps)

    def bits(self, s):
        place = lax.axis_index("rows")
        pick = lambda o, i: (place // o[min(i, self.steps - 1)]) % 2
        return jnp.stack([pick(o, i) for i in (s, s + 1) for o in self.orders]).astype(jnp.int32)

    def go(self):
        self.got = [swap(s, "rows", o[self.at]) for s, o in zip(self.sends, self.orders)]

    def step(self, *deps):
        if self.got is None:
            self.go()
        got, self.got = self.got, None
        last = self.at == self.steps - 1
        outs = stage(self.bits(self.at), *self.parts, *got, last, deps)
        self.parts, self.sends = outs[:2], outs[2:]
        self.at += 1
        return self.parts[0]

    def back(self, *deps):
        self.at -= 1
        got = [swap(p, "rows", o[self.at]) for p, o in zip(self.parts, self.orders)]
        self.parts = join(self.bits(self.at), *self.parts, *got, deps)
        return self.parts[0]

    def result(self):
        return [p.reshape(-1, HALF)[: self.count] for p in self.parts]


def swap(x, axis, bit):
    return lax.ppermute(x, axis, [(i, i ^ bit) for i in range(lax.axis_size(axis))])


def gather_seq(x):
    far = swap(x, "seq", 2)
    near = swap(x, "seq", 1)
    return [x, near, far, swap(far, "seq", 1)]


def trade(blocks):
    return [blocks[0], swap(blocks[1], "seq", 1), swap(blocks[2], "seq", 2), swap(blocks[3], "seq", 3)]


def all_sum(x, axis):
    for i in range(lax.axis_size(axis).bit_length() - 1):
        x = x + swap(x, axis, 1 << i)
    return x


def assemble(blocks, index):
    low = (index & 1) != 0
    high = (index & 2) != 0
    b = [jnp.where(low, blocks[m ^ 1], blocks[m]) for m in range(4)]
    return [jnp.where(high, b[m ^ 2], b[m]) for m in range(4)]


def cut(x, start, size, axis):
    return lax.dynamic_slice_in_dim(x, start, size, axis)


def local(
    frames,
    utterance_lengths,
    tap_dir,
    tap_scale,
    conv_bias,
    pos_gain,
    pos_shift,
    query_weight,
    query_bias,
    key_weight,
    value_weight,
    value_bias,
    proj_weight,
    proj_bias,
    attend_gain,
    attend_shift,
    inner_weight,
    inner_bias,
    outer_weight,
    outer_bias,
    final_gain,
    final_shift,
    out_grad,
):
    R = frames.shape[0]
    index = lax.axis_index("seq")
    idx = jnp.full((1,), index, jnp.int32)
    ends = utterance_lengths
    order = [index ^ m for m in range(4)]
    own = index * LW

    def packed(x):
        return jnp.concatenate([x[0::2], x[1::2]], axis=2).reshape(R * 128, PW)

    sent = trade([packed(cut(frames, b * LW, LW, 2)) for b in order])
    taps, squares = own_taps(idx, tap_scale, tap_dir)
    w = build_w(taps)
    bias4 = jnp.tile(cut(conv_bias, own, LW, 0).reshape(4, 1, 48), (1, 4, 1)).reshape(4, 1, LW)
    first, pre, xs = conv_fwd(ends, idx, sent, w, bias4)
    firsts = gather_seq(first)

    def xor_rows(a):
        return jnp.stack([cut(a, b * LW, LW, 0) for b in order])

    def pad_to(a, axis, size):
        widths = [(0, 0)] * a.ndim
        widths[axis] = (0, size - a.shape[axis])
        return jnp.pad(a, widths)

    own_cols = [
        pad_to(cut(a, own, LW, 1), 1, 256)
        for a in (query_weight * jnp.asarray(0.125, BF), key_weight, value_weight)
    ]
    w_qkv = pad_to(xor_rows(jnp.concatenate(own_cols, axis=1)), 1, 256)
    b_qkv = jnp.concatenate(
        [
            pad_to(cut(query_bias, own, LW, 0) * 0.125, 0, 512),
            pad_to(cut(value_bias, own, LW, 0), 0, 256),
        ]
    )[None]
    gain_x = xor_rows(pos_gain)[:, None]
    shift_x = xor_rows(pos_shift)[:, None]
    q, k, v, mixed_low, stat = qkv(firsts, w_qkv, b_qkv, gain_x, shift_x)
    att, att_full, lse = attn(idx, ends, q, k, v)
    att_blocks = trade([att[m] for m in range(4)])

    vecs = jnp.stack([pos_gain, pos_shift, proj_bias, attend_gain, attend_shift, outer_bias, final_gain, final_shift])
    layer_out, act, d_inner, middle_low, d_outer, d_proj, attended, d_att, second_x, sums, inner_sums = ff(
        idx, firsts, att_blocks, out_grad.reshape(R * 256, 768), proj_weight, inner_weight, outer_weight,
        inner_bias.reshape(4, 1, 768), vecs,
    )
    dos = trade_out(d_att)
    keep_out, send_out = weight_grads(outer_kernel, 800, idx, act, (d_outer, sums, inner_sums))
    got_out = swap(send_out, "seq", 1)
    keep_in, send_in = weight_grads(inner_kernel, 960, idx, d_inner, (middle_low, d_proj, attended), (send_out,))
    far = far_sum(keep_out, got_out, (send_in,))
    got_in = swap(send_in, "seq", 1)

    heads = attn_bwd(0, idx, ends, q, k, v, att_full, dos, lse, (far,))
    heads += attn_bwd(1, idx, ends, q, k, v, att_full, dos, lse, (heads[0],))
    grads = own_sum(keep_out, got_out, swap(far, "seq", 2), (heads[3],))
    keep, send, moments = dmix(idx, heads, w_qkv, second_x, firsts, stat, gain_x, (grads,))
    grads_out = lax.psum(grads, "rows")
    e_near, e_far, moments = near_far(keep, swap(send, "seq", 1), moments, swap(moments, "seq", 1))
    g_qkv, b_grads = qkvw(heads, mixed_low, (e_far,))
    e_sent = e_far
    e_far = swap(e_far, "seq", 2)
    far = swap(far_sum(keep_in, got_in, (e_sent, g_qkv)), "seq", 2)
    moments = moments.reshape(R * 4, 8, 256)

    tap_part, ds, d4, conv_b, vec = tap_grads(
        ends, e_near, e_far, first, stat.reshape(R * 1024, 128), moments, cut(pos_gain, own, LW, 0)[None], pre, xs, g_qkv,
    )
    if R > 2:
        tap_part = jnp.sum(tap_part.astype(F32), axis=0, keepdims=True).astype(BF)
    tap_part = tap_part[0]
    tap_sum = RowSum(tap_part.reshape(1, 11 * LW, 768))
    part = conv_back(0, ends, idx, ds, d4, w, None, tuple(tap_sum.sends))
    dir_own = own_dirs(idx, tap_dir, (part,))
    dir_turned = jnp.transpose(dir_own.reshape(128, 48, LW), (1, 2, 0))
    tap_sum.step(part)
    grads_in = lax.psum(own_sum(keep_in, got_in, far, (part, grads_out)), "rows")
    back = conv_back(2, ends, idx, ds, d4, w, part, tuple(tap_sum.sends))
    tap_sum.step(back)
    dots = tap_dots(tap_part, dir_own, tuple(tap_sum.sends))
    tap_sum.step(dots)
    dots = all_sum(dots[:, :, 0], "seq")
    back = trade_out(back)
    back = jnp.concatenate([b.reshape(R // 2, 1, 256, PW) for b in assemble(back, index)], axis=1)
    back = back.reshape(R // 2, 4, 256, 2, LW)
    frames_grad = jnp.transpose(back, (0, 3, 2, 1, 4)).reshape(R, 256, 768)
    while tap_sum.at:
        tap_sum.back()
    tap_left, tap_right = [p.reshape(11, LW, HALF) for p in tap_sum.result()]
    qkv_std = assemble([x[8:11, :, LW * m : LW * m + LW] for x in (tap_left, tap_right) for m in range(2)], index)
    t_qkv = jnp.concatenate(qkv_std, axis=2).astype(F32)
    t_outer, small = finish(grads_out, (tap_sum.parts[0],))
    lates = jnp.concatenate(
        [
            jnp.sum(conv_b, axis=(0, 2)).reshape(4, 4, 48).sum(1).reshape(LW),
            jnp.sum(vec[:, 0], axis=0),
            jnp.sum(vec[:, 1], axis=0),
            b_grads[0, 0:LW] * 0.125,
            b_grads[0, 512 : 512 + LW],
            dots.reshape(128),
            jnp.zeros((2048 - 1088,), F32),
        ]
    )
    lates = all_sum(lates.reshape(16, 128), "rows").reshape(2048)
    dots = lates[5 * LW : 5 * LW + 128]
    inverse = lax.rsqrt(squares[:, 0])
    coef = tap_scale * inverse
    turned = last_taps(coef, coef * dots * inverse * inverse, tap_left, tap_right, dir_turned, (frames_grad, t_outer))
    g_tap_dir = jnp.transpose(turned, (2, 0, 1))
    t_inner, t_proj = widen(grads_in, (turned,))
    g_tap_scale = cut(dots * inverse, index * 32, 32, 0)

    return (
        layer_out.reshape(R, 256, 768),
        frames_grad,
        g_tap_dir,
        g_tap_scale,
        lates[0:LW],
        lates[LW : 2 * LW],
        lates[2 * LW : 3 * LW],
        t_qkv[0].T * 0.125,
        lates[3 * LW : 4 * LW],
        t_qkv[1].T,
        t_qkv[2].T,
        lates[4 * LW : 5 * LW],
        t_proj.T,
        small[5, :LW],
        small[3, :LW],
        small[4, :LW],
        t_inner,
        small[8],
        t_outer.T,
        small[2, :LW],
        small[0, :LW],
        small[1, :LW],
    )


def trade_out(x):
    return trade([x[m] for m in range(4)])


def solution(mesh):
    split = P("rows", "seq", None)
    col = P(None, "seq")
    one = P("seq")
    return jax.shard_map(
        local,
        mesh=mesh,
        in_specs=(split, P("rows", None)) + (P(),) * 20 + (split,),
        out_specs=(split, split, P(None, None, "seq"), one, one, one, one)
        + (col, one, col, col, one, col, one, one, one, col, one, col, one, one, one),
        check_vma=False,
    )
```
